32 devices in a mesh: ctx: 8 (over z, x), tp: 4 (over y, core).
Axes of the slice: x: 2, y: 2, z: 4, core: 2. Of those that a mesh axis runs over, the one named last changes fastest.
Arguments:
- x_inputs: bfloat16 [4096, 4096], P('ctx', 'tp'), may hold values from -6 to 6
- state_maps: bfloat16 [4096, 1024], P('ctx', 'tp'), may hold values from -6 to 6
- z_gate: bfloat16 [4096, 4096], P('ctx', 'tp'), may hold values from -6 to 6
- step_raw: float32 [4096, 64], P('ctx', 'tp'), may hold values from -3 to 3
- step_bias: float32 [64], P('tp'), may hold values from -0.5 to 0.5
- decay_log: float32 [64], P('tp'), may hold values from -20 to -2
- skip_gain: float32 [64], P('tp'), may hold values from 0.5 to 1.5
- x_filter: bfloat16 [4, 4096], P(None, 'tp'), may hold values from -3 to 3
- state_filter: bfloat16 [4, 1024], P(None, 'tp'), may hold values from -3 to 3
- norm_gain: float32 [4096], P('tp'), may hold values from 0.1 to 1.9
- out_weight: bfloat16 [4096, 4096], P('tp'), may hold values from -0.09375 to 0.09375
Outputs:
- mixed: bfloat16 [4096, 4096], P(('ctx', 'tp'))
The draws below stay inside these ranges and needn't reach their ends.
All inputs are finite; a program needn't handle non-finite values.
Results may differ from the reference program's by a relative error of at most 0.017.
Values may be sent and summed in bfloat16 or wider, within the bound.
A program may use at most 128 MiB of HBM per device.

```python
import jax
import jax.numpy as jnp
from jax import lax

D = 4096
HEADS_DEV = 16
HEAD_DIM = 64
STATE = 128
CONV = 4
TOK_DEV = 512
BLOCK = 512
GROUPS = 4
HEADS = 64
SEQ = 4096


def draw_decay_log(key, part):
    key_one = jax.random.fold_in(jax.random.fold_in(key, 11), 0)
    lowest = -jnp.log(256.0 * SEQ)
    highest = -jnp.log(16.0)
    spread = jax.random.uniform(key_one, (HEADS,), jnp.float32)
    return lowest + spread * (highest - lowest)


def draw_step_raw(key, part):
    key_one, key_two = jax.random.split(jax.random.fold_in(key, 23), 2)
    blocks = SEQ // TOK_DEV
    noise = 0.5 * jnp.clip(jax.random.normal(key_one, (SEQ, HEADS), jnp.float32), -3.0, 3.0)
    offsets = jax.random.uniform(key_two, (blocks,), jnp.float32, minval=-0.8, maxval=0.8)
    return noise + jnp.repeat(offsets, TOK_DEV)[:, None]


def block_scale(stream_key, shape, cuts, smallest, high):
    factor_of = 1.0
    for position, parts in cuts:
        steps = jax.random.uniform(jax.random.fold_in(jax.random.fold_in(stream_key, 6), position), (parts,), jnp.float32, smallest / len(cuts), high / len(cuts))
        factor_of = factor_of * jnp.repeat(jnp.exp(steps), shape[position] // parts).reshape((-1,) + (1,) * (len(shape) - 1 - position))
    return factor_of


def bell_draw(own_key, extent, scale, reach, cuts=(), kind=jnp.bfloat16):
    array = jax.random.normal(own_key, extent, jnp.float32) * scale
    if len(cuts) > 0:
        array = block_scale(own_key, extent, cuts, -0.22, 0.18) * array
    return jnp.clip(array, min=-reach, max=reach).astype(kind)


def setup_inputs(seed: int = 0) -> dict:
    splits = jax.random.split(jax.random.key(seed), 12)
    return {
        "x_inputs": bell_draw(splits[0], (SEQ, HEADS * HEAD_DIM), 1.0, 6.0, ((0, 8), (1, 4))),
        "state_maps": bell_draw(splits[1], (SEQ, GROUPS * 2 * STATE), 1.0, 6.0, ((0, 8), (1, 4))),
        "z_gate": bell_draw(splits[2], (SEQ, HEADS * HEAD_DIM), 1.0, 6.0, ((0, 8), (1, 4))),
        "step_raw": draw_step_raw(jax.random.fold_in(splits[11], 71), 0),
        "step_bias": jnp.clip(jax.random.uniform(splits[4], (HEADS,), jnp.float32, -0.5, 0.5) * block_scale(splits[4], (HEADS,), ((0, 4),), -0.4, 0.0), -0.5, 0.5),
        "decay_log": draw_decay_log(jax.random.fold_in(splits[11], 71), 0),
        "skip_gain": jnp.clip(0.5 + 1.0 * jax.random.uniform(splits[6], (HEADS,), jnp.float32) ** block_scale(splits[6], (HEADS,), ((0, 4),), -0.2, 0.2), 0.5, 1.5),
        "x_filter": bell_draw(splits[7], (CONV, HEADS * HEAD_DIM), CONV ** -0.5, 3.0, ((1, 4),)),
        "state_filter": bell_draw(splits[8], (CONV, GROUPS * 2 * STATE), CONV ** -0.5, 3.0, ((1, 4),)),
        "norm_gain": jnp.clip(1.0 + 0.18 * jax.random.normal(splits[9], (HEADS * HEAD_DIM,), jnp.float32), 0.1, 1.9),
        "out_weight": bell_draw(splits[10], (HEADS * HEAD_DIM, D), (HEADS * HEAD_DIM) ** -0.5, 0.09375, ((0, 4),)),
    }


exactness = lax.Precision.HIGHEST

def causal_conv(padded, filters, length):
    total = jnp.zeros((length, padded.shape[1]), jnp.float32)
    for offset in range(filters.shape[0]):
        total = total + filters[offset].astype(jnp.float32) * padded[offset:offset + length].astype(jnp.float32)
    return total

def block_scan(values, b_rows, c_rows, log_decay, step_size, span):
    length, head_count, head_dim = values.shape
    state_size = b_rows.shape[1]
    pieces = length // span
    inputs = (values.reshape(pieces, span, head_count, head_dim), b_rows.reshape(pieces, span, state_size), c_rows.reshape(pieces, span, state_size), log_decay.reshape(pieces, span, head_count), step_size.reshape(pieces, span, head_count))
    row_ids = lax.broadcasted_iota(jnp.int32, (span, span), 0)
    col_ids = lax.broadcasted_iota(jnp.int32, (span, span), 1)
    causal = (row_ids >= col_ids)[None]

    def advance(carried, piece):
        piece_x, piece_b, piece_c, piece_rate, piece_step = piece
        x_wide = piece_x.astype(jnp.float32)
        b_wide = piece_b.astype(jnp.float32)
        c_wide = piece_c.astype(jnp.float32)
        cumulative = jnp.cumsum(piece_rate, axis=0)
        by_head = cumulative.T
        spread = by_head[:, :, None] - by_head[:, None, :]
        decay = jnp.where(causal, jnp.exp(-jnp.where(causal, spread, 0.0)), 0.0)
        scores = jnp.dot(piece_c, piece_b.T, preferred_element_type=jnp.float32)
        weights = decay * scores[None] * piece_step.T[:, None, :]
        weights = lax.optimization_barrier(weights.astype(jnp.bfloat16)).astype(jnp.float32)
        output = jnp.einsum('hts,shp->thp', weights, x_wide, precision=exactness)
        rounded = lax.optimization_barrier(carried.astype(jnp.bfloat16)).astype(jnp.float32)
        output = output + jnp.einsum('tn,hpn->thp', c_wide, rounded, precision=exactness) * jnp.exp(-cumulative)[:, :, None]
        tail = jnp.exp(-(cumulative[-1][None, :] - cumulative)) * piece_step
        weighted = lax.optimization_barrier((tail[:, :, None] * x_wide).astype(jnp.bfloat16)).astype(jnp.float32)
        fresh = jnp.exp(-cumulative[-1])[:, None, None] * carried
        fresh = fresh + jnp.einsum('shp,sn->hpn', weighted, b_wide, precision=exactness)
        return (fresh, output)
    start_state = jnp.zeros((head_count, head_dim, state_size), jnp.float32)
    final_state, outputs = lax.scan(advance, start_state, inputs)
    return (outputs.reshape(length, head_count, head_dim), final_state)

def reference(x_inputs, state_maps, z_gate, step_raw, step_bias, decay_log, skip_gain, x_filter, state_filter, norm_gain, out_weight):
    leading = CONV - 1
    x_pad = jnp.concatenate([jnp.zeros((leading, x_inputs.shape[1]), x_inputs.dtype), x_inputs], 0)
    x_conv = jax.nn.silu(causal_conv(x_pad, x_filter, SEQ)).astype(jnp.bfloat16)
    bc_pad = jnp.concatenate([jnp.zeros((leading, state_maps.shape[1]), state_maps.dtype), state_maps], 0)
    bc_conv = jax.nn.silu(causal_conv(bc_pad, state_filter, SEQ)).astype(jnp.bfloat16)
    step_size = jax.nn.softplus(step_raw + step_bias)
    log_decay = step_size * jnp.exp(decay_log)
    channels = HEADS_DEV * HEAD_DIM
    total = jnp.zeros((SEQ, D), jnp.float32)
    for group in range(GROUPS):
        heads_here = slice(group * HEADS_DEV, (group + 1) * HEADS_DEV)
        cols = slice(group * channels, (group + 1) * channels)
        values = x_conv[:, cols].reshape(SEQ, HEADS_DEV, HEAD_DIM)
        b_rows = bc_conv[:, 2 * group * STATE:(2 * group + 1) * STATE]
        c_rows = bc_conv[:, (2 * group + 1) * STATE:(2 * group + 2) * STATE]
        output, _ = block_scan(values, b_rows, c_rows, log_decay[:, heads_here], step_size[:, heads_here], BLOCK)
        output = output + skip_gain[heads_here][None, :, None] * values.astype(jnp.float32)
        gated = output.reshape(SEQ, channels) * jax.nn.silu(z_gate[:, cols].astype(jnp.float32))
        scale = lax.rsqrt(lax.optimization_barrier(jnp.mean(gated * gated, axis=-1, keepdims=True)) + 1e-05)
        normed = (gated * scale * norm_gain[cols]).astype(jnp.bfloat16)
        partial_sum = jnp.dot(normed, out_weight[cols], preferred_element_type=jnp.float32)
        total = total + lax.optimization_barrier(partial_sum.astype(jnp.bfloat16)).astype(jnp.float32)
    return total.astype(jnp.bfloat16)
```

```python
import functools

import jax
import jax.numpy as jnp
from jax import lax
from jax.experimental import pallas as pl
from jax.experimental.pallas import tpu as pltpu
from jax.sharding import PartitionSpec as P

MESH = pl.DeviceIdType.MESH
LANES = 128
HALO = 16


def half_silu(v):
    h = 0.5 * v
    return h + h * jnp.tanh(h)


def layer_kernel(
    n_ctx, n_tp, chunk,
    x_ref, m_ref, z_ref, step_ref, bias_ref, decay_ref, skip_ref, xf_ref, mf_ref, gain_ref, w_hbm,
    out_ref,
    w_ref, hx_ref, hm_ref, pad_ref, xfs_ref, mfs_ref, gains_ref, skips_ref,
    col_ref, sq_ref, at_ref, rt_ref, aexp_ref, dsend_ref, drecv_ref,
    xc_ref, bt_ref, c_ref, cb_ref, lown_ref, lsend_ref, lrecv_ref, csend_ref, crecv_ref, sr_ref,
    yg_ref, eg_ref, gated_ref, normed_ref, part_ref, core_ref, ysend_ref, yrecv_ref,
    w_sem, halo_send, halo_recv, dec_send, dec_recv, pair_send, pair_recv, chain_send, chain_recv,
    core_send, core_recv, y_send, y_recv,
):
    length = x_ref.shape[0]
    pairs = x_ref.shape[1] // LANES
    heads = step_ref.shape[1]
    n_y = n_tp // 2
    rows = length // n_tp
    n_chunks = w_hbm.shape[1] // chunk
    n_z = n_ctx // 2
    ctx = lax.axis_index("ctx")
    tp = lax.axis_index("tp")
    y, core = tp // 2, tp % 2
    z, odd = ctx // 2, ctx % 2
    mate = ctx + 1 - 2 * odd
    other_core = y * 2 + 1 - core

    w_copy = pltpu.make_async_copy(w_hbm, w_ref, w_sem)
    w_copy.start()

    barrier = pltpu.get_barrier_semaphore()
    for off in (1, n_ctx - 1, 2, n_ctx - 2):
        pl.semaphore_signal(barrier, inc=1, device_id={"ctx": (ctx + off) % n_ctx}, device_id_type=MESH)
    pl.semaphore_signal(barrier, inc=1, device_id={"tp": other_core}, device_id_type=MESH)
    for off in range(1, n_y):
        pl.semaphore_signal(
            barrier, inc=1, device_id={"tp": ((y + off) % n_y) * 2 + core}, device_id_type=MESH
        )
    pl.semaphore_wait(barrier, 4 + 1 + (n_y - 1))

    def remote(src, dst, send, recv, where):
        return pltpu.make_async_remote_copy(
            src_ref=src, dst_ref=dst, send_sem=send, recv_sem=recv, device_id=where, device_id_type=MESH
        )

    following = {"ctx": (ctx + 1) % n_ctx}
    halo_x = remote(x_ref.at[pl.ds(length - HALO, HALO)], hx_ref, halo_send.at[0], halo_recv.at[0], following)
    halo_m = remote(m_ref.at[pl.ds(length - HALO, HALO)], hm_ref, halo_send.at[1], halo_recv.at[1], following)
    halo_m.start()
    halo_x.start()

    step = jnp.log(1.0 + jnp.exp(step_ref[...] + bias_ref[...]))
    col_ref[...] = jnp.zeros_like(col_ref)
    col_ref[:, :heads] = step * jnp.exp(decay_ref[...])
    rate_t = col_ref[...].T[:heads]
    col_ref[:, :heads] = jnp.log(step)
    log_step_t = col_ref[...].T[:heads]
    s_ids = lax.broadcasted_iota(jnp.int32, (length, length), 0)
    t_ids = lax.broadcasted_iota(jnp.int32, (length, length), 1)
    upper = jnp.where(s_ids <= t_ids, 1.0, 0.0).astype(jnp.float32)
    sums = jnp.dot(rate_t, upper, precision=lax.Precision.HIGHEST, preferred_element_type=jnp.float32)
    at_ref[...] = sums
    rt_ref[...] = sums + log_step_t
    sq_ref[...] = jnp.zeros_like(sq_ref)
    sq_ref[:, :heads] = jnp.broadcast_to(skip_ref[...], (LANES, heads))
    skip_t = sq_ref[...].T
    lane_row = lax.broadcasted_iota(jnp.int32, (1, LANES), 1) < LANES // 2
    x_taps = xf_ref[...].astype(jnp.float32)
    m_taps = mf_ref[...].astype(jnp.float32)
    for p in range(pairs):
        skips_ref[p] = jnp.broadcast_to(
            jnp.where(lane_row, skip_t[2 * p : 2 * p + 1], skip_t[2 * p + 1 : 2 * p + 2]), (8, LANES)
        )
        gains_ref[p] = jnp.broadcast_to(gain_ref[:, p * LANES : (p + 1) * LANES], (8, LANES))
        xfs_ref[p] = x_taps[:, p * LANES : (p + 1) * LANES]
    for p in range(2):
        mfs_ref[p] = m_taps[:, p * LANES : (p + 1) * LANES]

    head_sub = lax.broadcasted_iota(jnp.int32, (LANES, length), 0) < LANES // 2

    def by_pair(ref, p):
        return jnp.where(head_sub, ref[pl.ds(2 * p, 1), :], ref[pl.ds(2 * p + 1, 1), :]).T

    def expand(p, _):
        spread = by_pair(at_ref, p)
        aexp_ref[p] = spread
        dsend_ref[p] = jnp.broadcast_to(spread[length - 1 : length], (8, LANES))
        return 0

    lax.fori_loop(0, pairs, expand, 0)
    dec_copy = remote(dsend_ref, drecv_ref, dec_send, dec_recv, {"ctx": mate})
    dec_copy.start()

    taps = xf_ref.shape[0]
    has_prev = jnp.where(ctx > 0, 1.0, 0.0).astype(jnp.float32)

    def conv(block, halo, filters):
        pad_ref[0:8] = halo.astype(jnp.float32)[HALO - 8 :] * has_prev
        pad_ref[8:] = block.astype(jnp.float32)
        total = filters[0:1] * pad_ref[9 - taps : 9 - taps + length]
        for k in range(1, taps):
            start = 9 - taps + k
            total = total + filters[k : k + 1] * pad_ref[start : start + length]
        return half_silu(total)

    halo_m.wait_recv()
    bt_ref[...] = conv(m_ref[:, :LANES], hm_ref[:, :LANES], mfs_ref[0]).T.astype(jnp.bfloat16)
    c_ref[...] = conv(m_ref[:, LANES:], hm_ref[:, LANES:], mfs_ref[1]).astype(jnp.bfloat16)
    halo_x.wait_recv()

    def pair_copy(p):
        return remote(lsend_ref.at[p], lrecv_ref.at[p], pair_send.at[p], pair_recv.at[p], {"ctx": mate})

    def local_state(p, _):
        cols = pl.ds(pl.multiple_of(p * LANES, LANES), LANES)
        xc = conv(x_ref[:, cols], hx_ref[:, cols], xfs_ref[p]).astype(jnp.bfloat16)
        xc_ref[p] = xc
        tail = jnp.exp(by_pair(rt_ref, p) - dsend_ref[p][0:1])
        u = (tail * xc.astype(jnp.float32)).astype(jnp.bfloat16)
        state = jnp.dot(bt_ref[...], u, preferred_element_type=jnp.float32)
        lown_ref[p] = state
        lsend_ref[p] = state.astype(jnp.bfloat16)
        pair_copy(p).start()
        return 0

    lax.fori_loop(0, pairs, local_state, 0)

    scores = jnp.dot(c_ref[...], bt_ref[...], preferred_element_type=jnp.float32)
    cb_ref[...] = jnp.where(s_ids >= t_ids, scores, 0.0)

    is_odd = odd.astype(jnp.float32)
    is_even = 1.0 - is_odd
    next_pair = {"ctx": (ctx + 2) % n_ctx}

    def chain_copy(p):
        return remote(csend_ref.at[p], crecv_ref.at[p], chain_send.at[p], chain_recv.at[p], next_pair)

    @pl.when(z == 0)
    def _():
        crecv_ref[...] = jnp.zeros_like(crecv_ref)

    dec_copy.wait_recv()

    def relay(p):
        pair_copy(p).wait_recv()
        mine = lown_ref[p]
        theirs = lrecv_ref[p].astype(jnp.float32)
        d_mine = jnp.exp(-dsend_ref[p][0:1])
        d_theirs = jnp.exp(-drecv_ref[p][0:1])
        l_even = mine * is_even + theirs * is_odd
        l_odd = mine * is_odd + theirs * is_even
        d_even = d_mine * is_even + d_theirs * is_odd
        d_odd = d_mine * is_odd + d_theirs * is_even

        @pl.when(z > 0)
        def _():
            chain_copy(p).wait_recv()

        entering = crecv_ref[p].astype(jnp.float32)
        middle = d_even * entering + l_even
        sr_ref[p] = (entering * is_even + middle * is_odd).astype(jnp.bfloat16)

        @pl.when(z < n_z - 1)
        def _():
            csend_ref[p] = (d_odd * middle + l_odd).astype(jnp.bfloat16)
            chain_copy(p).start()

    half = length // 2
    low_lanes = lax.broadcasted_iota(jnp.int32, (half, LANES), 1) < LANES // 2

    def within(p):
        xc = xc_ref[p]
        tops, bottoms = [], []
        for h in range(2):
            row_r = rt_ref[pl.ds(2 * p + h, 1), :]
            col_a = jnp.broadcast_to(at_ref[pl.ds(2 * p + h, 1), :], (LANES, length)).T
            col_a = jnp.concatenate([col_a] * (half // LANES), axis=1)

            def weigh(t0, s0, masked):
                power = row_r[:, s0 : s0 + half] - col_a[t0 : t0 + half]
                if masked:
                    power = jnp.minimum(power, 64.0)
                return (jnp.exp(power) * cb_ref[t0 : t0 + half, s0 : s0 + half]).astype(jnp.bfloat16)

            tops.append(jnp.dot(weigh(0, 0, True), xc[:half], preferred_element_type=jnp.float32))
            bottoms.append(
                jnp.dot(weigh(half, 0, False), xc[:half], preferred_element_type=jnp.float32)
                + jnp.dot(weigh(half, half, True), xc[half:], preferred_element_type=jnp.float32)
            )
        cols = pl.ds(pl.multiple_of(p * LANES, LANES), LANES)
        skip = skips_ref[p][0:1]
        for t0, both in ((0, tops), (half, bottoms)):
            here = pl.ds(t0, half)
            gate = half_silu(z_ref[here, cols].astype(jnp.float32))
            own = jnp.where(low_lanes, both[0], both[1])
            yg_ref[p, here] = (own + skip * xc[t0 : t0 + half].astype(jnp.float32)) * gate
            eg_ref[p, here] = jnp.exp(-aexp_ref[p, here]) * gate

    lag = jnp.minimum(2 * z, pairs)

    def turn(i, _):
        @pl.when((i >= lag) & (i < lag + pairs))
        def _():
            relay(i - lag)

        @pl.when(i < pairs)
        def _():
            within(i)

        return 0

    lax.fori_loop(0, 2 * pairs, turn, 0)

    span = 2 * rows
    channels = x_ref.shape[1]

    def project_rows(first):
        here = pl.ds(pl.multiple_of(first, span), span)
        c_rows = c_ref[here, :]

        def gate_pair(p, total):
            inter = jnp.dot(c_rows, sr_ref[p], preferred_element_type=jnp.float32)
            gated = yg_ref[p, here] + eg_ref[p, here] * inter
            gated_ref[p] = gated
            return total + gated * gated

        squares = lax.fori_loop(0, pairs, gate_pair, jnp.zeros((span, LANES), jnp.float32))
        scale = lax.rsqrt(jnp.sum(squares, axis=1, keepdims=True) / channels + 1e-05)
        for p in range(pairs):
            normed_ref[:, p * LANES : (p + 1) * LANES] = (
                gated_ref[p] * scale * gains_ref[p][0:1]
            ).astype(jnp.bfloat16)

    def core_copy(slot, k):
        return remote(
            part_ref.at[slot, k, 1 - core], core_ref.at[slot, k],
            core_send.at[slot, k], core_recv.at[slot, k], {"tp": other_core},
        )

    def y_copy(slot, k):
        target = ((y + slot) % n_y) * 2 + core
        return remote(
            ysend_ref.at[slot - 1, k], yrecv_ref.at[slot - 1, k],
            y_send.at[slot - 1, k], y_recv.at[slot - 1, k], {"tp": target},
        )

    def project(slot, k):
        cols = pl.ds(pl.multiple_of(k * chunk, chunk), chunk)
        part = jnp.dot(normed_ref[...], w_ref[:, cols], preferred_element_type=jnp.float32)
        part = part.astype(jnp.bfloat16)
        part_ref[slot, k, 0] = part[:rows]
        part_ref[slot, k, 1] = part[rows:]
        core_copy(slot, k).start()

    def chip_sum(slot, k):
        core_copy(slot, k).wait_recv()
        return part_ref[slot, k, core].astype(jnp.float32) + core_ref[slot, k].astype(jnp.float32)

    for slot in list(range(1, n_y)) + [0]:
        project_rows(((y + slot) % n_y) * span)
        if slot == (1 if n_y > 1 else 0):
            w_copy.wait()

        def forward(k, slot=slot):
            ysend_ref[slot - 1, k] = chip_sum(slot, k).astype(jnp.bfloat16)
            y_copy(slot, k).start()

        def column(k, _, slot=slot):
            project(slot, k)
            if slot > 0:

                @pl.when(k > 0)
                def _():
                    forward(k - 1)

            return 0

        lax.fori_loop(0, n_chunks, column, 0)
        if slot > 0:
            forward(n_chunks - 1)

    def finish(k, _):
        total = chip_sum(0, k)
        for slot in range(1, n_y):
            y_copy(slot, k).wait_recv()
            total = total + yrecv_ref[slot - 1, k].astype(jnp.float32)
        cols = pl.ds(pl.multiple_of(k * chunk, chunk), chunk)
        out_ref[:, cols] = total.astype(jnp.bfloat16)
        return 0

    lax.fori_loop(0, n_chunks, finish, 0)

    halo_m.wait_send()
    halo_x.wait_send()
    dec_copy.wait_send()

    def drain_states(p, _):
        pair_copy(p).wait_send()

        @pl.when(z < n_z - 1)
        def _():
            chain_copy(p).wait_send()

        return 0

    lax.fori_loop(0, pairs, drain_states, 0)

    def drain_parts(k, _):
        for slot in range(n_y):
            core_copy(slot, k).wait_send()
        for slot in range(1, n_y):
            y_copy(slot, k).wait_send()
        return 0

    lax.fori_loop(0, n_chunks, drain_parts, 0)


def on_device(n_ctx, n_tp, *args):
    (x_inputs, state_maps, z_gate, step_raw, step_bias, decay_log, skip_gain,
     x_filter, state_filter, norm_gain, out_weight) = args
    length, channels = x_inputs.shape
    heads = step_raw.shape[1]
    pairs = channels // LANES
    model = out_weight.shape[1]
    rows = length // n_tp
    n_y = n_tp // 2
    chunk = 512
    n_chunks = model // chunk
    state = state_maps.shape[1] // 2
    bf16, f32 = jnp.bfloat16, jnp.float32
    vmem = pl.BlockSpec(memory_space=pltpu.VMEM)
    dma = pltpu.SemaphoreType.DMA
    scratch = [
        pltpu.VMEM(out_weight.shape, bf16),
        pltpu.VMEM((HALO, channels), bf16),
        pltpu.VMEM((HALO, 2 * state), bf16),
        pltpu.VMEM((length + 8, LANES), f32),
        pltpu.VMEM((pairs, x_filter.shape[0], LANES), f32),
        pltpu.VMEM((2, x_filter.shape[0], LANES), f32),
        pltpu.VMEM((pairs, 8, LANES), f32),
        pltpu.VMEM((pairs, 8, LANES), f32),
        pltpu.VMEM((length, LANES), f32),
        pltpu.VMEM((LANES, LANES), f32),
        pltpu.VMEM((heads, length), f32),
        pltpu.VMEM((heads, length), f32),
        pltpu.VMEM((pairs, length, LANES), f32),
        pltpu.VMEM((pairs, 8, LANES), f32),
        pltpu.VMEM((pairs, 8, LANES), f32),
        pltpu.VMEM((pairs, length, LANES), bf16),
        pltpu.VMEM((state, length), bf16),
        pltpu.VMEM((length, state), bf16),
        pltpu.VMEM((length, length), f32),
        pltpu.VMEM((pairs, state, LANES), f32),
        pltpu.VMEM((pairs, state, LANES), bf16),
        pltpu.VMEM((pairs, state, LANES), bf16),
        pltpu.VMEM((pairs, state, LANES), bf16),
        pltpu.VMEM((pairs, state, LANES), bf16),
        pltpu.VMEM((pairs, state, LANES), bf16),
        pltpu.VMEM((pairs, length, LANES), f32),
        pltpu.VMEM((pairs, length, LANES), f32),
        pltpu.VMEM((pairs, 2 * rows, LANES), f32),
        pltpu.VMEM((2 * rows, channels), bf16),
        pltpu.VMEM((n_y, n_chunks, 2, rows, chunk), bf16),
        pltpu.VMEM((n_y, n_chunks, rows, chunk), bf16),
        pltpu.VMEM((n_y - 1, n_chunks, rows, chunk), bf16),
        pltpu.VMEM((n_y - 1, n_chunks, rows, chunk), bf16),
        dma, dma((2,)), dma((2,)), dma, dma,
        dma((pairs,)), dma((pairs,)), dma((pairs,)), dma((pairs,)),
        dma((n_y, n_chunks)), dma((n_y, n_chunks)),
        dma((n_y - 1, n_chunks)), dma((n_y - 1, n_chunks)),
    ]
    return pl.pallas_call(
        functools.partial(layer_kernel, n_ctx, n_tp, chunk),
        out_shape=jax.ShapeDtypeStruct((rows, model), bf16),
        in_specs=[vmem] * 10 + [pl.BlockSpec(memory_space=pl.ANY)],
        out_specs=vmem,
        scratch_shapes=scratch,
        compiler_params=pltpu.CompilerParams(
            collective_id=0, has_side_effects=True, vmem_limit_bytes=58 * 1024 * 1024
        ),
        cost_estimate=pl.CostEstimate(
            flops=2 * length * channels * (model + 2 * length), bytes_accessed=4 * out_weight.size,
            transcendentals=length * length * heads,
        ),
        name="layer",
    )(
        x_inputs, state_maps, z_gate, step_raw, step_bias[None], decay_log[None], skip_gain[None],
        x_filter, state_filter, norm_gain[None], out_weight,
    )


def solution(mesh):
    return jax.shard_map(
        functools.partial(on_device, mesh.shape["ctx"], mesh.shape["tp"]),
        mesh=mesh,
        in_specs=(
            P("ctx", "tp"),
            P("ctx", "tp"),
            P("ctx", "tp"),
            P("ctx", "tp"),
            P("tp"),
            P("tp"),
            P("tp"),
            P(None, "tp"),
            P(None, "tp"),
            P("tp"),
            P("tp", None),
        ),
        out_specs=P(("ctx", "tp"), None),
        check_vma=False,
    )
```

```python
import functools

import jax
import jax.numpy as jnp
from jax import lax
from jax.experimental import pallas as pl
from jax.experimental.pallas import tpu as pltpu
from jax.sharding import PartitionSpec as P

MESH = pl.DeviceIdType.MESH
LANES = 128
HALO = 16


def half_silu(v):
    h = 0.5 * v
    return h + h * jnp.tanh(h)


def layer_kernel(
    n_ctx, n_tp, chunk,
    x_ref, m_ref, z_ref, step_ref, bias_ref, decay_ref, skip_ref, xf_ref, mf_ref, gain_ref, w_hbm,
    out_ref,
    w_ref, hx_ref, hm_ref, pad_ref, xfs_ref, mfs_ref, gains_ref, skips_ref,
    sq_ref, parts_ref, left_ref, right_ref, dsend_ref, drecv_ref,
    xc_ref, bt_ref, c_ref, cb_ref, lown_ref, lsend_ref, lrecv_ref, csend_ref, crecv_ref, sr_ref,
    yg_ref, eg_ref, gated_ref, normed_ref, part_ref, core_ref, ysend_ref, yrecv_ref, out_buf,
    w_sem, out_sem, halo_send, halo_recv, dec_send, dec_recv, pair_send, pair_recv, chain_send, chain_recv,
    core_send, core_recv, y_send, y_recv,
):
    length = x_ref.shape[0]
    pairs = x_ref.shape[1] // LANES
    heads = step_ref.shape[0]
    n_y = n_tp // 2
    rows = length // n_tp
    n_chunks = w_hbm.shape[1] // chunk
    n_z = n_ctx // 2
    ctx = lax.axis_index("ctx")
    tp = lax.axis_index("tp")
    y, core = tp // 2, tp % 2
    z, odd = ctx // 2, ctx % 2
    mate = ctx + 1 - 2 * odd
    other_core = y * 2 + 1 - core

    w_copy = pltpu.make_async_copy(w_hbm, w_ref, w_sem)
    w_copy.start()

    barrier = pltpu.get_barrier_semaphore()
    for off in (1, n_ctx - 1, 2, n_ctx - 2):
        pl.semaphore_signal(barrier, inc=1, device_id={"ctx": (ctx + off) % n_ctx}, device_id_type=MESH)
    pl.semaphore_signal(barrier, inc=1, device_id={"tp": other_core}, device_id_type=MESH)
    for off in range(1, n_y):
        pl.semaphore_signal(
            barrier, inc=1, device_id={"tp": ((y + off) % n_y) * 2 + core}, device_id_type=MESH
        )

    def remote(src, dst, send, recv, where):
        return pltpu.make_async_remote_copy(
            src_ref=src, dst_ref=dst, send_sem=send, recv_sem=recv, device_id=where, device_id_type=MESH
        )

    def lane_column(ref):
        sq_ref[...] = jnp.zeros_like(sq_ref)
        sq_ref[:, :heads] = jnp.broadcast_to(ref[...], (LANES, heads))
        return sq_ref[...].T

    def three_terms(v):
        first = v.astype(jnp.bfloat16).astype(jnp.float32)
        second = (v - first).astype(jnp.bfloat16).astype(jnp.float32)
        return [first, second, (v - first - second).astype(jnp.bfloat16).astype(jnp.float32)]

    def all_tokens(column):
        return jnp.concatenate([column[:heads]] * (length // LANES), axis=1)

    step = jnp.log(1.0 + jnp.exp(step_ref[...] + all_tokens(lane_column(bias_ref))))
    rate = step * jnp.exp(all_tokens(lane_column(decay_ref)))
    skip_t = lane_column(skip_ref)
    s_ids = lax.broadcasted_iota(jnp.int32, (length, length), 0)
    t_ids = lax.broadcasted_iota(jnp.int32, (length, length), 1)
    upper = jnp.where(s_ids <= t_ids, 1.0, 0.0).astype(jnp.bfloat16)
    sums = jnp.dot(
        jnp.concatenate(three_terms(rate), axis=0).astype(jnp.bfloat16), upper,
        preferred_element_type=jnp.float32,
    )
    sums = sums[:heads] + sums[heads : 2 * heads] + sums[2 * heads :]
    source = sums + jnp.log(step)
    filler = jnp.ones((LANES - 6 * heads, length), jnp.float32)
    parts_ref[...] = jnp.concatenate(three_terms(sums) + three_terms(source) + [filler], axis=0)
    left_ref[...] = parts_ref[...].T.astype(jnp.bfloat16)

    pl.semaphore_wait(barrier, 4 + 1 + (n_y - 1))

    following = {"ctx": (ctx + 1) % n_ctx}
    halo_x = remote(x_ref.at[pl.ds(length - HALO, HALO)], hx_ref, halo_send.at[0], halo_recv.at[0], following)
    halo_m = remote(m_ref.at[pl.ds(length - HALO, HALO)], hm_ref, halo_send.at[1], halo_recv.at[1], following)
    halo_m.start()
    halo_x.start()

    lane_row = lax.broadcasted_iota(jnp.int32, (1, LANES), 1) < LANES // 2
    x_taps = xf_ref[...].astype(jnp.float32)
    m_taps = mf_ref[...].astype(jnp.float32)
    for p in range(pairs):
        skips_ref[p] = jnp.broadcast_to(
            jnp.where(lane_row, skip_t[2 * p : 2 * p + 1], skip_t[2 * p + 1 : 2 * p + 2]), (8, LANES)
        )
        gains_ref[p] = jnp.broadcast_to(gain_ref[:, p * LANES : (p + 1) * LANES], (8, LANES))
        xfs_ref[p] = x_taps[:, p * LANES : (p + 1) * LANES]
    for p in range(2):
        mfs_ref[p] = m_taps[:, p * LANES : (p + 1) * LANES]

    def picker(p, base):
        row = lax.broadcasted_iota(jnp.int32, (LANES, LANES), 0) - base
        head = 2 * p + (lax.broadcasted_iota(jnp.int32, (LANES, LANES), 1) >= LANES // 2).astype(jnp.int32)
        hit = (row == head) | (row == head + heads) | (row == head + 2 * heads)
        return jnp.where(hit, 1.0, 0.0).astype(jnp.bfloat16)

    def by_pair(start, p, base):
        return jnp.dot(left_ref[start:, :], picker(p, base), preferred_element_type=jnp.float32)

    def expand(p, _):
        last = by_pair(length - HALO, p, 0)
        dsend_ref[p] = jnp.broadcast_to(last[HALO - 1 :], (8, LANES))
        return 0

    lax.fori_loop(0, pairs, expand, 0)
    dec_copy = remote(dsend_ref, drecv_ref, dec_send, dec_recv, {"ctx": mate})
    dec_copy.start()

    taps = xf_ref.shape[0]
    has_prev = jnp.where(ctx > 0, 1.0, 0.0).astype(jnp.float32)

    def conv(block, halo, filters):
        pad_ref[0:8] = halo.astype(jnp.float32)[HALO - 8 :] * has_prev
        pad_ref[8:] = block.astype(jnp.float32)
        total = filters[0:1] * pad_ref[9 - taps : 9 - taps + length]
        for k in range(1, taps):
            start = 9 - taps + k
            total = total + filters[k : k + 1] * pad_ref[start : start + length]
        return half_silu(total)

    halo_m.wait_recv()
    bt_ref[...] = conv(m_ref[:, :LANES], hm_ref[:, :LANES], mfs_ref[0]).T.astype(jnp.bfloat16)
    c_ref[...] = conv(m_ref[:, LANES:], hm_ref[:, LANES:], mfs_ref[1]).astype(jnp.bfloat16)
    halo_x.wait_recv()

    def pair_copy(p):
        return remote(lsend_ref.at[p], lrecv_ref.at[p], pair_send.at[p], pair_recv.at[p], {"ctx": mate})

    def local_state(p):
        cols = pl.ds(pl.multiple_of(p * LANES, LANES), LANES)
        xc = conv(x_ref[:, cols], hx_ref[:, cols], xfs_ref[p]).astype(jnp.bfloat16)
        xc_ref[p] = xc
        tail = jnp.exp(by_pair(0, p, 3 * heads) - dsend_ref[p][0:1])
        u = (tail * xc.astype(jnp.float32)).astype(jnp.bfloat16)
        state = jnp.dot(bt_ref[...], u, preferred_element_type=jnp.float32)
        lown_ref[p] = state
        lsend_ref[p] = state.astype(jnp.bfloat16)
        pair_copy(p).start()

    scores = jnp.dot(c_ref[...], bt_ref[...], preferred_element_type=jnp.float32)
    cb_ref[...] = jnp.where(s_ids >= t_ids, scores, 0.0)

    is_odd = odd.astype(jnp.float32)
    is_even = 1.0 - is_odd
    next_pair = {"ctx": (ctx + 2) % n_ctx}

    def chain_copy(p):
        return remote(csend_ref.at[p], crecv_ref.at[p], chain_send.at[p], chain_recv.at[p], next_pair)

    @pl.when(z == 0)
    def _():
        crecv_ref[...] = jnp.zeros_like(crecv_ref)

    dec_copy.wait_recv()

    def relay(p):
        pair_copy(p).wait_recv()
        mine = lown_ref[p]
        theirs = lrecv_ref[p].astype(jnp.float32)
        d_mine = jnp.exp(-dsend_ref[p][0:1])
        d_theirs = jnp.exp(-drecv_ref[p][0:1])
        l_even = mine * is_even + theirs * is_odd
        l_odd = mine * is_odd + theirs * is_even
        d_even = d_mine * is_even + d_theirs * is_odd
        d_odd = d_mine * is_odd + d_theirs * is_even

        @pl.when(z > 0)
        def _():
            chain_copy(p).wait_recv()

        entering = crecv_ref[p].astype(jnp.float32)
        middle = d_even * entering + l_even
        sr_ref[p] = (entering * is_even + middle * is_odd).astype(jnp.bfloat16)

        @pl.when(z < n_z - 1)
        def _():
            csend_ref[p] = (d_odd * middle + l_odd).astype(jnp.bfloat16)
            chain_copy(p).start()

    half = length // 2
    low_lanes = lax.broadcasted_iota(jnp.int32, (half, LANES), 1) < LANES // 2

    row_ids = lax.broadcasted_iota(jnp.int32, (LANES, length), 0)

    def within(p):
        xc = xc_ref[p]
        tops, bottoms = [], []
        for h in range(2):
            head = 2 * p + h
            hit = (row_ids == head) | (row_ids == head + heads) | (row_ids == head + 2 * heads)
            right = jnp.where(hit, -1.0, 0.0)
            for term in range(3):
                row = parts_ref[pl.ds((3 + term) * heads + head, 1), :]
                right = jnp.where(row_ids == 6 * heads + term, row, right)
            right_ref[...] = right.astype(jnp.bfloat16)

            def weigh(t0, s0, masked):
                power = jnp.dot(
                    left_ref[t0 : t0 + half, :], right_ref[:, s0 : s0 + half],
                    preferred_element_type=jnp.float32,
                )
                if masked:
                    power = jnp.minimum(power, 64.0)
                return (jnp.exp(power) * cb_ref[t0 : t0 + half, s0 : s0 + half]).astype(jnp.bfloat16)

            tops.append(jnp.dot(weigh(0, 0, True), xc[:half], preferred_element_type=jnp.float32))
            bottoms.append(
                jnp.dot(weigh(half, 0, False), xc[:half], preferred_element_type=jnp.float32)
                + jnp.dot(weigh(half, half, True), xc[half:], preferred_element_type=jnp.float32)
            )
        cols = pl.ds(pl.multiple_of(p * LANES, LANES), LANES)
        skip = skips_ref[p][0:1]
        decay = jnp.exp(-by_pair(0, p, 0))
        for t0, both in ((0, tops), (half, bottoms)):
            here = pl.ds(t0, half)
            gate = half_silu(z_ref[here, cols].astype(jnp.float32))
            own = jnp.where(low_lanes, both[0], both[1])
            yg_ref[p, here] = (own + skip * xc[t0 : t0 + half].astype(jnp.float32)) * gate
            eg_ref[p, here] = decay[t0 : t0 + half] * gate

    lag = jnp.minimum(3 + 3 * z, 2 * pairs)

    def turn(i, _):
        @pl.when((i >= lag) & (i < lag + pairs))
        def _():
            relay(i - lag)

        @pl.when(i < pairs)
        def _():
            local_state(i)

        @pl.when((i >= pairs) & (i < 2 * pairs))
        def _():
            within(i - pairs)

        return 0

    lax.fori_loop(0, 3 * pairs, turn, 0)

    span = 2 * rows
    channels = x_ref.shape[1]

    def project_rows(first):
        here = pl.ds(pl.multiple_of(first, span), span)
        c_rows = c_ref[here, :]

        def gate_pair(p, total):
            inter = jnp.dot(c_rows, sr_ref[p], preferred_element_type=jnp.float32)
            gated = yg_ref[p, here] + eg_ref[p, here] * inter
            gated_ref[p] = gated
            return total + gated * gated

        squares = lax.fori_loop(0, pairs, gate_pair, jnp.zeros((span, LANES), jnp.float32))
        scale = lax.rsqrt(jnp.sum(squares, axis=1, keepdims=True) / channels + 1e-05)
        for p in range(pairs):
            normed_ref[:, p * LANES : (p + 1) * LANES] = (
                gated_ref[p] * scale * gains_ref[p][0:1]
            ).astype(jnp.bfloat16)

    def core_copy(slot, k):
        return remote(
            part_ref.at[slot, k, 1 - core], core_ref.at[slot, k],
            core_send.at[slot, k], core_recv.at[slot, k], {"tp": other_core},
        )

    def y_copy(slot, k):
        target = ((y + slot) % n_y) * 2 + core
        return remote(
            ysend_ref.at[slot - 1, k], yrecv_ref.at[slot - 1, k],
            y_send.at[slot - 1, k], y_recv.at[slot - 1, k], {"tp": target},
        )

    def project(slot, k):
        cols = pl.ds(pl.multiple_of(k * chunk, chunk), chunk)
        part = jnp.dot(normed_ref[...], w_ref[:, cols], preferred_element_type=jnp.float32)
        part = part.astype(jnp.bfloat16)
        part_ref[slot, k, 0] = part[:rows]
        part_ref[slot, k, 1] = part[rows:]
        core_copy(slot, k).start()

    def chip_sum(slot, k):
        core_copy(slot, k).wait_recv()
        return part_ref[slot, k, core].astype(jnp.float32) + core_ref[slot, k].astype(jnp.float32)

    for slot in list(range(1, n_y)) + [0]:
        project_rows(((y + slot) % n_y) * span)
        if slot == (1 if n_y > 1 else 0):
            w_copy.wait()

        def forward(k, slot=slot):
            ysend_ref[slot - 1, k] = chip_sum(slot, k).astype(jnp.bfloat16)
            y_copy(slot, k).start()

        def column(k, _, slot=slot):
            project(slot, k)
            if slot > 0:

                @pl.when(k > 0)
                def _():
                    forward(k - 1)

            return 0

        lax.fori_loop(0, n_chunks, column, 0)
        if slot > 0:
            forward(n_chunks - 1)

    def out_copy(k):
        cols = pl.ds(pl.multiple_of(k * chunk, chunk), chunk)
        return pltpu.make_async_copy(out_buf.at[k], out_ref.at[:, cols], out_sem.at[k])

    def finish(k, _):
        total = chip_sum(0, k)
        for slot in range(1, n_y):
            y_copy(slot, k).wait_recv()
            total = total + yrecv_ref[slot - 1, k].astype(jnp.float32)
        out_buf[k] = total.astype(jnp.bfloat16)
        out_copy(k).start()
        return 0

    lax.fori_loop(0, n_chunks, finish, 0)

    halo_m.wait_send()
    halo_x.wait_send()
    dec_copy.wait_send()

    def drain_states(p, _):
        pair_copy(p).wait_send()

        @pl.when(z < n_z - 1)
        def _():
            chain_copy(p).wait_send()

        return 0

    lax.fori_loop(0, pairs, drain_states, 0)

    def drain_parts(k, _):
        out_copy(k).wait()
        for slot in range(n_y):
            core_copy(slot, k).wait_send()
        for slot in range(1, n_y):
            y_copy(slot, k).wait_send()
        return 0

    lax.fori_loop(0, n_chunks, drain_parts, 0)


def on_device(n_ctx, n_tp, *args):
    (x_inputs, state_maps, z_gate, step_raw, step_bias, decay_log, skip_gain,
     x_filter, state_filter, norm_gain, out_weight) = args
    length, channels = x_inputs.shape
    heads = step_raw.shape[1]
    pairs = channels // LANES
    model = out_weight.shape[1]
    rows = length // n_tp
    n_y = n_tp // 2
    chunk = 512
    n_chunks = model // chunk
    state = state_maps.shape[1] // 2
    bf16, f32 = jnp.bfloat16, jnp.float32
    vmem = pl.BlockSpec(memory_space=pltpu.VMEM)
    dma = pltpu.SemaphoreType.DMA
    scratch = [
        pltpu.VMEM(out_weight.shape, bf16),
        pltpu.VMEM((HALO, channels), bf16),
        pltpu.VMEM((HALO, 2 * state), bf16),
        pltpu.VMEM((length + 8, LANES), f32),
        pltpu.VMEM((pairs, x_filter.shape[0], LANES), f32),
        pltpu.VMEM((2, x_filter.shape[0], LANES), f32),
        pltpu.VMEM((pairs, 8, LANES), f32),
        pltpu.VMEM((pairs, 8, LANES), f32),
        pltpu.VMEM((LANES, LANES), f32),
        pltpu.VMEM((LANES, length), f32),
        pltpu.VMEM((length, LANES), bf16),
        pltpu.VMEM((LANES, length), bf16),
        pltpu.VMEM((pairs, 8, LANES), f32),
        pltpu.VMEM((pairs, 8, LANES), f32),
        pltpu.VMEM((pairs, length, LANES), bf16),
        pltpu.VMEM((state, length), bf16),
        pltpu.VMEM((length, state), bf16),
        pltpu.VMEM((length, length), f32),
        pltpu.VMEM((pairs, state, LANES), f32),
        pltpu.VMEM((pairs, state, LANES), bf16),
        pltpu.VMEM((pairs, state, LANES), bf16),
        pltpu.VMEM((pairs, state, LANES), bf16),
        pltpu.VMEM((pairs, state, LANES), bf16),
        pltpu.VMEM((pairs, state, LANES), bf16),
        pltpu.VMEM((pairs, length, LANES), f32),
        pltpu.VMEM((pairs, length, LANES), f32),
        pltpu.VMEM((pairs, 2 * rows, LANES), f32),
        pltpu.VMEM((2 * rows, channels), bf16),
        pltpu.VMEM((n_y, n_chunks, 2, rows, chunk), bf16),
        pltpu.VMEM((n_y, n_chunks, rows, chunk), bf16),
        pltpu.VMEM((n_y - 1, n_chunks, rows, chunk), bf16),
        pltpu.VMEM((n_y - 1, n_chunks, rows, chunk), bf16),
        pltpu.VMEM((n_chunks, rows, chunk), bf16),
        dma, dma((n_chunks,)), dma((2,)), dma((2,)), dma, dma,
        dma((pairs,)), dma((pairs,)), dma((pairs,)), dma((pairs,)),
        dma((n_y, n_chunks)), dma((n_y, n_chunks)),
        dma((n_y - 1, n_chunks)), dma((n_y - 1, n_chunks)),
    ]
    return pl.pallas_call(
        functools.partial(layer_kernel, n_ctx, n_tp, chunk),
        out_shape=jax.ShapeDtypeStruct((rows, model), bf16),
        in_specs=[vmem] * 10 + [pl.BlockSpec(memory_space=pl.ANY)],
        out_specs=pl.BlockSpec(memory_space=pl.ANY),
        scratch_shapes=scratch,
        compiler_params=pltpu.CompilerParams(
            collective_id=0, has_side_effects=True, vmem_limit_bytes=58 * 1024 * 1024
        ),
        cost_estimate=pl.CostEstimate(
            flops=2 * length * channels * (model + 2 * length), bytes_accessed=4 * out_weight.size,
            transcendentals=length * length * heads,
        ),
        name="layer",
    )(
        x_inputs, state_maps, z_gate, step_raw.T, step_bias[None], decay_log[None], skip_gain[None],
        x_filter, state_filter, norm_gain[None], out_weight,
    )


def solution(mesh):
    return jax.shard_map(
        functools.partial(on_device, mesh.shape["ctx"], mesh.shape["tp"]),
        mesh=mesh,
        in_specs=(
            P("ctx", "tp"),
            P("ctx", "tp"),
            P("ctx", "tp"),
            P("ctx", "tp"),
            P("tp"),
            P("tp"),
            P("tp"),
            P(None, "tp"),
            P(None, "tp"),
            P("tp"),
            P("tp", None),
        ),
        out_specs=P(("ctx", "tp"), None),
        check_vma=False,
    )
```

```python
import functools

import jax
import jax.numpy as jnp
from jax import lax
from jax.experimental import pallas as pl
from jax.experimental.pallas import tpu as pltpu
from jax.sharding import PartitionSpec as P

MESH = pl.DeviceIdType.MESH
LANES = 128
HALO = 16


def half_silu(v):
    h = 0.5 * v
    return h + h * jnp.tanh(h)


def layer_kernel(
    n_ctx, n_tp, chunk,
    x_ref, m_ref, z_ref, step_ref, bias_ref, decay_ref, skip_ref, xf_ref, mf_ref, gain_ref, w_hbm,
    out_ref,
    w_ref, hx_ref, hm_ref, pad_ref, xfs_ref, mfs_ref, gains_ref, skips_ref,
    sq_ref, parts_ref, left_ref, pick_ref, dsend_ref, drecv_ref,
    xc_ref, uc_ref, aexp_ref, mid_ref, first_ref, bt_ref, c_ref, cb_ref, lown_ref, lsend_ref, lrecv_ref, csend_ref, crecv_ref, sr_ref,
    yg_ref, eg_ref, gated_ref, normed_ref, part_ref, core_ref, ysend_ref, yrecv_ref, out_buf,
    w_sem, out_sem, halo_send, halo_recv, dec_send, dec_recv, pair_send, pair_recv, chain_send, chain_recv,
    core_send, core_recv, y_send, y_recv,
):
    length = x_ref.shape[0]
    pairs = x_ref.shape[1] // LANES
    heads = step_ref.shape[0]
    n_y = n_tp // 2
    rows = length // n_tp
    n_chunks = w_hbm.shape[1] // chunk
    n_z = n_ctx // 2
    ctx = lax.axis_index("ctx")
    tp = lax.axis_index("tp")
    y, core = tp // 2, tp % 2
    z, odd = ctx // 2, ctx % 2
    mate = ctx + 1 - 2 * odd
    other_core = y * 2 + 1 - core

    w_copy = pltpu.make_async_copy(w_hbm, w_ref, w_sem)
    w_copy.start()

    barrier = pltpu.get_barrier_semaphore()
    for off in (1, n_ctx - 1, 2, n_ctx - 2):
        pl.semaphore_signal(barrier, inc=1, device_id={"ctx": (ctx + off) % n_ctx}, device_id_type=MESH)
    pl.semaphore_signal(barrier, inc=1, device_id={"tp": other_core}, device_id_type=MESH)
    for off in range(1, n_y):
        pl.semaphore_signal(
            barrier, inc=1, device_id={"tp": ((y + off) % n_y) * 2 + core}, device_id_type=MESH
        )

    def remote(src, dst, send, recv, where):
        return pltpu.make_async_remote_copy(
            src_ref=src, dst_ref=dst, send_sem=send, recv_sem=recv, device_id=where, device_id_type=MESH
        )

    def lane_column(ref):
        sq_ref[...] = jnp.zeros_like(sq_ref)
        sq_ref[:, :heads] = jnp.broadcast_to(ref[...], (LANES, heads))
        return sq_ref[...].T

    def three_terms(v):
        first = v.astype(jnp.bfloat16).astype(jnp.float32)
        second = (v - first).astype(jnp.bfloat16).astype(jnp.float32)
        return [first, second, (v - first - second).astype(jnp.bfloat16).astype(jnp.float32)]

    def all_tokens(column):
        return jnp.concatenate([column[:heads]] * (length // LANES), axis=1)

    step = jnp.log(1.0 + jnp.exp(step_ref[...] + all_tokens(lane_column(bias_ref))))
    rate = step * jnp.exp(all_tokens(lane_column(decay_ref)))
    skip_t = lane_column(skip_ref)
    s_ids = lax.broadcasted_iota(jnp.int32, (length, length), 0)
    t_ids = lax.broadcasted_iota(jnp.int32, (length, length), 1)
    upper = jnp.where(s_ids <= t_ids, 1.0, 0.0).astype(jnp.bfloat16)
    sums = jnp.dot(
        jnp.concatenate(three_terms(rate), axis=0).astype(jnp.bfloat16), upper,
        preferred_element_type=jnp.float32,
    )
    sums = sums[:heads] + sums[heads : 2 * heads] + sums[2 * heads :]
    source = sums + jnp.log(step)
    filler = jnp.ones((LANES - 6 * heads, length), jnp.float32)
    parts_ref[...] = jnp.concatenate(three_terms(sums) + three_terms(source) + [filler], axis=0)
    left_ref[...] = parts_ref[...].T.astype(jnp.bfloat16)

    pl.semaphore_wait(barrier, 4 + 1 + (n_y - 1))

    following = {"ctx": (ctx + 1) % n_ctx}
    halo_x = remote(x_ref.at[pl.ds(length - HALO, HALO)], hx_ref, halo_send.at[0], halo_recv.at[0], following)
    halo_m = remote(m_ref.at[pl.ds(length - HALO, HALO)], hm_ref, halo_send.at[1], halo_recv.at[1], following)
    halo_m.start()
    halo_x.start()

    lane_row = lax.broadcasted_iota(jnp.int32, (1, LANES), 1) < LANES // 2
    x_taps = xf_ref[...].astype(jnp.float32)
    m_taps = mf_ref[...].astype(jnp.float32)
    for p in range(pairs):
        skips_ref[p] = jnp.broadcast_to(
            jnp.where(lane_row, skip_t[2 * p : 2 * p + 1], skip_t[2 * p + 1 : 2 * p + 2]), (8, LANES)
        )
        gains_ref[p] = jnp.broadcast_to(gain_ref[:, p * LANES : (p + 1) * LANES], (8, LANES))
        xfs_ref[p] = x_taps[:, p * LANES : (p + 1) * LANES]
    for p in range(2):
        mfs_ref[p] = m_taps[:, p * LANES : (p + 1) * LANES]

    channels = x_ref.shape[1]
    term = lax.broadcasted_iota(jnp.int32, (LANES, channels), 0)
    owner = lax.broadcasted_iota(jnp.int32, (LANES, channels), 1) // (channels // heads)
    match = term % heads == owner
    pick_sum = jnp.where(match & (term < 3 * heads), 1.0, 0.0).astype(jnp.bfloat16)
    pick_source = jnp.where(match & (term >= 3 * heads) & (term < 6 * heads), 1.0, 0.0).astype(jnp.bfloat16)
    last = jnp.dot(left_ref[length - HALO :, :], pick_sum, preferred_element_type=jnp.float32)[HALO - 1 :]
    for p in range(pairs):
        cols = slice(p * LANES, (p + 1) * LANES)
        pick_ref[p, :, :LANES] = pick_sum[:, cols]
        pick_ref[p, :, LANES:] = pick_source[:, cols]
        dsend_ref[p] = jnp.broadcast_to(last[:, cols], (8, LANES))
    dec_copy = remote(dsend_ref, drecv_ref, dec_send, dec_recv, {"ctx": mate})
    dec_copy.start()

    taps = xf_ref.shape[0]
    has_prev = jnp.where(ctx > 0, 1.0, 0.0).astype(jnp.float32)

    def conv(block, halo, filters, slot):
        pad_ref[slot, 0:8] = halo.astype(jnp.float32)[HALO - 8 :] * has_prev
        pad_ref[slot, 8:] = block.astype(jnp.float32)
        total = filters[0:1] * pad_ref[slot, 9 - taps : 9 - taps + length]
        for k in range(1, taps):
            start = 9 - taps + k
            total = total + filters[k : k + 1] * pad_ref[slot, start : start + length]
        return half_silu(total)

    halo_m.wait_recv()
    bt_ref[...] = conv(m_ref[:, :LANES], hm_ref[:, :LANES], mfs_ref[0], 0).T.astype(jnp.bfloat16)
    c_ref[...] = conv(m_ref[:, LANES:], hm_ref[:, LANES:], mfs_ref[1], 1).astype(jnp.bfloat16)
    halo_x.wait_recv()

    def pair_copy(p):
        return remote(lsend_ref.at[p], lrecv_ref.at[p], pair_send.at[p], pair_recv.at[p], {"ctx": mate})

    half = length // 2

    def local_state(p, slot):
        cols = pl.ds(pl.multiple_of(p * LANES, LANES), LANES)
        xc = conv(x_ref[:, cols], hx_ref[:, cols], xfs_ref[p], slot).astype(jnp.bfloat16)
        xc_ref[p] = xc
        both = jnp.dot(left_ref[...], pick_ref[p], preferred_element_type=jnp.float32)
        sums, source = both[:, :LANES], both[:, LANES:]
        aexp_ref[p] = sums
        wide = xc.astype(jnp.float32)
        end = dsend_ref[p][0:1]
        border = sums[half - 1 : half]
        mids, states = [], []
        for j, stop in ((0, border), (1, end)):
            here = slice(j * half, (j + 1) * half)
            mid = sums[j * half + half // 2 - 1 : j * half + half // 2]
            mid_ref[p, j] = jnp.broadcast_to(mid, (8, LANES))
            u = (jnp.exp(source[here] - mid) * wide[here]).astype(jnp.bfloat16)
            uc_ref[p, here] = u
            fresh = jnp.dot(bt_ref[:, here], u, preferred_element_type=jnp.float32)
            mids.append(mid)
            states.append(fresh * jnp.exp(mid - stop))
        first_ref[p] = (states[0] * jnp.exp(border - mids[1])).astype(jnp.bfloat16)
        state = states[0] * jnp.exp(border - end) + states[1]
        lown_ref[p] = state
        lsend_ref[p] = state.astype(jnp.bfloat16)
        pair_copy(p).start()

    row_half = lax.broadcasted_iota(jnp.int32, (half, half), 0)
    col_half = lax.broadcasted_iota(jnp.int32, (half, half), 1)
    for j in range(2):
        here = slice(j * half, (j + 1) * half)
        scores = jnp.dot(c_ref[here, :], bt_ref[:, here], preferred_element_type=jnp.float32)
        cb_ref[j] = jnp.where(row_half >= col_half, scores, 0.0).astype(jnp.bfloat16)

    is_odd = odd.astype(jnp.float32)
    is_even = 1.0 - is_odd
    next_pair = {"ctx": (ctx + 2) % n_ctx}

    def chain_copy(p):
        return remote(csend_ref.at[p], crecv_ref.at[p], chain_send.at[p], chain_recv.at[p], next_pair)

    @pl.when(z == 0)
    def _():
        crecv_ref[...] = jnp.zeros_like(crecv_ref)

    dec_copy.wait_recv()

    def relay(p):
        pair_copy(p).wait_recv()
        mine = lown_ref[p]
        theirs = lrecv_ref[p].astype(jnp.float32)
        d_mine = jnp.exp(-dsend_ref[p][0:1])
        d_theirs = jnp.exp(-drecv_ref[p][0:1])
        l_even = mine * is_even + theirs * is_odd
        l_odd = mine * is_odd + theirs * is_even
        d_even = d_mine * is_even + d_theirs * is_odd
        d_odd = d_mine * is_odd + d_theirs * is_even

        @pl.when(z > 0)
        def _():
            chain_copy(p).wait_recv()

        entering = crecv_ref[p].astype(jnp.float32)
        middle = d_even * entering + l_even
        sr_ref[p] = (entering * is_even + middle * is_odd).astype(jnp.bfloat16)

        @pl.when(z < n_z - 1)
        def _():
            csend_ref[p] = (d_odd * middle + l_odd).astype(jnp.bfloat16)
            chain_copy(p).start()

    def within(p):
        cols = pl.ds(pl.multiple_of(p * LANES, LANES), LANES)
        skip = skips_ref[p][0:1]
        for j in range(2):
            here = slice(j * half, (j + 1) * half)
            own = jnp.dot(cb_ref[j], uc_ref[p, here], preferred_element_type=jnp.float32)
            if j == 1:
                own = own + jnp.dot(c_ref[here, :], first_ref[p], preferred_element_type=jnp.float32)
            mid = mid_ref[p, j][0:1]
            decay = jnp.exp(mid - aexp_ref[p, here])
            gate = half_silu(z_ref[here, cols].astype(jnp.float32))
            yg_ref[p, here] = (decay * own + skip * xc_ref[p, here].astype(jnp.float32)) * gate
            eg_ref[p, here] = decay * jnp.exp(-mid) * gate

    twos = pairs // 2
    lag = jnp.minimum(2 + 2 * z, 2 * twos)

    def turn(i, _):
        @pl.when((i >= lag) & (i < lag + twos))
        def _():
            for slot in range(2):
                relay(2 * (i - lag) + slot)

        @pl.when(i < twos)
        def _():
            for slot in range(2):
                local_state(2 * i + slot, slot)

        @pl.when((i >= twos) & (i < 2 * twos))
        def _():
            for slot in range(2):
                within(2 * (i - twos) + slot)

        return 0

    lax.fori_loop(0, 3 * twos, turn, 0)

    span = 2 * rows

    def project_rows(first):
        here = pl.ds(pl.multiple_of(first, span), span)
        c_rows = c_ref[here, :]

        def gate_pair(p, total):
            inter = jnp.dot(c_rows, sr_ref[p], preferred_element_type=jnp.float32)
            gated = yg_ref[p, here] + eg_ref[p, here] * inter
            gated_ref[p] = gated
            return total + gated * gated

        squares = lax.fori_loop(0, pairs, gate_pair, jnp.zeros((span, LANES), jnp.float32))
        scale = lax.rsqrt(jnp.sum(squares, axis=1, keepdims=True) / channels + 1e-05)
        for p in range(pairs):
            normed_ref[:, p * LANES : (p + 1) * LANES] = (
                gated_ref[p] * scale * gains_ref[p][0:1]
            ).astype(jnp.bfloat16)

    def core_copy(slot, k):
        return remote(
            part_ref.at[slot, k, 1 - core], core_ref.at[slot, k],
            core_send.at[slot, k], core_recv.at[slot, k], {"tp": other_core},
        )

    def y_copy(slot, k):
        target = ((y + slot) % n_y) * 2 + core
        return remote(
            ysend_ref.at[slot - 1, k], yrecv_ref.at[slot - 1, k],
            y_send.at[slot - 1, k], y_recv.at[slot - 1, k], {"tp": target},
        )

    def project(slot, k):
        cols = pl.ds(pl.multiple_of(k * chunk, chunk), chunk)
        part = jnp.dot(normed_ref[...], w_ref[:, cols], preferred_element_type=jnp.float32)
        part = part.astype(jnp.bfloat16)
        part_ref[slot, k, 0] = part[:rows]
        part_ref[slot, k, 1] = part[rows:]
        core_copy(slot, k).start()

    def chip_sum(slot, k):
        core_copy(slot, k).wait_recv()
        return part_ref[slot, k, core].astype(jnp.float32) + core_ref[slot, k].astype(jnp.float32)

    for slot in list(range(1, n_y)) + [0]:
        project_rows(((y + slot) % n_y) * span)
        if slot == (1 if n_y > 1 else 0):
            w_copy.wait()

        def forward(k, slot=slot):
            ysend_ref[slot - 1, k] = chip_sum(slot, k).astype(jnp.bfloat16)
            y_copy(slot, k).start()

        def column(k, _, slot=slot):
            project(slot, k)
            if slot > 0:

                @pl.when(k > 0)
                def _():
                    forward(k - 1)

            return 0

        lax.fori_loop(0, n_chunks, column, 0)
        if slot > 0:
            forward(n_chunks - 1)

    def out_copy(k):
        cols = pl.ds(pl.multiple_of(k * chunk, chunk), chunk)
        return pltpu.make_async_copy(out_buf.at[k], out_ref.at[:, cols], out_sem.at[k])

    def finish(k, _):
        total = chip_sum(0, k)
        for slot in range(1, n_y):
            y_copy(slot, k).wait_recv()
            total = total + yrecv_ref[slot - 1, k].astype(jnp.float32)
        out_buf[k] = total.astype(jnp.bfloat16)
        out_copy(k).start()
        return 0

    lax.fori_loop(0, n_chunks, finish, 0)

    halo_m.wait_send()
    halo_x.wait_send()
    dec_copy.wait_send()

    def drain_states(p, _):
        pair_copy(p).wait_send()

        @pl.when(z < n_z - 1)
        def _():
            chain_copy(p).wait_send()

        return 0

    lax.fori_loop(0, pairs, drain_states, 0)

    def drain_parts(k, _):
        out_copy(k).wait()
        for slot in range(n_y):
            core_copy(slot, k).wait_send()
        for slot in range(1, n_y):
            y_copy(slot, k).wait_send()
        return 0

    lax.fori_loop(0, n_chunks, drain_parts, 0)


def on_device(n_ctx, n_tp, *args):
    (x_inputs, state_maps, z_gate, step_raw, step_bias, decay_log, skip_gain,
     x_filter, state_filter, norm_gain, out_weight) = args
    length, channels = x_inputs.shape
    heads = step_raw.shape[1]
    pairs = channels // LANES
    model = out_weight.shape[1]
    rows = length // n_tp
    n_y = n_tp // 2
    chunk = 512
    n_chunks = model // chunk
    state = state_maps.shape[1] // 2
    bf16, f32 = jnp.bfloat16, jnp.float32
    vmem = pl.BlockSpec(memory_space=pltpu.VMEM)
    dma = pltpu.SemaphoreType.DMA
    scratch = [
        pltpu.VMEM(out_weight.shape, bf16),
        pltpu.VMEM((HALO, channels), bf16),
        pltpu.VMEM((HALO, 2 * state), bf16),
        pltpu.VMEM((2, length + 8, LANES), f32),
        pltpu.VMEM((pairs, x_filter.shape[0], LANES), f32),
        pltpu.VMEM((2, x_filter.shape[0], LANES), f32),
        pltpu.VMEM((pairs, 8, LANES), f32),
        pltpu.VMEM((pairs, 8, LANES), f32),
        pltpu.VMEM((LANES, LANES), f32),
        pltpu.VMEM((LANES, length), f32),
        pltpu.VMEM((length, LANES), bf16),
        pltpu.VMEM((pairs, LANES, 2 * LANES), bf16),
        pltpu.VMEM((pairs, 8, LANES), f32),
        pltpu.VMEM((pairs, 8, LANES), f32),
        pltpu.VMEM((pairs, length, LANES), bf16),
        pltpu.VMEM((pairs, length, LANES), bf16),
        pltpu.VMEM((pairs, length, LANES), f32),
        pltpu.VMEM((pairs, 2, 8, LANES), f32),
        pltpu.VMEM((pairs, state, LANES), bf16),
        pltpu.VMEM((state, length), bf16),
        pltpu.VMEM((length, state), bf16),
        pltpu.VMEM((2, length // 2, length // 2), bf16),
        pltpu.VMEM((pairs, state, LANES), f32),
        pltpu.VMEM((pairs, state, LANES), bf16),
        pltpu.VMEM((pairs, state, LANES), bf16),
        pltpu.VMEM((pairs, state, LANES), bf16),
        pltpu.VMEM((pairs, state, LANES), bf16),
        pltpu.VMEM((pairs, state, LANES), bf16),
        pltpu.VMEM((pairs, length, LANES), f32),
        pltpu.VMEM((pairs, length, LANES), f32),
        pltpu.VMEM((pairs, 2 * rows, LANES), f32),
        pltpu.VMEM((2 * rows, channels), bf16),
        pltpu.VMEM((n_y, n_chunks, 2, rows, chunk), bf16),
        pltpu.VMEM((n_y, n_chunks, rows, chunk), bf16),
        pltpu.VMEM((n_y - 1, n_chunks, rows, chunk), bf16),
        pltpu.VMEM((n_y - 1, n_chunks, rows, chunk), bf16),
        pltpu.VMEM((n_chunks, rows, chunk), bf16),
        dma, dma((n_chunks,)), dma((2,)), dma((2,)), dma, dma,
        dma((pairs,)), dma((pairs,)), dma((pairs,)), dma((pairs,)),
        dma((n_y, n_chunks)), dma((n_y, n_chunks)),
        dma((n_y - 1, n_chunks)), dma((n_y - 1, n_chunks)),
    ]
    return pl.pallas_call(
        functools.partial(layer_kernel, n_ctx, n_tp, chunk),
        out_shape=jax.ShapeDtypeStruct((rows, model), bf16),
        in_specs=[vmem] * 10 + [pl.BlockSpec(memory_space=pl.ANY)],
        out_specs=pl.BlockSpec(memory_space=pl.ANY),
        scratch_shapes=scratch,
        compiler_params=pltpu.CompilerParams(
            collective_id=0, has_side_effects=True, vmem_limit_bytes=58 * 1024 * 1024
        ),
        cost_estimate=pl.CostEstimate(
            flops=2 * length * channels * (model + 2 * length), bytes_accessed=4 * out_weight.size,
            transcendentals=length * length * heads,
        ),
        name="layer",
    )(
        x_inputs, state_maps, z_gate, step_raw.T, step_bias[None], decay_log[None], skip_gain[None],
        x_filter, state_filter, norm_gain[None], out_weight,
    )


def solution(mesh):
    return jax.shard_map(
        functools.partial(on_device, mesh.shape["ctx"], mesh.shape["tp"]),
        mesh=mesh,
        in_specs=(
            P("ctx", "tp"),
            P("ctx", "tp"),
            P("ctx", "tp"),
            P("ctx", "tp"),
            P("tp"),
            P("tp"),
            P("tp"),
            P(None, "tp"),
            P(None, "tp"),
            P("tp"),
            P("tp", None),
        ),
        out_specs=P(("ctx", "tp"), None),
        check_vma=False,
    )
```

```python
import functools

import jax
import jax.numpy as jnp
from jax import lax
from jax.experimental import pallas as pl
from jax.experimental.pallas import tpu as pltpu
from jax.sharding import PartitionSpec as P

MESH = pl.DeviceIdType.MESH
LANES = 128
HALO = 16


def half_silu(v):
    h = 0.5 * v
    return h + h * jnp.tanh(h)


def layer_kernel(
    n_ctx, n_tp, chunk,
    x_hbm, m_hbm, z_hbm, step_ref, bias_ref, decay_ref, skip_ref, xf_ref, mf_ref, gain_ref, w_hbm,
    out_ref,
    w_ref, x_ref, m_ref, z_ref, hx_ref, hm_ref, pad_ref, xfs_ref, mfs_ref, gains_ref, skips_ref,
    sq_ref, parts_ref, left_ref, pick_ref, dsend_ref, drecv_ref,
    xc_ref, uc_ref, aexp_ref, mid_ref, first_ref, bt_ref, c_ref, cb_ref, lown_ref, lsend_ref, lrecv_ref, csend_ref, crecv_ref, sr_ref,
    yg_ref, eg_ref, gated_ref, normed_ref, part_ref, core_ref, ysend_ref, yrecv_ref, out_buf,
    w_sem, in_sem, out_sem, halo_send, halo_recv, dec_send, dec_recv, pair_send, pair_recv, chain_send, chain_recv,
    core_send, core_recv, y_send, y_recv,
):
    length = x_ref.shape[0]
    pairs = x_ref.shape[1] // LANES
    heads = step_ref.shape[0]
    n_y = n_tp // 2
    rows = length // n_tp
    n_chunks = w_hbm.shape[1] // chunk
    n_z = n_ctx // 2
    ctx = lax.axis_index("ctx")
    tp = lax.axis_index("tp")
    y, core = tp // 2, tp % 2
    z, odd = ctx // 2, ctx % 2
    mate = ctx + 1 - 2 * odd
    other_core = y * 2 + 1 - core

    w_copy = pltpu.make_async_copy(w_hbm, w_ref, w_sem)
    m_copy = pltpu.make_async_copy(m_hbm, m_ref, in_sem.at[0])
    x_copy = pltpu.make_async_copy(x_hbm, x_ref, in_sem.at[1])
    z_copy = pltpu.make_async_copy(z_hbm, z_ref, in_sem.at[2])

    barrier = pltpu.get_barrier_semaphore()
    for off in (1, n_ctx - 1, 2, n_ctx - 2):
        pl.semaphore_signal(barrier, inc=1, device_id={"ctx": (ctx + off) % n_ctx}, device_id_type=MESH)
    pl.semaphore_signal(barrier, inc=1, device_id={"tp": other_core}, device_id_type=MESH)
    for off in range(1, n_y):
        pl.semaphore_signal(
            barrier, inc=1, device_id={"tp": ((y + off) % n_y) * 2 + core}, device_id_type=MESH
        )

    for copy in (m_copy, x_copy, z_copy, w_copy):
        copy.start()

    def remote(src, dst, send, recv, where):
        return pltpu.make_async_remote_copy(
            src_ref=src, dst_ref=dst, send_sem=send, recv_sem=recv, device_id=where, device_id_type=MESH
        )

    def lane_column(ref):
        sq_ref[...] = jnp.zeros_like(sq_ref)
        sq_ref[:, :heads] = jnp.broadcast_to(ref[...], (LANES, heads))
        return sq_ref[...].T

    def three_terms(v):
        first = v.astype(jnp.bfloat16).astype(jnp.float32)
        second = (v - first).astype(jnp.bfloat16).astype(jnp.float32)
        return [first, second, (v - first - second).astype(jnp.bfloat16).astype(jnp.float32)]

    def all_tokens(column):
        return jnp.concatenate([column[:heads]] * (length // LANES), axis=1)

    step = jnp.log(1.0 + jnp.exp(step_ref[...] + all_tokens(lane_column(bias_ref))))
    rate = step * jnp.exp(all_tokens(lane_column(decay_ref)))
    skip_t = lane_column(skip_ref)

    pl.semaphore_wait(barrier, 4 + 1 + (n_y - 1))

    following = {"ctx": (ctx + 1) % n_ctx}
    halo_x = remote(x_hbm.at[pl.ds(length - HALO, HALO)], hx_ref, halo_send.at[0], halo_recv.at[0], following)
    halo_m = remote(m_hbm.at[pl.ds(length - HALO, HALO)], hm_ref, halo_send.at[1], halo_recv.at[1], following)
    halo_m.start()
    halo_x.start()

    s_ids = lax.broadcasted_iota(jnp.int32, (length, length), 0)
    t_ids = lax.broadcasted_iota(jnp.int32, (length, length), 1)
    upper = jnp.where(s_ids <= t_ids, 1.0, 0.0).astype(jnp.bfloat16)
    sums = jnp.dot(
        jnp.concatenate(three_terms(rate), axis=0).astype(jnp.bfloat16), upper,
        preferred_element_type=jnp.float32,
    )
    sums = sums[:heads] + sums[heads : 2 * heads] + sums[2 * heads :]
    source = sums + jnp.log(step)
    filler = jnp.ones((LANES - 6 * heads, length), jnp.float32)
    parts_ref[...] = jnp.concatenate(three_terms(sums) + three_terms(source) + [filler], axis=0)
    left_ref[...] = parts_ref[...].T.astype(jnp.bfloat16)

    lane_row = lax.broadcasted_iota(jnp.int32, (1, LANES), 1) < LANES // 2
    x_taps = xf_ref[...].astype(jnp.float32)
    m_taps = mf_ref[...].astype(jnp.float32)
    for p in range(pairs):
        skips_ref[p] = jnp.broadcast_to(
            jnp.where(lane_row, skip_t[2 * p : 2 * p + 1], skip_t[2 * p + 1 : 2 * p + 2]), (8, LANES)
        )
        gains_ref[p] = jnp.broadcast_to(gain_ref[:, p * LANES : (p + 1) * LANES], (8, LANES))
        xfs_ref[p] = x_taps[:, p * LANES : (p + 1) * LANES]
    for p in range(2):
        mfs_ref[p] = m_taps[:, p * LANES : (p + 1) * LANES]

    channels = x_ref.shape[1]
    term = lax.broadcasted_iota(jnp.int32, (LANES, channels), 0)
    lane = lax.broadcasted_iota(jnp.int32, (LANES, channels), 1)
    width = channels // heads
    match = (lane >= (term & (heads - 1)) * width) & (lane < ((term & (heads - 1)) + 1) * width)
    pick_sum = jnp.where(match & (term < 3 * heads), 1.0, 0.0).astype(jnp.bfloat16)
    pick_source = jnp.where(match & (term >= 3 * heads) & (term < 6 * heads), 1.0, 0.0).astype(jnp.bfloat16)
    last = jnp.dot(left_ref[length - HALO :, :], pick_sum, preferred_element_type=jnp.float32)[HALO - 1 :]
    for p in range(pairs):
        cols = slice(p * LANES, (p + 1) * LANES)
        pick_ref[p, :, :LANES] = pick_sum[:, cols]
        pick_ref[p, :, LANES:] = pick_source[:, cols]
        dsend_ref[p] = jnp.broadcast_to(last[:, cols], (8, LANES))
    dec_copy = remote(dsend_ref, drecv_ref, dec_send, dec_recv, {"ctx": mate})
    dec_copy.start()

    taps = xf_ref.shape[0]
    has_prev = jnp.where(ctx > 0, 1.0, 0.0).astype(jnp.float32)

    def conv(block, halo, filters, slot):
        pad_ref[slot, 0:8] = halo.astype(jnp.float32)[HALO - 8 :] * has_prev
        pad_ref[slot, 8:] = block.astype(jnp.float32)
        total = filters[0:1] * pad_ref[slot, 9 - taps : 9 - taps + length]
        for k in range(1, taps):
            start = 9 - taps + k
            total = total + filters[k : k + 1] * pad_ref[slot, start : start + length]
        return half_silu(total)

    m_copy.wait()
    halo_m.wait_recv()
    bt_ref[...] = conv(m_ref[:, :LANES], hm_ref[:, :LANES], mfs_ref[0], 0).T.astype(jnp.bfloat16)
    c_ref[...] = conv(m_ref[:, LANES:], hm_ref[:, LANES:], mfs_ref[1], 1).astype(jnp.bfloat16)
    x_copy.wait()
    halo_x.wait_recv()

    def pair_copy(p):
        return remote(lsend_ref.at[p], lrecv_ref.at[p], pair_send.at[p], pair_recv.at[p], {"ctx": mate})

    half = length // 2

    def local_state(p, slot):
        cols = pl.ds(pl.multiple_of(p * LANES, LANES), LANES)
        xc = conv(x_ref[:, cols], hx_ref[:, cols], xfs_ref[p], slot).astype(jnp.bfloat16)
        xc_ref[p] = xc
        both = jnp.dot(left_ref[...], pick_ref[p], preferred_element_type=jnp.float32)
        sums, source = both[:, :LANES], both[:, LANES:]
        aexp_ref[p] = sums
        wide = xc.astype(jnp.float32)
        end = dsend_ref[p][0:1]
        border = sums[half - 1 : half]
        mids, states = [], []
        for j, stop in ((0, border), (1, end)):
            here = slice(j * half, (j + 1) * half)
            mid = sums[j * half + half // 2 - 1 : j * half + half // 2]
            mid_ref[p, j] = jnp.broadcast_to(mid, (8, LANES))
            u = (jnp.exp(source[here] - mid) * wide[here]).astype(jnp.bfloat16)
            uc_ref[p, here] = u
            fresh = jnp.dot(bt_ref[:, here], u, preferred_element_type=jnp.float32)
            mids.append(mid)
            states.append(fresh * jnp.exp(mid - stop))
        first_ref[p] = (states[0] * jnp.exp(border - mids[1])).astype(jnp.bfloat16)
        state = states[0] * jnp.exp(border - end) + states[1]
        lown_ref[p] = state
        lsend_ref[p] = state.astype(jnp.bfloat16)
        pair_copy(p).start()

    row_half = lax.broadcasted_iota(jnp.int32, (half, half), 0)
    col_half = lax.broadcasted_iota(jnp.int32, (half, half), 1)
    for j in range(2):
        here = slice(j * half, (j + 1) * half)
        scores = jnp.dot(c_ref[here, :], bt_ref[:, here], preferred_element_type=jnp.float32)
        cb_ref[j] = jnp.where(row_half >= col_half, scores, 0.0).astype(jnp.bfloat16)

    is_odd = odd.astype(jnp.float32)
    is_even = 1.0 - is_odd
    next_pair = {"ctx": (ctx + 2) % n_ctx}

    def chain_copy(p):
        return remote(csend_ref.at[p], crecv_ref.at[p], chain_send.at[p], chain_recv.at[p], next_pair)

    @pl.when(z == 0)
    def _():
        crecv_ref[...] = jnp.zeros_like(crecv_ref)

    dec_copy.wait_recv()

    def relay(p):
        pair_copy(p).wait_recv()
        mine = lown_ref[p]
        theirs = lrecv_ref[p].astype(jnp.float32)
        d_mine = jnp.exp(-dsend_ref[p][0:1])
        d_theirs = jnp.exp(-drecv_ref[p][0:1])
        l_even = mine * is_even + theirs * is_odd
        l_odd = mine * is_odd + theirs * is_even
        d_even = d_mine * is_even + d_theirs * is_odd
        d_odd = d_mine * is_odd + d_theirs * is_even

        @pl.when(z > 0)
        def _():
            chain_copy(p).wait_recv()

        entering = crecv_ref[p].astype(jnp.float32)
        middle = d_even * entering + l_even
        sr_ref[p] = (entering * is_even + middle * is_odd).astype(jnp.bfloat16)

        @pl.when(z < n_z - 1)
        def _():
            csend_ref[p] = (d_odd * middle + l_odd).astype(jnp.bfloat16)
            chain_copy(p).start()

    def within(p):
        cols = pl.ds(pl.multiple_of(p * LANES, LANES), LANES)
        skip = skips_ref[p][0:1]
        for j in range(2):
            here = slice(j * half, (j + 1) * half)
            own = jnp.dot(cb_ref[j], uc_ref[p, here], preferred_element_type=jnp.float32)
            if j == 1:
                own = own + jnp.dot(c_ref[here, :], first_ref[p], preferred_element_type=jnp.float32)
            mid = mid_ref[p, j][0:1]
            decay = jnp.exp(mid - aexp_ref[p, here])
            gate = half_silu(z_ref[here, cols].astype(jnp.float32))
            yg_ref[p, here] = (decay * own + skip * xc_ref[p, here].astype(jnp.float32)) * gate
            eg_ref[p, here] = decay * jnp.exp(-mid) * gate

    z_copy.wait()
    twos = pairs // 2
    lag = jnp.minimum(2 + 2 * z, 2 * twos)

    def turn(i, _):
        @pl.when((i >= lag) & (i < lag + twos))
        def _():
            for slot in range(2):
                relay(2 * (i - lag) + slot)

        @pl.when(i < twos)
        def _():
            for slot in range(2):
                local_state(2 * i + slot, slot)

        @pl.when((i >= twos) & (i < 2 * twos))
        def _():
            for slot in range(2):
                within(2 * (i - twos) + slot)

        return 0

    lax.fori_loop(0, 3 * twos, turn, 0)

    span = 2 * rows

    def project_rows(first):
        here = pl.ds(pl.multiple_of(first, span), span)
        c_rows = c_ref[here, :]

        squares = jnp.zeros((span, LANES), jnp.float32)
        for p in range(pairs):
            inter = jnp.dot(c_rows, sr_ref[p], preferred_element_type=jnp.float32)
            gated = yg_ref[p, here] + eg_ref[p, here] * inter
            gated_ref[p] = gated
            squares = squares + gated * gated
        scale = lax.rsqrt(jnp.sum(squares, axis=1, keepdims=True) / channels + 1e-05)
        for p in range(pairs):
            normed_ref[:, p * LANES : (p + 1) * LANES] = (
                gated_ref[p] * scale * gains_ref[p][0:1]
            ).astype(jnp.bfloat16)

    def core_copy(slot, k):
        return remote(
            part_ref.at[slot, k, 1 - core], core_ref.at[slot, k],
            core_send.at[slot, k], core_recv.at[slot, k], {"tp": other_core},
        )

    def y_copy(slot, k):
        target = ((y + slot) % n_y) * 2 + core
        return remote(
            ysend_ref.at[slot - 1, k], yrecv_ref.at[slot - 1, k],
            y_send.at[slot - 1, k], y_recv.at[slot - 1, k], {"tp": target},
        )

    def project(slot, k):
        cols = pl.ds(pl.multiple_of(k * chunk, chunk), chunk)
        part = jnp.dot(normed_ref[...], w_ref[:, cols], preferred_element_type=jnp.float32)
        part = part.astype(jnp.bfloat16)
        part_ref[slot, k, 0] = part[:rows]
        part_ref[slot, k, 1] = part[rows:]
        core_copy(slot, k).start()

    def chip_sum(slot, k):
        core_copy(slot, k).wait_recv()
        return part_ref[slot, k, core].astype(jnp.float32) + core_ref[slot, k].astype(jnp.float32)

    for slot in list(range(1, n_y)) + [0]:
        project_rows(((y + slot) % n_y) * span)
        if slot == (1 if n_y > 1 else 0):
            w_copy.wait()

        def forward(k, slot=slot):
            ysend_ref[slot - 1, k] = chip_sum(slot, k).astype(jnp.bfloat16)
            y_copy(slot, k).start()

        def column(k, _, slot=slot):
            project(slot, k)
            if slot > 0:

                @pl.when(k > 0)
                def _():
                    forward(k - 1)

            return 0

        lax.fori_loop(0, n_chunks, column, 0)
        if slot > 0:
            forward(n_chunks - 1)

    def out_copy(k):
        cols = pl.ds(pl.multiple_of(k * chunk, chunk), chunk)
        return pltpu.make_async_copy(out_buf.at[k], out_ref.at[:, cols], out_sem.at[k])

    def finish(k, _):
        total = chip_sum(0, k)
        for slot in range(1, n_y):
            y_copy(slot, k).wait_recv()
            total = total + yrecv_ref[slot - 1, k].astype(jnp.float32)
        out_buf[k] = total.astype(jnp.bfloat16)
        out_copy(k).start()
        return 0

    lax.fori_loop(0, n_chunks, finish, 0)

    halo_m.wait_send()
    halo_x.wait_send()
    dec_copy.wait_send()

    def drain_states(p, _):
        pair_copy(p).wait_send()

        @pl.when(z < n_z - 1)
        def _():
            chain_copy(p).wait_send()

        return 0

    lax.fori_loop(0, pairs, drain_states, 0)

    def drain_parts(k, _):
        out_copy(k).wait()
        for slot in range(n_y):
            core_copy(slot, k).wait_send()
        for slot in range(1, n_y):
            y_copy(slot, k).wait_send()
        return 0

    lax.fori_loop(0, n_chunks, drain_parts, 0)


def on_device(n_ctx, n_tp, *args):
    (x_inputs, state_maps, z_gate, step_raw, step_bias, decay_log, skip_gain,
     x_filter, state_filter, norm_gain, out_weight) = args
    length, channels = x_inputs.shape
    heads = step_raw.shape[1]
    pairs = channels // LANES
    model = out_weight.shape[1]
    rows = length // n_tp
    n_y = n_tp // 2
    chunk = 512
    n_chunks = model // chunk
    state = state_maps.shape[1] // 2
    bf16, f32 = jnp.bfloat16, jnp.float32
    vmem = pl.BlockSpec(memory_space=pltpu.VMEM)
    anywhere = pl.BlockSpec(memory_space=pl.ANY)
    dma = pltpu.SemaphoreType.DMA
    scratch = [
        pltpu.VMEM(out_weight.shape, bf16),
        pltpu.VMEM(x_inputs.shape, bf16),
        pltpu.VMEM(state_maps.shape, bf16),
        pltpu.VMEM(z_gate.shape, bf16),
        pltpu.VMEM((HALO, channels), bf16),
        pltpu.VMEM((HALO, 2 * state), bf16),
        pltpu.VMEM((2, length + 8, LANES), f32),
        pltpu.VMEM((pairs, x_filter.shape[0], LANES), f32),
        pltpu.VMEM((2, x_filter.shape[0], LANES), f32),
        pltpu.VMEM((pairs, 8, LANES), f32),
        pltpu.VMEM((pairs, 8, LANES), f32),
        pltpu.VMEM((LANES, LANES), f32),
        pltpu.VMEM((LANES, length), f32),
        pltpu.VMEM((length, LANES), bf16),
        pltpu.VMEM((pairs, LANES, 2 * LANES), bf16),
        pltpu.VMEM((pairs, 8, LANES), f32),
        pltpu.VMEM((pairs, 8, LANES), f32),
        pltpu.VMEM((pairs, length, LANES), bf16),
        pltpu.VMEM((pairs, length, LANES), bf16),
        pltpu.VMEM((pairs, length, LANES), f32),
        pltpu.VMEM((pairs, 2, 8, LANES), f32),
        pltpu.VMEM((pairs, state, LANES), bf16),
        pltpu.VMEM((state, length), bf16),
        pltpu.VMEM((length, state), bf16),
        pltpu.VMEM((2, length // 2, length // 2), bf16),
        pltpu.VMEM((pairs, state, LANES), f32),
        pltpu.VMEM((pairs, state, LANES), bf16),
        pltpu.VMEM((pairs, state, LANES), bf16),
        pltpu.VMEM((pairs, state, LANES), bf16),
        pltpu.VMEM((pairs, state, LANES), bf16),
        pltpu.VMEM((pairs, state, LANES), bf16),
        pltpu.VMEM((pairs, length, LANES), f32),
        pltpu.VMEM((pairs, length, LANES), f32),
        pltpu.VMEM((pairs, 2 * rows, LANES), f32),
        pltpu.VMEM((2 * rows, channels), bf16),
        pltpu.VMEM((n_y, n_chunks, 2, rows, chunk), bf16),
        pltpu.VMEM((n_y, n_chunks, rows, chunk), bf16),
        pltpu.VMEM((n_y - 1, n_chunks, rows, chunk), bf16),
        pltpu.VMEM((n_y - 1, n_chunks, rows, chunk), bf16),
        pltpu.VMEM((n_chunks, rows, chunk), bf16),
        dma, dma((3,)), dma((n_chunks,)), dma((2,)), dma((2,)), dma, dma,
        dma((pairs,)), dma((pairs,)), dma((pairs,)), dma((pairs,)),
        dma((n_y, n_chunks)), dma((n_y, n_chunks)),
        dma((n_y - 1, n_chunks)), dma((n_y - 1, n_chunks)),
    ]
    mixed = pl.pallas_call(
        functools.partial(layer_kernel, n_ctx, n_tp, chunk),
        out_shape=jax.ShapeDtypeStruct((rows, model), bf16),
        in_specs=[anywhere] * 3 + [vmem] * 7 + [anywhere],
        out_specs=anywhere,
        scratch_shapes=scratch,
        compiler_params=pltpu.CompilerParams(
            collective_id=0, has_side_effects=True, vmem_limit_bytes=58 * 1024 * 1024
        ),
        cost_estimate=pl.CostEstimate(
            flops=2 * length * channels * (model + 2 * length), bytes_accessed=4 * out_weight.size,
            transcendentals=length * length * heads,
        ),
        name="layer",
    )(
        x_inputs, state_maps, z_gate, step_raw.T, step_bias[None], decay_log[None], skip_gain[None],
        x_filter, state_filter, norm_gain[None], out_weight,
    )
    return pl.pallas_call(
        hand_over,
        out_shape=jax.ShapeDtypeStruct((rows, model), bf16),
        in_specs=[anywhere],
        out_specs=anywhere,
        scratch_shapes=[dma((4,))],
        name="hand_over",
    )(mixed)


def hand_over(from_ref, to_ref, sems):
    part = from_ref.shape[0] // 4
    copies = [
        pltpu.make_async_copy(from_ref.at[pl.ds(i * part, part)], to_ref.at[pl.ds(i * part, part)], sems.at[i])
        for i in range(4)
    ]
    for copy in copies:
        copy.start()
    for copy in copies:
        copy.wait()


def solution(mesh):
    return jax.shard_map(
        functools.partial(on_device, mesh.shape["ctx"], mesh.shape["tp"]),
        mesh=mesh,
        in_specs=(
            P("ctx", "tp"),
            P("ctx", "tp"),
            P("ctx", "tp"),
            P("ctx", "tp"),
            P("tp"),
            P("tp"),
            P("tp"),
            P(None, "tp"),
            P(None, "tp"),
            P("tp"),
            P("tp", None),
        ),
        out_specs=P(("ctx", "tp"), None),
        check_vma=False,
    )
```

```python
import functools

import jax
import jax.numpy as jnp
from jax import lax
from jax.experimental import pallas as pl
from jax.experimental.pallas import tpu as pltpu
from jax.sharding import PartitionSpec as P

MESH = pl.DeviceIdType.MESH
LANES = 128
HALO = 16


def half_silu(v):
    h = 0.5 * v
    return h + h * jnp.tanh(h)


def layer_kernel(
    n_ctx, n_tp, chunk,
    x_hbm, m_hbm, z_hbm, step_ref, bias_ref, decay_ref, skip_ref, xf_ref, mf_ref, gain_ref, w_hbm,
    out_ref,
    w_ref, x_ref, m_ref, z_ref, hx_ref, hm_ref, pad_ref, xfs_ref, mfs_ref, gains_ref, skips_ref,
    sq_ref, parts_ref, left_ref, pick_ref, dsend_ref, drecv_ref,
    xc_ref, uc_ref, aexp_ref, mid_ref, first_ref, bt_ref, c_ref, cb_ref, lown_ref, lsend_ref, lrecv_ref, csend_ref, crecv_ref, sr_ref,
    yg_ref, eg_ref, gated_ref, normed_ref, part_ref, core_ref, ysend_ref, yrecv_ref, out_buf,
    w_sem, in_sem, out_sem, halo_send, halo_recv, dec_send, dec_recv, pair_send, pair_recv, chain_send, chain_recv,
    core_send, core_recv, y_send, y_recv,
):
    length = x_ref.shape[0]
    pairs = x_ref.shape[1] // LANES
    heads = step_ref.shape[0]
    n_y = n_tp // 2
    rows = length // n_tp
    n_chunks = w_hbm.shape[1] // chunk
    n_z = n_ctx // 2
    ctx = lax.axis_index("ctx")
    tp = lax.axis_index("tp")
    y, core = tp // 2, tp % 2
    z, odd = ctx // 2, ctx % 2
    mate = ctx + 1 - 2 * odd
    other_core = y * 2 + 1 - core

    w_copy = pltpu.make_async_copy(w_hbm, w_ref, w_sem)
    m_copy = pltpu.make_async_copy(m_hbm, m_ref, in_sem.at[0])
    x_copy = pltpu.make_async_copy(x_hbm, x_ref, in_sem.at[1])
    z_copy = pltpu.make_async_copy(z_hbm, z_ref, in_sem.at[2])

    barrier = pltpu.get_barrier_semaphore()
    for off in (1, n_ctx - 1, 2, n_ctx - 2):
        pl.semaphore_signal(barrier, inc=1, device_id={"ctx": (ctx + off) % n_ctx}, device_id_type=MESH)
    pl.semaphore_signal(barrier, inc=1, device_id={"tp": other_core}, device_id_type=MESH)
    for off in range(1, n_y):
        pl.semaphore_signal(
            barrier, inc=1, device_id={"tp": ((y + off) % n_y) * 2 + core}, device_id_type=MESH
        )

    for copy in (m_copy, x_copy, z_copy, w_copy):
        copy.start()

    def remote(src, dst, send, recv, where):
        return pltpu.make_async_remote_copy(
            src_ref=src, dst_ref=dst, send_sem=send, recv_sem=recv, device_id=where, device_id_type=MESH
        )

    def lane_column(ref):
        sq_ref[...] = jnp.zeros_like(sq_ref)
        sq_ref[:, :heads] = jnp.broadcast_to(ref[...], (LANES, heads))
        return sq_ref[...].T

    def three_terms(v):
        first = v.astype(jnp.bfloat16).astype(jnp.float32)
        second = (v - first).astype(jnp.bfloat16).astype(jnp.float32)
        return [first, second, (v - first - second).astype(jnp.bfloat16).astype(jnp.float32)]

    def all_tokens(column):
        return jnp.concatenate([column[:heads]] * (length // LANES), axis=1)

    step = jnp.log(1.0 + jnp.exp(step_ref[...] + all_tokens(lane_column(bias_ref))))
    rate = step * jnp.exp(all_tokens(lane_column(decay_ref)))
    skip_t = lane_column(skip_ref)

    pl.semaphore_wait(barrier, 4 + 1 + (n_y - 1))

    following = {"ctx": (ctx + 1) % n_ctx}
    halo_x = remote(x_hbm.at[pl.ds(length - HALO, HALO)], hx_ref, halo_send.at[0], halo_recv.at[0], following)
    halo_m = remote(m_hbm.at[pl.ds(length - HALO, HALO)], hm_ref, halo_send.at[1], halo_recv.at[1], following)
    halo_m.start()
    halo_x.start()

    s_ids = lax.broadcasted_iota(jnp.int32, (length, length), 0)
    t_ids = lax.broadcasted_iota(jnp.int32, (length, length), 1)
    upper = jnp.where(s_ids <= t_ids, 1.0, 0.0).astype(jnp.bfloat16)
    sums = jnp.dot(
        jnp.concatenate(three_terms(rate), axis=0).astype(jnp.bfloat16), upper,
        preferred_element_type=jnp.float32,
    )
    sums = sums[:heads] + sums[heads : 2 * heads] + sums[2 * heads :]
    source = sums + jnp.log(step)
    filler = jnp.ones((LANES - 6 * heads, length), jnp.float32)
    parts_ref[...] = jnp.concatenate(three_terms(sums) + three_terms(source) + [filler], axis=0)
    left_ref[...] = parts_ref[...].T.astype(jnp.bfloat16)

    lane_row = lax.broadcasted_iota(jnp.int32, (1, LANES), 1) < LANES // 2
    x_taps = xf_ref[...].astype(jnp.float32)
    m_taps = mf_ref[...].astype(jnp.float32)
    for p in range(pairs):
        skips_ref[p] = jnp.broadcast_to(
            jnp.where(lane_row, skip_t[2 * p : 2 * p + 1], skip_t[2 * p + 1 : 2 * p + 2]), (8, LANES)
        )
        gains_ref[p] = jnp.broadcast_to(gain_ref[:, p * LANES : (p + 1) * LANES], (8, LANES))
        xfs_ref[p] = x_taps[:, p * LANES : (p + 1) * LANES]
    for p in range(2):
        mfs_ref[p] = m_taps[:, p * LANES : (p + 1) * LANES]

    channels = x_ref.shape[1]
    term = lax.broadcasted_iota(jnp.int32, (LANES, channels), 0)
    lane = lax.broadcasted_iota(jnp.int32, (LANES, channels), 1)
    width = channels // heads
    match = (lane >= (term & (heads - 1)) * width) & (lane < ((term & (heads - 1)) + 1) * width)
    pick_sum = jnp.where(match & (term < 3 * heads), 1.0, 0.0).astype(jnp.bfloat16)
    pick_source = jnp.where(match & (term >= 3 * heads) & (term < 6 * heads), 1.0, 0.0).astype(jnp.bfloat16)
    last = jnp.dot(left_ref[length - HALO :, :], pick_sum, preferred_element_type=jnp.float32)[HALO - 1 :]
    for p in range(pairs):
        cols = slice(p * LANES, (p + 1) * LANES)
        pick_ref[p, :, :LANES] = pick_sum[:, cols]
        pick_ref[p, :, LANES:] = pick_source[:, cols]
        dsend_ref[p] = jnp.broadcast_to(last[:, cols], (8, LANES))
    dec_copy = remote(dsend_ref, drecv_ref, dec_send, dec_recv, {"ctx": mate})
    dec_copy.start()

    taps = xf_ref.shape[0]
    has_prev = jnp.where(ctx > 0, 1.0, 0.0).astype(jnp.float32)

    def conv(block, halo, filters, slot):
        pad_ref[slot, 0:8] = halo.astype(jnp.float32)[HALO - 8 :] * has_prev
        pad_ref[slot, 8:] = block.astype(jnp.float32)
        total = filters[0:1] * pad_ref[slot, 9 - taps : 9 - taps + length]
        for k in range(1, taps):
            start = 9 - taps + k
            total = total + filters[k : k + 1] * pad_ref[slot, start : start + length]
        return half_silu(total)

    m_copy.wait()
    halo_m.wait_recv()
    bt_ref[...] = conv(m_ref[:, :LANES], hm_ref[:, :LANES], mfs_ref[0], 0).T.astype(jnp.bfloat16)
    c_ref[...] = conv(m_ref[:, LANES:], hm_ref[:, LANES:], mfs_ref[1], 1).astype(jnp.bfloat16)
    x_copy.wait()
    halo_x.wait_recv()

    def pair_copy(p):
        return remote(lsend_ref.at[p], lrecv_ref.at[p], pair_send.at[p], pair_recv.at[p], {"ctx": mate})

    half = length // 2

    def local_state(p, slot):
        cols = pl.ds(pl.multiple_of(p * LANES, LANES), LANES)
        xc = conv(x_ref[:, cols], hx_ref[:, cols], xfs_ref[p], slot).astype(jnp.bfloat16)
        xc_ref[p] = xc
        both = jnp.dot(left_ref[...], pick_ref[p], preferred_element_type=jnp.float32)
        sums, source = both[:, :LANES], both[:, LANES:]
        aexp_ref[p] = sums
        wide = xc.astype(jnp.float32)
        end = dsend_ref[p][0:1]
        border = sums[half - 1 : half]
        mids, states = [], []
        for j, stop in ((0, border), (1, end)):
            here = slice(j * half, (j + 1) * half)
            mid = sums[j * half + half // 2 - 1 : j * half + half // 2]
            mid_ref[p, j] = jnp.broadcast_to(mid, (8, LANES))
            u = (jnp.exp(source[here] - mid) * wide[here]).astype(jnp.bfloat16)
            uc_ref[p, here] = u
            fresh = jnp.dot(bt_ref[:, here], u, preferred_element_type=jnp.float32)
            mids.append(mid)
            states.append(fresh * jnp.exp(mid - stop))
        first_ref[p] = (states[0] * jnp.exp(border - mids[1])).astype(jnp.bfloat16)
        state = states[0] * jnp.exp(border - end) + states[1]
        lown_ref[p] = state
        lsend_ref[p] = state.astype(jnp.bfloat16)
        pair_copy(p).start()

    row_half = lax.broadcasted_iota(jnp.int32, (half, half), 0)
    col_half = lax.broadcasted_iota(jnp.int32, (half, half), 1)
    for j in range(2):
        here = slice(j * half, (j + 1) * half)
        scores = jnp.dot(c_ref[here, :], bt_ref[:, here], preferred_element_type=jnp.float32)
        cb_ref[j] = jnp.where(row_half >= col_half, scores, 0.0).astype(jnp.bfloat16)

    is_odd = odd.astype(jnp.float32)
    is_even = 1.0 - is_odd
    next_pair = {"ctx": (ctx + 2) % n_ctx}

    def chain_copy(p):
        return remote(csend_ref.at[p], crecv_ref.at[p], chain_send.at[p], chain_recv.at[p], next_pair)

    @pl.when(z == 0)
    def _():
        crecv_ref[...] = jnp.zeros_like(crecv_ref)

    dec_copy.wait_recv()

    def relay(p):
        pair_copy(p).wait_recv()
        mine = lown_ref[p]
        theirs = lrecv_ref[p].astype(jnp.float32)
        d_mine = jnp.exp(-dsend_ref[p][0:1])
        d_theirs = jnp.exp(-drecv_ref[p][0:1])
        l_even = mine * is_even + theirs * is_odd
        l_odd = mine * is_odd + theirs * is_even
        d_even = d_mine * is_even + d_theirs * is_odd
        d_odd = d_mine * is_odd + d_theirs * is_even

        @pl.when(z > 0)
        def _():
            chain_copy(p).wait_recv()

        entering = crecv_ref[p].astype(jnp.float32)
        middle = d_even * entering + l_even
        sr_ref[p] = (entering * is_even + middle * is_odd).astype(jnp.bfloat16)

        @pl.when(z < n_z - 1)
        def _():
            csend_ref[p] = (d_odd * middle + l_odd).astype(jnp.bfloat16)
            chain_copy(p).start()

    def within(p):
        cols = pl.ds(pl.multiple_of(p * LANES, LANES), LANES)
        skip = skips_ref[p][0:1]
        for j in range(2):
            here = slice(j * half, (j + 1) * half)
            own = jnp.dot(cb_ref[j], uc_ref[p, here], preferred_element_type=jnp.float32)
            if j == 1:
                own = own + jnp.dot(c_ref[here, :], first_ref[p], preferred_element_type=jnp.float32)
            mid = mid_ref[p, j][0:1]
            decay = jnp.exp(mid - aexp_ref[p, here])
            gate = half_silu(z_ref[here, cols].astype(jnp.float32))
            yg_ref[p, here] = (decay * own + skip * xc_ref[p, here].astype(jnp.float32)) * gate
            eg_ref[p, here] = decay * jnp.exp(-mid) * gate

    z_copy.wait()
    twos = pairs // 2
    lag = jnp.minimum(2 + 2 * z, 2 * twos)

    def turn(i, _):
        @pl.when((i >= lag) & (i < lag + twos))
        def _():
            for slot in range(2):
                relay(2 * (i - lag) + slot)

        @pl.when(i < twos)
        def _():
            for slot in range(2):
                local_state(2 * i + slot, slot)

        @pl.when((i >= twos) & (i < 2 * twos))
        def _():
            for slot in range(2):
                within(2 * (i - twos) + slot)

        return 0

    lax.fori_loop(0, 3 * twos, turn, 0)

    squares = jnp.zeros((length, LANES), jnp.float32)
    for p in range(pairs):
        inter = jnp.dot(c_ref[...], sr_ref[p], preferred_element_type=jnp.float32)
        gated = yg_ref[p] + eg_ref[p] * inter
        gated_ref[p] = gated
        squares = squares + gated * gated
    scale = lax.rsqrt(jnp.sum(squares, axis=1, keepdims=True) / channels + 1e-05)
    for p in range(pairs):
        normed_ref[:, p * LANES : (p + 1) * LANES] = (
            gated_ref[p] * scale * gains_ref[p][0:1]
        ).astype(jnp.bfloat16)

    def core_copy(slot, k):
        rows_of = (y + slot) % n_y
        return remote(
            part_ref.at[rows_of, k, 1 - core], core_ref.at[rows_of, k],
            core_send.at[slot, k], core_recv.at[slot, k], {"tp": other_core},
        )

    def y_copy(slot, k):
        target = ((y + slot) % n_y) * 2 + core
        return remote(
            ysend_ref.at[slot - 1, k], yrecv_ref.at[slot - 1, k],
            y_send.at[slot - 1, k], y_recv.at[slot - 1, k], {"tp": target},
        )

    def chip_sum(slot, k):
        core_copy(slot, k).wait_recv()
        rows_of = (y + slot) % n_y
        return part_ref[rows_of, k, core].astype(jnp.float32) + core_ref[rows_of, k].astype(jnp.float32)

    def forward(k):
        for slot in range(1, n_y):
            ysend_ref[slot - 1, k] = chip_sum(slot, k).astype(jnp.bfloat16)
            y_copy(slot, k).start()

    def column(k, _):
        cols = pl.ds(pl.multiple_of(k * chunk, chunk), chunk)
        part = jnp.dot(normed_ref[...], w_ref[:, cols], preferred_element_type=jnp.float32)
        part = part.astype(jnp.bfloat16)
        for row_y in range(n_y):
            for row_core in range(2):
                first = (2 * row_y + row_core) * rows
                part_ref[row_y, k, row_core] = part[first : first + rows]
        for slot in list(range(1, n_y)) + [0]:
            core_copy(slot, k).start()

        @pl.when(k > 0)
        def _():
            forward(k - 1)

        return 0

    w_copy.wait()
    lax.fori_loop(0, n_chunks, column, 0)
    forward(n_chunks - 1)

    def out_copy(k):
        cols = pl.ds(pl.multiple_of(k * chunk, chunk), chunk)
        return pltpu.make_async_copy(out_buf.at[k], out_ref.at[:, cols], out_sem.at[k])

    def finish(k, _):
        total = chip_sum(0, k)
        for slot in range(1, n_y):
            y_copy(slot, k).wait_recv()
            total = total + yrecv_ref[slot - 1, k].astype(jnp.float32)
        out_buf[k] = total.astype(jnp.bfloat16)
        out_copy(k).start()
        return 0

    lax.fori_loop(0, n_chunks, finish, 0)

    halo_m.wait_send()
    halo_x.wait_send()
    dec_copy.wait_send()

    def drain_states(p, _):
        pair_copy(p).wait_send()

        @pl.when(z < n_z - 1)
        def _():
            chain_copy(p).wait_send()

        return 0

    lax.fori_loop(0, pairs, drain_states, 0)

    def drain_parts(k, _):
        out_copy(k).wait()
        for slot in range(n_y):
            core_copy(slot, k).wait_send()
        for slot in range(1, n_y):
            y_copy(slot, k).wait_send()
        return 0

    lax.fori_loop(0, n_chunks, drain_parts, 0)


def on_device(n_ctx, n_tp, *args):
    (x_inputs, state_maps, z_gate, step_raw, step_bias, decay_log, skip_gain,
     x_filter, state_filter, norm_gain, out_weight) = args
    length, channels = x_inputs.shape
    heads = step_raw.shape[1]
    pairs = channels // LANES
    model = out_weight.shape[1]
    rows = length // n_tp
    n_y = n_tp // 2
    chunk = 256
    n_chunks = model // chunk
    state = state_maps.shape[1] // 2
    bf16, f32 = jnp.bfloat16, jnp.float32
    vmem = pl.BlockSpec(memory_space=pltpu.VMEM)
    anywhere = pl.BlockSpec(memory_space=pl.ANY)
    dma = pltpu.SemaphoreType.DMA
    scratch = [
        pltpu.VMEM(out_weight.shape, bf16),
        pltpu.VMEM(x_inputs.shape, bf16),
        pltpu.VMEM(state_maps.shape, bf16),
        pltpu.VMEM(z_gate.shape, bf16),
        pltpu.VMEM((HALO, channels), bf16),
        pltpu.VMEM((HALO, 2 * state), bf16),
        pltpu.VMEM((2, length + 8, LANES), f32),
        pltpu.VMEM((pairs, x_filter.shape[0], LANES), f32),
        pltpu.VMEM((2, x_filter.shape[0], LANES), f32),
        pltpu.VMEM((pairs, 8, LANES), f32),
        pltpu.VMEM((pairs, 8, LANES), f32),
        pltpu.VMEM((LANES, LANES), f32),
        pltpu.VMEM((LANES, length), f32),
        pltpu.VMEM((length, LANES), bf16),
        pltpu.VMEM((pairs, LANES, 2 * LANES), bf16),
        pltpu.VMEM((pairs, 8, LANES), f32),
        pltpu.VMEM((pairs, 8, LANES), f32),
        pltpu.VMEM((pairs, length, LANES), bf16),
        pltpu.VMEM((pairs, length, LANES), bf16),
        pltpu.VMEM((pairs, length, LANES), f32),
        pltpu.VMEM((pairs, 2, 8, LANES), f32),
        pltpu.VMEM((pairs, state, LANES), bf16),
        pltpu.VMEM((state, length), bf16),
        pltpu.VMEM((length, state), bf16),
        pltpu.VMEM((2, length // 2, length // 2), bf16),
        pltpu.VMEM((pairs, state, LANES), f32),
        pltpu.VMEM((pairs, state, LANES), bf16),
        pltpu.VMEM((pairs, state, LANES), bf16),
        pltpu.VMEM((pairs, state, LANES), bf16),
        pltpu.VMEM((pairs, state, LANES), bf16),
        pltpu.VMEM((pairs, state, LANES), bf16),
        pltpu.VMEM((pairs, length, LANES), f32),
        pltpu.VMEM((pairs, length, LANES), f32),
        pltpu.VMEM((pairs, length, LANES), f32),
        pltpu.VMEM((length, channels), bf16),
        pltpu.VMEM((n_y, n_chunks, 2, rows, chunk), bf16),
        pltpu.VMEM((n_y, n_chunks, rows, chunk), bf16),
        pltpu.VMEM((n_y - 1, n_chunks, rows, chunk), bf16),
        pltpu.VMEM((n_y - 1, n_chunks, rows, chunk), bf16),
        pltpu.VMEM((n_chunks, rows, chunk), bf16),
        dma, dma((3,)), dma((n_chunks,)), dma((2,)), dma((2,)), dma, dma,
        dma((pairs,)), dma((pairs,)), dma((pairs,)), dma((pairs,)),
        dma((n_y, n_chunks)), dma((n_y, n_chunks)),
        dma((n_y - 1, n_chunks)), dma((n_y - 1, n_chunks)),
    ]
    return pl.pallas_call(
        functools.partial(layer_kernel, n_ctx, n_tp, chunk),
        out_shape=jax.ShapeDtypeStruct((rows, model), bf16),
        in_specs=[anywhere] * 3 + [vmem] * 7 + [anywhere],
        out_specs=anywhere,
        scratch_shapes=scratch,
        compiler_params=pltpu.CompilerParams(
            collective_id=0, has_side_effects=True, vmem_limit_bytes=58 * 1024 * 1024
        ),
        cost_estimate=pl.CostEstimate(
            flops=2 * length * channels * (model + 2 * length), bytes_accessed=4 * out_weight.size,
            transcendentals=length * length * heads,
        ),
        name="layer",
    )(
        x_inputs, state_maps, z_gate, step_raw.T, step_bias[None], decay_log[None], skip_gain[None],
        x_filter, state_filter, norm_gain[None], out_weight,
    )


def solution(mesh):
    return jax.shard_map(
        functools.partial(on_device, mesh.shape["ctx"], mesh.shape["tp"]),
        mesh=mesh,
        in_specs=(
            P("ctx", "tp"),
            P("ctx", "tp"),
            P("ctx", "tp"),
            P("ctx", "tp"),
            P("tp"),
            P("tp"),
            P("tp"),
            P(None, "tp"),
            P(None, "tp"),
            P("tp"),
            P("tp", None),
        ),
        out_specs=P(("ctx", "tp"), None),
        check_vma=False,
    )
```

```python
import functools

import jax
import jax.numpy as jnp
from jax import lax
from jax.experimental import pallas as pl
from jax.experimental.pallas import tpu as pltpu
from jax.sharding import PartitionSpec as P

MESH = pl.DeviceIdType.MESH
LANES = 128
HALO = 16


def half_silu(v):
    h = 0.5 * v
    return h + h * jnp.tanh(h)


def layer_kernel(
    n_ctx, n_tp, chunk,
    x_hbm, m_hbm, z_hbm, step_ref, bias_ref, decay_ref, skip_ref, xf_ref, mf_ref, gain_ref, w_hbm,
    out_ref,
    w_ref, x_ref, m_ref, z_ref, hx_ref, hm_ref, pad_ref, xfs_ref, mfs_ref, gains_ref, skips_ref,
    sq_ref, parts_ref, left_ref, pick_ref, dsend_ref, drecv_ref,
    xc_ref, uc_ref, mid_ref, first_ref, bt_ref, c_ref, cb_ref, lown_ref, lsend_ref, lrecv_ref, csend_ref, crecv_ref, sr_ref,
    yg_ref, eg_ref, gated_ref, normed_ref, part_ref, core_ref, ysend_ref, yrecv_ref, out_buf,
    w_sem, in_sem, out_sem, halo_send, halo_recv, dec_send, dec_recv, pair_send, pair_recv, chain_send, chain_recv,
    core_send, core_recv, y_send, y_recv,
):
    length = x_ref.shape[0]
    pairs = x_ref.shape[1] // LANES
    heads = step_ref.shape[0]
    n_y = n_tp // 2
    rows = length // n_tp
    n_chunks = w_hbm.shape[1] // chunk
    n_z = n_ctx // 2
    ctx = lax.axis_index("ctx")
    tp = lax.axis_index("tp")
    y, core = tp // 2, tp % 2
    z, odd = ctx // 2, ctx % 2
    mate = ctx + 1 - 2 * odd
    other_core = y * 2 + 1 - core

    w_copy = pltpu.make_async_copy(w_hbm, w_ref, w_sem)
    m_copy = pltpu.make_async_copy(m_hbm, m_ref, in_sem.at[0])
    x_copy = pltpu.make_async_copy(x_hbm, x_ref, in_sem.at[1])
    z_copy = pltpu.make_async_copy(z_hbm, z_ref, in_sem.at[2])

    barrier = pltpu.get_barrier_semaphore()
    has_prev, has_next = ctx >= 1, ctx <= n_ctx - 2
    for there, off in ((has_prev, -1), (has_next, 1), (ctx >= 2, -2), (ctx <= n_ctx - 3, 2)):

        @pl.when(there)
        def _(off=off):
            pl.semaphore_signal(barrier, inc=1, device_id={"ctx": ctx + off}, device_id_type=MESH)

    pl.semaphore_signal(barrier, inc=1, device_id={"tp": other_core}, device_id_type=MESH)
    for off in range(1, n_y):
        pl.semaphore_signal(
            barrier, inc=1, device_id={"tp": ((y + off) % n_y) * 2 + core}, device_id_type=MESH
        )

    for copy in (m_copy, x_copy, z_copy, w_copy):
        copy.start()

    def remote(src, dst, send, recv, where):
        return pltpu.make_async_remote_copy(
            src_ref=src, dst_ref=dst, send_sem=send, recv_sem=recv, device_id=where, device_id_type=MESH
        )

    def lane_column(ref):
        sq_ref[...] = jnp.zeros_like(sq_ref)
        sq_ref[:, :heads] = jnp.broadcast_to(ref[...], (LANES, heads))
        return sq_ref[...].T

    def three_terms(v):
        first = v.astype(jnp.bfloat16).astype(jnp.float32)
        second = (v - first).astype(jnp.bfloat16).astype(jnp.float32)
        return [first, second, (v - first - second).astype(jnp.bfloat16).astype(jnp.float32)]

    def all_tokens(column):
        return jnp.concatenate([column[:heads]] * (length // LANES), axis=1)

    step = jnp.log(1.0 + jnp.exp(step_ref[...] + all_tokens(lane_column(bias_ref))))
    rate = step * jnp.exp(all_tokens(lane_column(decay_ref)))
    skip_t = lane_column(skip_ref)

    greeted = jnp.minimum(ctx, 2) + jnp.minimum(n_ctx - 1 - ctx, 2)
    pl.semaphore_wait(barrier, greeted + 1 + (n_y - 1))

    following = {"ctx": (ctx + 1) % n_ctx}
    halo_x = remote(x_hbm.at[pl.ds(length - HALO, HALO)], hx_ref, halo_send.at[0], halo_recv.at[0], following)
    halo_m = remote(m_hbm.at[pl.ds(length - HALO, HALO)], hm_ref, halo_send.at[1], halo_recv.at[1], following)

    @pl.when(has_next)
    def _():
        halo_m.start()
        halo_x.start()

    @pl.when(ctx == 0)
    def _():
        hm_ref[...] = jnp.zeros_like(hm_ref)
        hx_ref[...] = jnp.zeros_like(hx_ref)


    s_ids = lax.broadcasted_iota(jnp.int32, (length, length), 0)
    t_ids = lax.broadcasted_iota(jnp.int32, (length, length), 1)
    upper = jnp.where(s_ids <= t_ids, 1.0, 0.0).astype(jnp.bfloat16)
    sums = jnp.dot(
        jnp.concatenate(three_terms(rate), axis=0).astype(jnp.bfloat16), upper,
        preferred_element_type=jnp.float32,
    )
    sums = sums[:heads] + sums[heads : 2 * heads] + sums[2 * heads :]
    source = sums + jnp.log(step)
    filler = jnp.ones((LANES - 6 * heads, length), jnp.float32)
    parts_ref[...] = jnp.concatenate(three_terms(sums) + three_terms(source) + [filler], axis=0)
    left_ref[...] = parts_ref[...].T.astype(jnp.bfloat16)

    lane_row = lax.broadcasted_iota(jnp.int32, (1, LANES), 1) < LANES // 2
    x_taps = xf_ref[...].astype(jnp.float32)
    m_taps = mf_ref[...].astype(jnp.float32)
    for p in range(pairs):
        skips_ref[p] = jnp.broadcast_to(
            jnp.where(lane_row, skip_t[2 * p : 2 * p + 1], skip_t[2 * p + 1 : 2 * p + 2]), (8, LANES)
        )
        gains_ref[p] = jnp.broadcast_to(gain_ref[:, p * LANES : (p + 1) * LANES], (8, LANES))
        xfs_ref[p] = x_taps[:, p * LANES : (p + 1) * LANES]
    for p in range(2):
        mfs_ref[p] = m_taps[:, p * LANES : (p + 1) * LANES]

    channels = x_ref.shape[1]
    term = lax.broadcasted_iota(jnp.int32, (LANES, channels), 0)
    lane = lax.broadcasted_iota(jnp.int32, (LANES, channels), 1)
    width = channels // heads
    match = (lane >= (term & (heads - 1)) * width) & (lane < ((term & (heads - 1)) + 1) * width)
    pick_sum = jnp.where(match & (term < 3 * heads), 1.0, 0.0).astype(jnp.bfloat16)
    pick_source = jnp.where(match & (term >= 3 * heads) & (term < 6 * heads), 1.0, 0.0).astype(jnp.bfloat16)
    quarter = length // 4
    few = jnp.concatenate([left_ref[(j + 1) * quarter - HALO : (j + 1) * quarter, :] for j in range(4)], axis=0)
    few = jnp.dot(few, pick_sum, preferred_element_type=jnp.float32)
    for p in range(pairs):
        cols = slice(p * LANES, (p + 1) * LANES)
        pick_ref[p, :, :LANES] = pick_sum[:, cols]
        pick_ref[p, :, LANES:] = pick_source[:, cols]
        for j in range(4):
            row = few[(j + 1) * HALO - 1 : (j + 1) * HALO, cols]
            mid_ref[p, j] = jnp.broadcast_to(row, (8, LANES))
        dsend_ref[p] = jnp.broadcast_to(few[4 * HALO - 1 :, cols], (8, LANES))
    dec_copy = remote(dsend_ref, drecv_ref, dec_send, dec_recv, {"ctx": mate})
    dec_copy.start()

    taps = xf_ref.shape[0]

    def conv(block, halo, filters, slot):
        pad_ref[slot, 0:8] = halo.astype(jnp.float32)[HALO - 8 :]
        pad_ref[slot, 8:] = block.astype(jnp.float32)
        total = filters[0:1] * pad_ref[slot, 9 - taps : 9 - taps + length]
        for k in range(1, taps):
            start = 9 - taps + k
            total = total + filters[k : k + 1] * pad_ref[slot, start : start + length]
        return half_silu(total)

    m_copy.wait()

    @pl.when(has_prev)
    def _():
        halo_m.wait_recv()
        halo_x.wait_recv()

    bt_ref[...] = conv(m_ref[:, :LANES], hm_ref[:, :LANES], mfs_ref[0], 0).T.astype(jnp.bfloat16)
    x_copy.wait()

    def pair_copy(p):
        return remote(lsend_ref.at[p], lrecv_ref.at[p], pair_send.at[p], pair_recv.at[p], {"ctx": mate})

    half = length // 2

    def local_state(p, slot):
        cols = pl.ds(pl.multiple_of(p * LANES, LANES), LANES)
        xc = conv(x_ref[:, cols], hx_ref[:, cols], xfs_ref[p], slot).astype(jnp.bfloat16)
        xc_ref[p] = xc
        source = jnp.dot(left_ref[...], pick_ref[p, :, LANES:], preferred_element_type=jnp.float32)
        wide = xc.astype(jnp.float32)
        end = dsend_ref[p][0:1]
        border = mid_ref[p, 1][0:1]
        mids, states = [], []
        for j, stop in ((0, border), (1, end)):
            here = slice(j * half, (j + 1) * half)
            mid = mid_ref[p, 2 * j][0:1]
            u = (jnp.exp(source[here] - mid) * wide[here]).astype(jnp.bfloat16)
            uc_ref[p, here] = u
            fresh = jnp.dot(bt_ref[:, here], u, preferred_element_type=jnp.float32)
            mids.append(mid)
            states.append(fresh * jnp.exp(mid - stop))
        first_ref[p] = (states[0] * jnp.exp(border - mids[1])).astype(jnp.bfloat16)
        state = states[0] * jnp.exp(border - end) + states[1]
        lown_ref[p] = state
        lsend_ref[p] = state.astype(jnp.bfloat16)
        pair_copy(p).start()

    is_odd = odd.astype(jnp.float32)
    is_even = 1.0 - is_odd
    next_pair = {"ctx": (ctx + 2) % n_ctx}

    def chain_copy(p):
        return remote(csend_ref.at[p], crecv_ref.at[p], chain_send.at[p], chain_recv.at[p], next_pair)

    @pl.when(z == 0)
    def _():
        crecv_ref[...] = jnp.zeros_like(crecv_ref)

    dec_copy.wait_recv()

    def relay(p):
        pair_copy(p).wait_recv()
        mine = lown_ref[p]
        theirs = lrecv_ref[p].astype(jnp.float32)
        d_mine = jnp.exp(-dsend_ref[p][0:1])
        d_theirs = jnp.exp(-drecv_ref[p][0:1])
        l_even = mine * is_even + theirs * is_odd
        l_odd = mine * is_odd + theirs * is_even
        d_even = d_mine * is_even + d_theirs * is_odd
        d_odd = d_mine * is_odd + d_theirs * is_even

        @pl.when(z > 0)
        def _():
            chain_copy(p).wait_recv()

        entering = crecv_ref[p].astype(jnp.float32)
        middle = d_even * entering + l_even
        sr_ref[p] = (entering * is_even + middle * is_odd).astype(jnp.bfloat16)

        @pl.when(z < n_z - 1)
        def _():
            csend_ref[p] = (d_odd * middle + l_odd).astype(jnp.bfloat16)
            chain_copy(p).start()

    def scores_of_halves():
        c_ref[...] = conv(m_ref[:, LANES:], hm_ref[:, LANES:], mfs_ref[1], 1).astype(jnp.bfloat16)
        row_half = lax.broadcasted_iota(jnp.int32, (half, half), 0)
        col_half = lax.broadcasted_iota(jnp.int32, (half, half), 1)
        for j in range(2):
            here = slice(j * half, (j + 1) * half)
            scores = jnp.dot(c_ref[here, :], bt_ref[:, here], preferred_element_type=jnp.float32)
            cb_ref[j] = jnp.where(row_half >= col_half, scores, 0.0).astype(jnp.bfloat16)

    def within(p):
        cols = pl.ds(pl.multiple_of(p * LANES, LANES), LANES)
        skip = skips_ref[p][0:1]
        sums = jnp.dot(left_ref[...], pick_ref[p, :, :LANES], preferred_element_type=jnp.float32)
        for j in range(2):
            here = slice(j * half, (j + 1) * half)
            own = jnp.dot(cb_ref[j], uc_ref[p, here], preferred_element_type=jnp.float32)
            if j == 1:
                own = own + jnp.dot(c_ref[here, :], first_ref[p], preferred_element_type=jnp.float32)
            mid = mid_ref[p, 2 * j][0:1]
            decay = jnp.exp(mid - sums[here])
            gate = half_silu(z_ref[here, cols].astype(jnp.float32))
            yg_ref[p, here] = (decay * own + skip * xc_ref[p, here].astype(jnp.float32)) * gate
            eg_ref[p, here] = decay * jnp.exp(-mid) * gate

    z_copy.wait()
    twos = pairs // 2
    lag = jnp.minimum(2 + 2 * z, 2 * twos)

    def turn(i, _):
        @pl.when((i >= lag) & (i < lag + twos))
        def _():
            for slot in range(2):
                relay(2 * (i - lag) + slot)

        @pl.when(i < twos)
        def _():
            for slot in range(2):
                local_state(2 * i + slot, slot)

        @pl.when(i == twos)
        def _():
            scores_of_halves()

        @pl.when((i >= twos) & (i < 2 * twos))
        def _():
            for slot in range(2):
                within(2 * (i - twos) + slot)

        return 0

    lax.fori_loop(0, 3 * twos, turn, 0)

    squares = jnp.zeros((length, LANES), jnp.float32)
    for p in range(pairs):
        inter = jnp.dot(c_ref[...], sr_ref[p], preferred_element_type=jnp.float32)
        gated = yg_ref[p] + eg_ref[p] * inter
        gated_ref[p] = gated
        squares = squares + gated * gated
    scale = lax.rsqrt(jnp.sum(squares, axis=1, keepdims=True) / channels + 1e-05)
    for p in range(pairs):
        normed_ref[:, p * LANES : (p + 1) * LANES] = (
            gated_ref[p] * scale * gains_ref[p][0:1]
        ).astype(jnp.bfloat16)

    def core_copy(slot, k):
        rows_of = (y + slot) % n_y
        return remote(
            part_ref.at[rows_of, k, 1 - core], core_ref.at[rows_of, k],
            core_send.at[slot, k], core_recv.at[slot, k], {"tp": other_core},
        )

    def y_copy(slot, k):
        target = ((y + slot) % n_y) * 2 + core
        return remote(
            ysend_ref.at[slot - 1, k], yrecv_ref.at[slot - 1, k],
            y_send.at[slot - 1, k], y_recv.at[slot - 1, k], {"tp": target},
        )

    def chip_sum(slot, k):
        core_copy(slot, k).wait_recv()
        rows_of = (y + slot) % n_y
        return part_ref[rows_of, k, core].astype(jnp.float32) + core_ref[rows_of, k].astype(jnp.float32)

    def forward(k):
        for slot in range(1, n_y):
            ysend_ref[slot - 1, k] = chip_sum(slot, k).astype(jnp.bfloat16)
            y_copy(slot, k).start()

    def column(k, _):
        cols = pl.ds(pl.multiple_of(k * chunk, chunk), chunk)
        part = jnp.dot(normed_ref[...], w_ref[:, cols], preferred_element_type=jnp.float32)
        part = part.astype(jnp.bfloat16)
        for row_y in range(n_y):
            for row_core in range(2):
                first = (2 * row_y + row_core) * rows
                part_ref[row_y, k, row_core] = part[first : first + rows]
        for slot in list(range(1, n_y)) + [0]:
            core_copy(slot, k).start()

        @pl.when(k > 0)
        def _():
            forward(k - 1)

        return 0

    w_copy.wait()
    lax.fori_loop(0, n_chunks, column, 0)
    forward(n_chunks - 1)

    def out_copy(k):
        cols = pl.ds(pl.multiple_of(k * chunk, chunk), chunk)
        return pltpu.make_async_copy(out_buf.at[k], out_ref.at[:, cols], out_sem.at[k])

    def finish(k, _):
        total = chip_sum(0, k)
        for slot in range(1, n_y):
            y_copy(slot, k).wait_recv()
            total = total + yrecv_ref[slot - 1, k].astype(jnp.float32)
        out_buf[k] = total.astype(jnp.bfloat16)
        out_copy(k).start()
        return 0

    lax.fori_loop(0, n_chunks, finish, 0)

    @pl.when(has_next)
    def _():
        halo_m.wait_send()
        halo_x.wait_send()

    dec_copy.wait_send()

    def drain_states(p, _):
        pair_copy(p).wait_send()

        @pl.when(z < n_z - 1)
        def _():
            chain_copy(p).wait_send()

        return 0

    lax.fori_loop(0, pairs, drain_states, 0)

    def drain_parts(k, _):
        out_copy(k).wait()
        for slot in range(n_y):
            core_copy(slot, k).wait_send()
        for slot in range(1, n_y):
            y_copy(slot, k).wait_send()
        return 0

    lax.fori_loop(0, n_chunks, drain_parts, 0)


def on_device(n_ctx, n_tp, *args):
    (x_inputs, state_maps, z_gate, step_raw, step_bias, decay_log, skip_gain,
     x_filter, state_filter, norm_gain, out_weight) = args
    length, channels = x_inputs.shape
    heads = step_raw.shape[1]
    pairs = channels // LANES
    model = out_weight.shape[1]
    rows = length // n_tp
    n_y = n_tp // 2
    chunk = 256
    n_chunks = model // chunk
    state = state_maps.shape[1] // 2
    bf16, f32 = jnp.bfloat16, jnp.float32
    vmem = pl.BlockSpec(memory_space=pltpu.VMEM)
    anywhere = pl.BlockSpec(memory_space=pl.ANY)
    dma = pltpu.SemaphoreType.DMA
    scratch = [
        pltpu.VMEM(out_weight.shape, bf16),
        pltpu.VMEM(x_inputs.shape, bf16),
        pltpu.VMEM(state_maps.shape, bf16),
        pltpu.VMEM(z_gate.shape, bf16),
        pltpu.VMEM((HALO, channels), bf16),
        pltpu.VMEM((HALO, 2 * state), bf16),
        pltpu.VMEM((2, length + 8, LANES), f32),
        pltpu.VMEM((pairs, x_filter.shape[0], LANES), f32),
        pltpu.VMEM((2, x_filter.shape[0], LANES), f32),
        pltpu.VMEM((pairs, 8, LANES), f32),
        pltpu.VMEM((pairs, 8, LANES), f32),
        pltpu.VMEM((LANES, LANES), f32),
        pltpu.VMEM((LANES, length), f32),
        pltpu.VMEM((length, LANES), bf16),
        pltpu.VMEM((pairs, LANES, 2 * LANES), bf16),
        pltpu.VMEM((pairs, 8, LANES), f32),
        pltpu.VMEM((pairs, 8, LANES), f32),
        pltpu.VMEM((pairs, length, LANES), bf16),
        pltpu.VMEM((pairs, length, LANES), bf16),
        pltpu.VMEM((pairs, 4, 8, LANES), f32),
        pltpu.VMEM((pairs, state, LANES), bf16),
        pltpu.VMEM((state, length), bf16),
        pltpu.VMEM((length, state), bf16),
        pltpu.VMEM((2, length // 2, length // 2), bf16),
        pltpu.VMEM((pairs, state, LANES), f32),
        pltpu.VMEM((pairs, state, LANES), bf16),
        pltpu.VMEM((pairs, state, LANES), bf16),
        pltpu.VMEM((pairs, state, LANES), bf16),
        pltpu.VMEM((pairs, state, LANES), bf16),
        pltpu.VMEM((pairs, state, LANES), bf16),
        pltpu.VMEM((pairs, length, LANES), f32),
        pltpu.VMEM((pairs, length, LANES), f32),
        pltpu.VMEM((pairs, length, LANES), f32),
        pltpu.VMEM((length, channels), bf16),
        pltpu.VMEM((n_y, n_chunks, 2, rows, chunk), bf16),
        pltpu.VMEM((n_y, n_chunks, rows, chunk), bf16),
        pltpu.VMEM((n_y - 1, n_chunks, rows, chunk), bf16),
        pltpu.VMEM((n_y - 1, n_chunks, rows, chunk), bf16),
        pltpu.VMEM((n_chunks, rows, chunk), bf16),
        dma, dma((3,)), dma((n_chunks,)), dma((2,)), dma((2,)), dma, dma,
        dma((pairs,)), dma((pairs,)), dma((pairs,)), dma((pairs,)),
        dma((n_y, n_chunks)), dma((n_y, n_chunks)),
        dma((n_y - 1, n_chunks)), dma((n_y - 1, n_chunks)),
    ]
    return pl.pallas_call(
        functools.partial(layer_kernel, n_ctx, n_tp, chunk),
        out_shape=jax.ShapeDtypeStruct((rows, model), bf16),
        in_specs=[anywhere] * 3 + [vmem] * 7 + [anywhere],
        out_specs=anywhere,
        scratch_shapes=scratch,
        compiler_params=pltpu.CompilerParams(
            collective_id=0, has_side_effects=True, vmem_limit_bytes=58 * 1024 * 1024
        ),
        cost_estimate=pl.CostEstimate(
            flops=2 * length * channels * (model + 2 * length), bytes_accessed=4 * out_weight.size,
            transcendentals=length * length * heads,
        ),
        name="layer",
    )(
        x_inputs, state_maps, z_gate, step_raw.T, step_bias[None], decay_log[None], skip_gain[None],
        x_filter, state_filter, norm_gain[None], out_weight,
    )


def solution(mesh):
    return jax.shard_map(
        functools.partial(on_device, mesh.shape["ctx"], mesh.shape["tp"]),
        mesh=mesh,
        in_specs=(
            P("ctx", "tp"),
            P("ctx", "tp"),
            P("ctx", "tp"),
            P("ctx", "tp"),
            P("tp"),
            P("tp"),
            P("tp"),
            P(None, "tp"),
            P(None, "tp"),
            P("tp"),
            P("tp", None),
        ),
        out_specs=P(("ctx", "tp"), None),
        check_vma=False,
    )
```

```python
import functools

import jax
import jax.numpy as jnp
from jax import lax
from jax.experimental import pallas as pl
from jax.experimental.pallas import tpu as pltpu
from jax.sharding import PartitionSpec as P

MESH = pl.DeviceIdType.MESH
LANES = 128
HALO = 16


def half_silu(v):
    h = 0.5 * v
    return h + h * jnp.tanh(h)


def layer_kernel(
    n_ctx, n_tp, chunk,
    x_hbm, m_hbm, z_hbm, step_ref, bias_ref, decay_ref, skip_ref, xf_ref, mf_ref, gain_ref, w_hbm,
    out_ref,
    w_ref, x_ref, m_ref, z_ref, hx_ref, hm_ref, pad_ref, xfs_ref, mfs_ref, gains_ref, skips_ref,
    parts_ref, left_ref, pick_ref, dsend_ref, drecv_ref,
    xc_ref, uc_ref, mid_ref, first_ref, bt_ref, c_ref, cb_ref, lown_ref, lsend_ref, lrecv_ref, csend_ref, crecv_ref, sr_ref,
    yg_ref, eg_ref, squares_ref, gated_ref, normed_ref, part_ref, core_ref, ysend_ref, yrecv_ref, out_buf,
    w_sem, in_sem, out_sem, halo_send, halo_recv, dec_send, dec_recv, pair_send, pair_recv, chain_send, chain_recv,
    core_send, core_recv, y_send, y_recv,
):
    length = x_ref.shape[0]
    pairs = x_ref.shape[1] // LANES
    heads = step_ref.shape[0]
    n_y = n_tp // 2
    rows = length // n_tp
    n_chunks = w_hbm.shape[1] // chunk
    n_z = n_ctx // 2
    ctx = lax.axis_index("ctx")
    tp = lax.axis_index("tp")
    y, core = tp // 2, tp % 2
    z, odd = ctx // 2, ctx % 2
    mate = ctx + 1 - 2 * odd
    other_core = y * 2 + 1 - core

    w_copy = pltpu.make_async_copy(w_hbm, w_ref, w_sem)
    m_copy = pltpu.make_async_copy(m_hbm, m_ref, in_sem.at[0])
    x_copy = pltpu.make_async_copy(x_hbm, x_ref, in_sem.at[1])
    z_copy = pltpu.make_async_copy(z_hbm, z_ref, in_sem.at[2])

    barrier = pltpu.get_barrier_semaphore()
    has_prev, has_next = ctx >= 1, ctx <= n_ctx - 2
    for there, off in ((has_prev, -1), (has_next, 1), (ctx >= 2, -2), (ctx <= n_ctx - 3, 2)):

        @pl.when(there)
        def _(off=off):
            pl.semaphore_signal(barrier, inc=1, device_id={"ctx": ctx + off}, device_id_type=MESH)

    pl.semaphore_signal(barrier, inc=1, device_id={"tp": other_core}, device_id_type=MESH)
    for off in range(1, n_y):
        pl.semaphore_signal(
            barrier, inc=1, device_id={"tp": ((y + off) % n_y) * 2 + core}, device_id_type=MESH
        )

    for copy in (m_copy, x_copy, z_copy, w_copy):
        copy.start()

    def remote(src, dst, send, recv, where):
        return pltpu.make_async_remote_copy(
            src_ref=src, dst_ref=dst, send_sem=send, recv_sem=recv, device_id=where, device_id_type=MESH
        )

    def three_terms(v):
        first = v.astype(jnp.bfloat16).astype(jnp.float32)
        second = (v - first).astype(jnp.bfloat16).astype(jnp.float32)
        return [first, second, (v - first - second).astype(jnp.bfloat16).astype(jnp.float32)]

    def all_tokens(column):
        return jnp.concatenate([column] * (length // LANES), axis=1)

    filling = jnp.zeros((1, LANES - 3 * heads), jnp.float32)
    vectors = jnp.concatenate([bias_ref[...], decay_ref[...], skip_ref[...], filling], axis=1)
    columns = jnp.broadcast_to(vectors, (LANES, LANES)).T
    step = jnp.log(1.0 + jnp.exp(step_ref[...] + all_tokens(columns[:heads])))
    rate = step * jnp.exp(all_tokens(columns[heads : 2 * heads]))
    skip_t = columns[2 * heads : 3 * heads]

    greeted = jnp.minimum(ctx, 2) + jnp.minimum(n_ctx - 1 - ctx, 2)
    pl.semaphore_wait(barrier, greeted + 1 + (n_y - 1))

    following = {"ctx": (ctx + 1) % n_ctx}
    halo_x = remote(x_hbm.at[pl.ds(length - HALO, HALO)], hx_ref, halo_send.at[0], halo_recv.at[0], following)
    halo_m = remote(m_hbm.at[pl.ds(length - HALO, HALO)], hm_ref, halo_send.at[1], halo_recv.at[1], following)

    @pl.when(has_next)
    def _():
        halo_m.start()
        halo_x.start()

    @pl.when(ctx == 0)
    def _():
        hm_ref[...] = jnp.zeros_like(hm_ref)
        hx_ref[...] = jnp.zeros_like(hx_ref)


    s_ids = lax.broadcasted_iota(jnp.int32, (length, length), 0)
    t_ids = lax.broadcasted_iota(jnp.int32, (length, length), 1)
    upper = jnp.where(s_ids <= t_ids, 1.0, 0.0).astype(jnp.bfloat16)
    sums = jnp.dot(
        jnp.concatenate(three_terms(rate), axis=0).astype(jnp.bfloat16), upper,
        preferred_element_type=jnp.float32,
    )
    sums = sums[:heads] + sums[heads : 2 * heads] + sums[2 * heads :]
    source = sums + jnp.log(step)
    filler = jnp.ones((LANES - 6 * heads, length), jnp.float32)
    parts_ref[...] = jnp.concatenate(three_terms(sums) + three_terms(source) + [filler], axis=0)
    left_ref[...] = parts_ref[...].T.astype(jnp.bfloat16)

    lane_row = lax.broadcasted_iota(jnp.int32, (1, LANES), 1) < LANES // 2
    x_taps = xf_ref[...].astype(jnp.float32)
    m_taps = mf_ref[...].astype(jnp.float32)
    for p in range(pairs):
        skips_ref[p] = jnp.broadcast_to(
            jnp.where(lane_row, skip_t[2 * p : 2 * p + 1], skip_t[2 * p + 1 : 2 * p + 2]), (8, LANES)
        )
        gains_ref[p] = jnp.broadcast_to(gain_ref[:, p * LANES : (p + 1) * LANES], (8, LANES))
        xfs_ref[p] = x_taps[:, p * LANES : (p + 1) * LANES]
    for p in range(2):
        mfs_ref[p] = m_taps[:, p * LANES : (p + 1) * LANES]

    channels = x_ref.shape[1]
    term = lax.broadcasted_iota(jnp.int32, (LANES, channels), 0)
    lane = lax.broadcasted_iota(jnp.int32, (LANES, channels), 1)
    width = channels // heads
    match = (lane >= (term & (heads - 1)) * width) & (lane < ((term & (heads - 1)) + 1) * width)
    pick_sum = jnp.where(match & (term < 3 * heads), 1.0, 0.0).astype(jnp.bfloat16)
    pick_source = jnp.where(match & (term >= 3 * heads) & (term < 6 * heads), 1.0, 0.0).astype(jnp.bfloat16)
    quarter = length // 4
    few = jnp.concatenate([left_ref[(j + 1) * quarter - HALO : (j + 1) * quarter, :] for j in range(4)], axis=0)
    few = jnp.dot(few, pick_sum, preferred_element_type=jnp.float32)
    for p in range(pairs):
        cols = slice(p * LANES, (p + 1) * LANES)
        pick_ref[p, :, :LANES] = pick_sum[:, cols]
        pick_ref[p, :, LANES:] = pick_source[:, cols]
        for j in range(4):
            row = few[(j + 1) * HALO - 1 : (j + 1) * HALO, cols]
            mid_ref[p, j] = jnp.broadcast_to(row, (8, LANES))
        dsend_ref[p] = jnp.broadcast_to(few[4 * HALO - 1 :, cols], (8, LANES))
    dec_copy = remote(dsend_ref, drecv_ref, dec_send, dec_recv, {"ctx": mate})
    dec_copy.start()

    taps = xf_ref.shape[0]

    def conv(block, halo, filters, slot):
        pad_ref[slot, 0:8] = halo.astype(jnp.float32)[HALO - 8 :]
        pad_ref[slot, 8:] = block.astype(jnp.float32)
        total = filters[0:1] * pad_ref[slot, 9 - taps : 9 - taps + length]
        for k in range(1, taps):
            start = 9 - taps + k
            total = total + filters[k : k + 1] * pad_ref[slot, start : start + length]
        return half_silu(total)

    m_copy.wait()

    @pl.when(has_prev)
    def _():
        halo_m.wait_recv()
        halo_x.wait_recv()

    bt_ref[...] = conv(m_ref[:, :LANES], hm_ref[:, :LANES], mfs_ref[0], 0).T.astype(jnp.bfloat16)
    x_copy.wait()

    def pair_copy(p):
        return remote(lsend_ref.at[p], lrecv_ref.at[p], pair_send.at[p], pair_recv.at[p], {"ctx": mate})

    half = length // 2

    def local_state(p, slot):
        cols = pl.ds(pl.multiple_of(p * LANES, LANES), LANES)
        xc = conv(x_ref[:, cols], hx_ref[:, cols], xfs_ref[p], slot).astype(jnp.bfloat16)
        xc_ref[p] = xc
        source = jnp.dot(left_ref[...], pick_ref[p, :, LANES:], preferred_element_type=jnp.float32)
        wide = xc.astype(jnp.float32)
        end = dsend_ref[p][0:1]
        border = mid_ref[p, 1][0:1]
        mids, states = [], []
        for j, stop in ((0, border), (1, end)):
            here = slice(j * half, (j + 1) * half)
            mid = mid_ref[p, 2 * j][0:1]
            u = (jnp.exp(source[here] - mid) * wide[here]).astype(jnp.bfloat16)
            uc_ref[p, here] = u
            fresh = jnp.dot(bt_ref[:, here], u, preferred_element_type=jnp.float32)
            mids.append(mid)
            states.append(fresh * jnp.exp(mid - stop))
        first_ref[p] = (states[0] * jnp.exp(border - mids[1])).astype(jnp.bfloat16)
        state = states[0] * jnp.exp(border - end) + states[1]
        lown_ref[p] = state
        lsend_ref[p] = state.astype(jnp.bfloat16)
        pair_copy(p).start()

    is_odd = odd.astype(jnp.float32)
    is_even = 1.0 - is_odd
    next_pair = {"ctx": (ctx + 2) % n_ctx}

    def chain_copy(p):
        return remote(csend_ref.at[p], crecv_ref.at[p], chain_send.at[p], chain_recv.at[p], next_pair)

    @pl.when(z == 0)
    def _():
        crecv_ref[...] = jnp.zeros_like(crecv_ref)

    dec_copy.wait_recv()

    def relay(p):
        pair_copy(p).wait_recv()
        mine = lown_ref[p]
        theirs = lrecv_ref[p].astype(jnp.float32)
        d_mine = jnp.exp(-dsend_ref[p][0:1])
        d_theirs = jnp.exp(-drecv_ref[p][0:1])
        l_even = mine * is_even + theirs * is_odd
        l_odd = mine * is_odd + theirs * is_even
        d_even = d_mine * is_even + d_theirs * is_odd
        d_odd = d_mine * is_odd + d_theirs * is_even

        @pl.when(z > 0)
        def _():
            chain_copy(p).wait_recv()

        entering = crecv_ref[p].astype(jnp.float32)
        middle = d_even * entering + l_even
        sr_ref[p] = (entering * is_even + middle * is_odd).astype(jnp.bfloat16)

        @pl.when(z < n_z - 1)
        def _():
            csend_ref[p] = (d_odd * middle + l_odd).astype(jnp.bfloat16)
            chain_copy(p).start()

    def scores_of_halves():
        c_ref[...] = conv(m_ref[:, LANES:], hm_ref[:, LANES:], mfs_ref[1], 1).astype(jnp.bfloat16)
        row_half = lax.broadcasted_iota(jnp.int32, (half, half), 0)
        col_half = lax.broadcasted_iota(jnp.int32, (half, half), 1)
        for j in range(2):
            here = slice(j * half, (j + 1) * half)
            scores = jnp.dot(c_ref[here, :], bt_ref[:, here], preferred_element_type=jnp.float32)
            cb_ref[j] = jnp.where(row_half >= col_half, scores, 0.0).astype(jnp.bfloat16)

    def within(p):
        cols = pl.ds(pl.multiple_of(p * LANES, LANES), LANES)
        skip = skips_ref[p][0:1]
        sums = jnp.dot(left_ref[...], pick_ref[p, :, :LANES], preferred_element_type=jnp.float32)
        for j in range(2):
            here = slice(j * half, (j + 1) * half)
            own = jnp.dot(cb_ref[j], uc_ref[p, here], preferred_element_type=jnp.float32)
            if j == 1:
                own = own + jnp.dot(c_ref[here, :], first_ref[p], preferred_element_type=jnp.float32)
            mid = mid_ref[p, 2 * j][0:1]
            decay = jnp.exp(mid - sums[here])
            gate = half_silu(z_ref[here, cols].astype(jnp.float32))
            yg_ref[p, here] = (decay * own + skip * xc_ref[p, here].astype(jnp.float32)) * gate
            eg_ref[p, here] = decay * jnp.exp(-mid) * gate

    z_copy.wait()
    twos = pairs // 2
    lag = jnp.minimum(2 + 2 * z, 2 * twos)

    gate_lag = jnp.maximum(lag, twos)
    squares_ref[...] = jnp.zeros_like(squares_ref)

    def gate_rows(p):
        inter = jnp.dot(c_ref[...], sr_ref[p], preferred_element_type=jnp.float32)
        gated = yg_ref[p] + eg_ref[p] * inter
        gated_ref[p] = gated
        squares_ref[...] += gated * gated

    def turn(i, _):
        @pl.when(i < twos)
        def _():
            for slot in range(2):
                local_state(2 * i + slot, slot)

        @pl.when((i >= lag) & (i < lag + twos))
        def _():
            for slot in range(2):
                relay(2 * (i - lag) + slot)

        @pl.when(i == twos)
        def _():
            scores_of_halves()

        @pl.when((i >= twos) & (i < 2 * twos))
        def _():
            for slot in range(2):
                within(2 * (i - twos) + slot)

        @pl.when((i >= gate_lag) & (i < gate_lag + twos))
        def _():
            for slot in range(2):
                gate_rows(2 * (i - gate_lag) + slot)

        return 0

    lax.fori_loop(0, 3 * twos, turn, 0)

    scale = lax.rsqrt(jnp.sum(squares_ref[...], axis=1, keepdims=True) / channels + 1e-05)
    for p in range(pairs):
        normed_ref[:, p * LANES : (p + 1) * LANES] = (
            gated_ref[p] * scale * gains_ref[p][0:1]
        ).astype(jnp.bfloat16)

    def core_copy(slot, k):
        rows_of = (y + slot) % n_y
        return remote(
            part_ref.at[rows_of, k, 1 - core], core_ref.at[rows_of, k],
            core_send.at[slot, k], core_recv.at[slot, k], {"tp": other_core},
        )

    def y_copy(slot, k):
        target = ((y + slot) % n_y) * 2 + core
        return remote(
            ysend_ref.at[slot - 1, k], yrecv_ref.at[slot - 1, k],
            y_send.at[slot - 1, k], y_recv.at[slot - 1, k], {"tp": target},
        )

    def chip_sum(slot, k):
        core_copy(slot, k).wait_recv()
        rows_of = (y + slot) % n_y
        return part_ref[rows_of, k, core].astype(jnp.float32) + core_ref[rows_of, k].astype(jnp.float32)

    def forward(k):
        for slot in range(1, n_y):
            ysend_ref[slot - 1, k] = chip_sum(slot, k).astype(jnp.bfloat16)
            y_copy(slot, k).start()

    def column(k, _):
        cols = pl.ds(pl.multiple_of(k * chunk, chunk), chunk)
        part = jnp.dot(normed_ref[...], w_ref[:, cols], preferred_element_type=jnp.float32)
        part = part.astype(jnp.bfloat16)
        for row_y in range(n_y):
            for row_core in range(2):
                first = (2 * row_y + row_core) * rows
                part_ref[row_y, k, row_core] = part[first : first + rows]
        for slot in list(range(1, n_y)) + [0]:
            core_copy(slot, k).start()

        @pl.when(k > 0)
        def _():
            forward(k - 1)

        return 0

    w_copy.wait()
    lax.fori_loop(0, n_chunks, column, 0)
    forward(n_chunks - 1)

    def out_copy(k):
        cols = pl.ds(pl.multiple_of(k * chunk, chunk), chunk)
        return pltpu.make_async_copy(out_buf.at[k], out_ref.at[:, cols], out_sem.at[k])

    def finish(k, _):
        total = chip_sum(0, k)
        for slot in range(1, n_y):
            y_copy(slot, k).wait_recv()
            total = total + yrecv_ref[slot - 1, k].astype(jnp.float32)
        out_buf[k] = total.astype(jnp.bfloat16)
        out_copy(k).start()
        return 0

    lax.fori_loop(0, n_chunks, finish, 0)

    @pl.when(has_next)
    def _():
        halo_m.wait_send()
        halo_x.wait_send()

    dec_copy.wait_send()

    def drain_states(p, _):
        pair_copy(p).wait_send()

        @pl.when(z < n_z - 1)
        def _():
            chain_copy(p).wait_send()

        return 0

    lax.fori_loop(0, pairs, drain_states, 0)

    def drain_parts(k, _):
        out_copy(k).wait()
        for slot in range(n_y):
            core_copy(slot, k).wait_send()
        for slot in range(1, n_y):
            y_copy(slot, k).wait_send()
        return 0

    lax.fori_loop(0, n_chunks, drain_parts, 0)


def on_device(n_ctx, n_tp, *args):
    (x_inputs, state_maps, z_gate, step_raw, step_bias, decay_log, skip_gain,
     x_filter, state_filter, norm_gain, out_weight) = args
    length, channels = x_inputs.shape
    heads = step_raw.shape[1]
    pairs = channels // LANES
    model = out_weight.shape[1]
    rows = length // n_tp
    n_y = n_tp // 2
    chunk = 256
    n_chunks = model // chunk
    state = state_maps.shape[1] // 2
    bf16, f32 = jnp.bfloat16, jnp.float32
    vmem = pl.BlockSpec(memory_space=pltpu.VMEM)
    anywhere = pl.BlockSpec(memory_space=pl.ANY)
    dma = pltpu.SemaphoreType.DMA
    scratch = [
        pltpu.VMEM(out_weight.shape, bf16),
        pltpu.VMEM(x_inputs.shape, bf16),
        pltpu.VMEM(state_maps.shape, bf16),
        pltpu.VMEM(z_gate.shape, bf16),
        pltpu.VMEM((HALO, channels), bf16),
        pltpu.VMEM((HALO, 2 * state), bf16),
        pltpu.VMEM((2, length + 8, LANES), f32),
        pltpu.VMEM((pairs, x_filter.shape[0], LANES), f32),
        pltpu.VMEM((2, x_filter.shape[0], LANES), f32),
        pltpu.VMEM((pairs, 8, LANES), f32),
        pltpu.VMEM((pairs, 8, LANES), f32),
        pltpu.VMEM((LANES, length), f32),
        pltpu.VMEM((length, LANES), bf16),
        pltpu.VMEM((pairs, LANES, 2 * LANES), bf16),
        pltpu.VMEM((pairs, 8, LANES), f32),
        pltpu.VMEM((pairs, 8, LANES), f32),
        pltpu.VMEM((pairs, length, LANES), bf16),
        pltpu.VMEM((pairs, length, LANES), bf16),
        pltpu.VMEM((pairs, 4, 8, LANES), f32),
        pltpu.VMEM((pairs, state, LANES), bf16),
        pltpu.VMEM((state, length), bf16),
        pltpu.VMEM((length, state), bf16),
        pltpu.VMEM((2, length // 2, length // 2), bf16),
        pltpu.VMEM((pairs, state, LANES), f32),
        pltpu.VMEM((pairs, state, LANES), bf16),
        pltpu.VMEM((pairs, state, LANES), bf16),
        pltpu.VMEM((pairs, state, LANES), bf16),
        pltpu.VMEM((pairs, state, LANES), bf16),
        pltpu.VMEM((pairs, state, LANES), bf16),
        pltpu.VMEM((pairs, length, LANES), f32),
        pltpu.VMEM((pairs, length, LANES), f32),
        pltpu.VMEM((length, LANES), f32),
        pltpu.VMEM((pairs, length, LANES), f32),
        pltpu.VMEM((length, channels), bf16),
        pltpu.VMEM((n_y, n_chunks, 2, rows, chunk), bf16),
        pltpu.VMEM((n_y, n_chunks, rows, chunk), bf16),
        pltpu.VMEM((n_y - 1, n_chunks, rows, chunk), bf16),
        pltpu.VMEM((n_y - 1, n_chunks, rows, chunk), bf16),
        pltpu.VMEM((n_chunks, rows, chunk), bf16),
        dma, dma((3,)), dma((n_chunks,)), dma((2,)), dma((2,)), dma, dma,
        dma((pairs,)), dma((pairs,)), dma((pairs,)), dma((pairs,)),
        dma((n_y, n_chunks)), dma((n_y, n_chunks)),
        dma((n_y - 1, n_chunks)), dma((n_y - 1, n_chunks)),
    ]
    return pl.pallas_call(
        functools.partial(layer_kernel, n_ctx, n_tp, chunk),
        out_shape=jax.ShapeDtypeStruct((rows, model), bf16),
        in_specs=[anywhere] * 3 + [vmem] * 7 + [anywhere],
        out_specs=anywhere,
        scratch_shapes=scratch,
        compiler_params=pltpu.CompilerParams(
            collective_id=0, has_side_effects=True, vmem_limit_bytes=58 * 1024 * 1024
        ),
        cost_estimate=pl.CostEstimate(
            flops=2 * length * channels * (model + 2 * length), bytes_accessed=4 * out_weight.size,
            transcendentals=length * length * heads,
        ),
        name="layer",
    )(
        x_inputs, state_maps, z_gate, step_raw.T, step_bias[None], decay_log[None], skip_gain[None],
        x_filter, state_filter, norm_gain[None], out_weight,
    )


def solution(mesh):
    return jax.shard_map(
        functools.partial(on_device, mesh.shape["ctx"], mesh.shape["tp"]),
        mesh=mesh,
        in_specs=(
            P("ctx", "tp"),
            P("ctx", "tp"),
            P("ctx", "tp"),
            P("ctx", "tp"),
            P("tp"),
            P("tp"),
            P("tp"),
            P(None, "tp"),
            P(None, "tp"),
            P("tp"),
            P("tp", None),
        ),
        out_specs=P(("ctx", "tp"), None),
        check_vma=False,
    )
```

```python
import functools

import jax
import jax.numpy as jnp
from jax import lax
from jax.experimental import pallas as pl
from jax.experimental.pallas import tpu as pltpu
from jax.sharding import PartitionSpec as P

MESH = pl.DeviceIdType.MESH
LANES = 128
HALO = 16


def half_silu(v):
    h = 0.5 * v
    return h + h * jnp.tanh(h)


def layer_kernel(
    n_ctx, n_tp, chunk,
    x_hbm, m_hbm, z_hbm, step_ref, bias_ref, decay_ref, skip_ref, xf_ref, mf_ref, gain_ref, w_hbm,
    out_ref,
    w_ref, x_ref, m_ref, z_ref, hx_ref, hm_ref, pad_ref, xfs_ref, mfs_ref, gains_ref, skips_ref,
    parts_ref, left_ref, pick_ref, dsend_ref, drecv_ref,
    xc_ref, uc_ref, mid_ref, first_ref, bt_ref, c_ref, cb_ref, lown_ref, lsend_ref, lrecv_ref, csend_ref, crecv_ref, sr_ref,
    yg_ref, eg_ref, squares_ref, gated_ref, normed_ref, part_ref, core_ref, ysend_ref, yrecv_ref, out_buf,
    w_sem, in_sem, out_sem, halo_send, halo_recv, dec_send, dec_recv, pair_send, pair_recv, chain_send, chain_recv,
    core_send, core_recv, y_send, y_recv,
):
    length = x_ref.shape[0]
    pairs = x_ref.shape[1] // LANES
    heads = step_ref.shape[0]
    n_y = n_tp // 2
    rows = length // n_tp
    n_chunks = w_hbm.shape[1] // chunk
    n_z = n_ctx // 2
    ctx = lax.axis_index("ctx")
    tp = lax.axis_index("tp")
    y, core = tp // 2, tp % 2
    z, odd = ctx // 2, ctx % 2
    mate = ctx + 1 - 2 * odd
    other_core = y * 2 + 1 - core

    w_copy = pltpu.make_async_copy(w_hbm, w_ref, w_sem)
    m_copy = pltpu.make_async_copy(m_hbm, m_ref, in_sem.at[0])
    x_copy = pltpu.make_async_copy(x_hbm, x_ref, in_sem.at[1])
    z_copy = pltpu.make_async_copy(z_hbm, z_ref, in_sem.at[2])

    barrier = pltpu.get_barrier_semaphore()
    has_prev, has_next = ctx >= 1, ctx <= n_ctx - 2
    for there, off in ((has_prev, -1), (has_next, 1), (ctx >= 2, -2), (ctx <= n_ctx - 3, 2)):

        @pl.when(there)
        def _(off=off):
            pl.semaphore_signal(barrier, inc=1, device_id={"ctx": ctx + off}, device_id_type=MESH)

    pl.semaphore_signal(barrier, inc=1, device_id={"tp": other_core}, device_id_type=MESH)
    for off in range(1, n_y):
        pl.semaphore_signal(
            barrier, inc=1, device_id={"tp": ((y + off) % n_y) * 2 + core}, device_id_type=MESH
        )

    for copy in (m_copy, x_copy, z_copy, w_copy):
        copy.start()

    def remote(src, dst, send, recv, where):
        return pltpu.make_async_remote_copy(
            src_ref=src, dst_ref=dst, send_sem=send, recv_sem=recv, device_id=where, device_id_type=MESH
        )

    def three_terms(v):
        first = v.astype(jnp.bfloat16).astype(jnp.float32)
        second = (v - first).astype(jnp.bfloat16).astype(jnp.float32)
        return [first, second, (v - first - second).astype(jnp.bfloat16).astype(jnp.float32)]

    def all_tokens(column):
        return jnp.concatenate([column] * (length // LANES), axis=1)

    filling = jnp.zeros((1, LANES - 3 * heads), jnp.float32)
    vectors = jnp.concatenate([bias_ref[...], decay_ref[...], skip_ref[...], filling], axis=1)
    columns = jnp.broadcast_to(vectors, (LANES, LANES)).T
    step = jnp.log(1.0 + jnp.exp(step_ref[...] + all_tokens(columns[:heads])))
    rate = step * jnp.exp(all_tokens(columns[heads : 2 * heads]))
    skip_t = columns[2 * heads : 3 * heads]

    greeted = jnp.minimum(ctx, 2) + jnp.minimum(n_ctx - 1 - ctx, 2)
    pl.semaphore_wait(barrier, greeted + 1 + (n_y - 1))

    following = {"ctx": (ctx + 1) % n_ctx}
    halo_x = remote(x_hbm.at[pl.ds(length - HALO, HALO)], hx_ref, halo_send.at[0], halo_recv.at[0], following)
    halo_m = remote(m_hbm.at[pl.ds(length - HALO, HALO)], hm_ref, halo_send.at[1], halo_recv.at[1], following)

    @pl.when(has_next)
    def _():
        halo_m.start()
        halo_x.start()

    @pl.when(ctx == 0)
    def _():
        hm_ref[...] = jnp.zeros_like(hm_ref)
        hx_ref[...] = jnp.zeros_like(hx_ref)


    s_ids = lax.broadcasted_iota(jnp.int32, (length, length), 0)
    t_ids = lax.broadcasted_iota(jnp.int32, (length, length), 1)
    upper = jnp.where(s_ids <= t_ids, 1.0, 0.0).astype(jnp.bfloat16)
    sums = jnp.dot(
        jnp.concatenate(three_terms(rate), axis=0).astype(jnp.bfloat16), upper,
        preferred_element_type=jnp.float32,
    )
    sums = sums[:heads] + sums[heads : 2 * heads] + sums[2 * heads :]
    source = sums + jnp.log(step)
    filler = jnp.ones((LANES - 6 * heads, length), jnp.float32)
    parts_ref[...] = jnp.concatenate(three_terms(sums) + three_terms(source) + [filler], axis=0)
    left_ref[...] = parts_ref[...].T.astype(jnp.bfloat16)

    lane_row = lax.broadcasted_iota(jnp.int32, (1, LANES), 1) < LANES // 2
    x_taps = xf_ref[...].astype(jnp.float32)
    m_taps = mf_ref[...].astype(jnp.float32)
    for p in range(pairs):
        skips_ref[p] = jnp.broadcast_to(
            jnp.where(lane_row, skip_t[2 * p : 2 * p + 1], skip_t[2 * p + 1 : 2 * p + 2]), (8, LANES)
        )
        gains_ref[p] = jnp.broadcast_to(gain_ref[:, p * LANES : (p + 1) * LANES], (8, LANES))
        xfs_ref[p] = x_taps[:, p * LANES : (p + 1) * LANES]
    for p in range(2):
        mfs_ref[p] = m_taps[:, p * LANES : (p + 1) * LANES]

    channels = x_ref.shape[1]
    term = lax.broadcasted_iota(jnp.int32, (LANES, channels), 0)
    lane = lax.broadcasted_iota(jnp.int32, (LANES, channels), 1)
    width = channels // heads
    match = (lane >= (term & (heads - 1)) * width) & (lane < ((term & (heads - 1)) + 1) * width)
    pick_sum = jnp.where(match & (term < 3 * heads), 1.0, 0.0).astype(jnp.bfloat16)
    pick_source = jnp.where(match & (term >= 3 * heads) & (term < 6 * heads), 1.0, 0.0).astype(jnp.bfloat16)
    quarter = length // 4
    few = jnp.concatenate([left_ref[(j + 1) * quarter - HALO : (j + 1) * quarter, :] for j in range(4)], axis=0)
    few = jnp.dot(few, pick_sum, preferred_element_type=jnp.float32)
    for p in range(pairs):
        cols = slice(p * LANES, (p + 1) * LANES)
        pick_ref[p, :, :LANES] = pick_sum[:, cols]
        pick_ref[p, :, LANES:] = pick_source[:, cols]
        for j in range(4):
            row = few[(j + 1) * HALO - 1 : (j + 1) * HALO, cols]
            mid_ref[p, j] = jnp.broadcast_to(row, (8, LANES))
        dsend_ref[p] = jnp.broadcast_to(few[4 * HALO - 1 :, cols], (8, LANES))
    dec_copy = remote(dsend_ref, drecv_ref, dec_send, dec_recv, {"ctx": mate})
    dec_copy.start()

    taps = xf_ref.shape[0]

    def conv(block, halo, filters, slot):
        pad_ref[slot, 0:8] = halo.astype(jnp.float32)[HALO - 8 :]
        pad_ref[slot, 8:] = block.astype(jnp.float32)
        total = filters[0:1] * pad_ref[slot, 9 - taps : 9 - taps + length]
        for k in range(1, taps):
            start = 9 - taps + k
            total = total + filters[k : k + 1] * pad_ref[slot, start : start + length]
        return half_silu(total)

    m_copy.wait()

    @pl.when(has_prev)
    def _():
        halo_m.wait_recv()
        halo_x.wait_recv()

    bt_ref[...] = conv(m_ref[:, :LANES], hm_ref[:, :LANES], mfs_ref[0], 0).T.astype(jnp.bfloat16)
    x_copy.wait()

    def pair_copy(p):
        return remote(lsend_ref.at[p], lrecv_ref.at[p], pair_send.at[p], pair_recv.at[p], {"ctx": mate})

    half = length // 2

    def local_state(p, slot):
        cols = pl.ds(pl.multiple_of(p * LANES, LANES), LANES)
        xc = conv(x_ref[:, cols], hx_ref[:, cols], xfs_ref[p], slot).astype(jnp.bfloat16)
        xc_ref[p] = xc
        source = jnp.dot(left_ref[...], pick_ref[p, :, LANES:], preferred_element_type=jnp.float32)
        wide = xc.astype(jnp.float32)
        end = dsend_ref[p][0:1]
        border = mid_ref[p, 1][0:1]
        mids, states = [], []
        for j, stop in ((0, border), (1, end)):
            here = slice(j * half, (j + 1) * half)
            mid = mid_ref[p, 2 * j][0:1]
            u = (jnp.exp(source[here] - mid) * wide[here]).astype(jnp.bfloat16)
            uc_ref[p, here] = u
            fresh = jnp.dot(bt_ref[:, here], u, preferred_element_type=jnp.float32)
            mids.append(mid)
            states.append(fresh * jnp.exp(mid - stop))
        first_ref[p] = (states[0] * jnp.exp(border - mids[1])).astype(jnp.bfloat16)
        state = states[0] * jnp.exp(border - end) + states[1]
        lown_ref[p] = state
        lsend_ref[p] = state.astype(jnp.bfloat16)
        pair_copy(p).start()

    is_odd = odd.astype(jnp.float32)
    is_even = 1.0 - is_odd
    next_pair = {"ctx": (ctx + 2) % n_ctx}

    def chain_copy(p):
        return remote(csend_ref.at[p], crecv_ref.at[p], chain_send.at[p], chain_recv.at[p], next_pair)

    @pl.when(z == 0)
    def _():
        crecv_ref[...] = jnp.zeros_like(crecv_ref)

    dec_copy.wait_recv()

    def relay(p):
        pair_copy(p).wait_recv()
        mine = lown_ref[p]
        theirs = lrecv_ref[p].astype(jnp.float32)
        d_mine = jnp.exp(-dsend_ref[p][0:1])
        d_theirs = jnp.exp(-drecv_ref[p][0:1])
        l_even = mine * is_even + theirs * is_odd
        l_odd = mine * is_odd + theirs * is_even
        d_even = d_mine * is_even + d_theirs * is_odd
        d_odd = d_mine * is_odd + d_theirs * is_even

        @pl.when(z > 0)
        def _():
            chain_copy(p).wait_recv()

        entering = crecv_ref[p].astype(jnp.float32)
        middle = d_even * entering + l_even
        sr_ref[p] = (entering * is_even + middle * is_odd).astype(jnp.bfloat16)

        @pl.when(z < n_z - 1)
        def _():
            csend_ref[p] = (d_odd * middle + l_odd).astype(jnp.bfloat16)
            chain_copy(p).start()

    def scores_of_halves():
        c_ref[...] = conv(m_ref[:, LANES:], hm_ref[:, LANES:], mfs_ref[1], 1).astype(jnp.bfloat16)
        row_half = lax.broadcasted_iota(jnp.int32, (half, half), 0)
        col_half = lax.broadcasted_iota(jnp.int32, (half, half), 1)
        for j in range(2):
            here = slice(j * half, (j + 1) * half)
            scores = jnp.dot(c_ref[here, :], bt_ref[:, here], preferred_element_type=jnp.float32)
            cb_ref[j] = jnp.where(row_half >= col_half, scores, 0.0).astype(jnp.bfloat16)

    def within(p):
        cols = pl.ds(pl.multiple_of(p * LANES, LANES), LANES)
        skip = skips_ref[p][0:1]
        sums = jnp.dot(left_ref[...], pick_ref[p, :, :LANES], preferred_element_type=jnp.float32)
        for j in range(2):
            here = slice(j * half, (j + 1) * half)
            own = jnp.dot(cb_ref[j], uc_ref[p, here], preferred_element_type=jnp.float32)
            if j == 1:
                own = own + jnp.dot(c_ref[here, :], first_ref[p], preferred_element_type=jnp.float32)
            mid = mid_ref[p, 2 * j][0:1]
            decay = jnp.exp(mid - sums[here])
            gate = half_silu(z_ref[here, cols].astype(jnp.float32))
            yg_ref[p, here] = (decay * own + skip * xc_ref[p, here].astype(jnp.float32)) * gate
            eg_ref[p, here] = decay * jnp.exp(-mid) * gate

    z_copy.wait()
    twos = pairs // 2
    lag = jnp.minimum(2 + 2 * z, 2 * twos)

    gate_lag = jnp.maximum(lag, twos)
    squares_ref[...] = jnp.zeros_like(squares_ref)

    def gate_rows(p):
        inter = jnp.dot(c_ref[...], sr_ref[p], preferred_element_type=jnp.float32)
        gated = yg_ref[p] + eg_ref[p] * inter
        gated_ref[p] = gated
        squares_ref[...] += gated * gated

    def turn(i, _):
        @pl.when(i < twos)
        def _():
            for slot in range(2):
                local_state(2 * i + slot, slot)

        @pl.when((i >= lag) & (i < lag + twos))
        def _():
            for slot in range(2):
                relay(2 * (i - lag) + slot)

        @pl.when(i == twos)
        def _():
            scores_of_halves()

        @pl.when((i >= twos) & (i < 2 * twos))
        def _():
            for slot in range(2):
                within(2 * (i - twos) + slot)

        @pl.when((i >= gate_lag) & (i < gate_lag + twos))
        def _():
            for slot in range(2):
                gate_rows(2 * (i - gate_lag) + slot)

        return 0

    lax.fori_loop(0, 3 * twos, turn, 0)

    scale = lax.rsqrt(jnp.sum(squares_ref[...], axis=1, keepdims=True) / channels + 1e-05)
    for p in range(pairs):
        normed_ref[:, p * LANES : (p + 1) * LANES] = (
            gated_ref[p] * scale * gains_ref[p][0:1]
        ).astype(jnp.bfloat16)

    def core_copy(slot, k):
        rows_of = (y + slot) % n_y
        return remote(
            part_ref.at[rows_of, k, 1 - core], core_ref.at[rows_of, k],
            core_send.at[slot, k], core_recv.at[slot, k], {"tp": other_core},
        )

    def y_copy(slot, k):
        target = ((y + slot) % n_y) * 2 + core
        return remote(
            ysend_ref.at[slot - 1, k], yrecv_ref.at[slot - 1, k],
            y_send.at[slot - 1, k], y_recv.at[slot - 1, k], {"tp": target},
        )

    def chip_sum(slot, k):
        core_copy(slot, k).wait_recv()
        rows_of = (y + slot) % n_y
        return part_ref[rows_of, k, core].astype(jnp.float32) + core_ref[rows_of, k].astype(jnp.float32)

    def forward(k):
        for slot in range(1, n_y):
            ysend_ref[slot - 1, k] = chip_sum(slot, k).astype(jnp.bfloat16)
            y_copy(slot, k).start()

    def column(k, _):
        cols = pl.ds(pl.multiple_of(k * chunk, chunk), chunk)
        part = jnp.dot(normed_ref[...], w_ref[:, cols], preferred_element_type=jnp.float32)
        part = part.astype(jnp.bfloat16)
        for row_y in range(n_y):
            for row_core in range(2):
                first = (2 * row_y + row_core) * rows
                part_ref[row_y, k, row_core] = part[first : first + rows]
        for slot in range(1, n_y):
            core_copy(slot, k).start()

        @pl.when(k > 0)
        def _():
            forward(k - 1)

        return 0

    w_copy.wait()
    lax.fori_loop(0, n_chunks, column, 0)
    forward(n_chunks - 1)

    def share_own(k, _):
        core_copy(0, k).start()
        return 0

    lax.fori_loop(0, n_chunks, share_own, 0)

    def out_copy(k):
        cols = pl.ds(pl.multiple_of(k * chunk, chunk), chunk)
        return pltpu.make_async_copy(out_buf.at[k], out_ref.at[:, cols], out_sem.at[k])

    def finish(k, _):
        total = chip_sum(0, k)
        for slot in range(1, n_y):
            y_copy(slot, k).wait_recv()
            total = total + yrecv_ref[slot - 1, k].astype(jnp.float32)
        out_buf[k] = total.astype(jnp.bfloat16)
        out_copy(k).start()
        return 0

    lax.fori_loop(0, n_chunks, finish, 0)

    @pl.when(has_next)
    def _():
        halo_m.wait_send()
        halo_x.wait_send()

    dec_copy.wait_send()

    def drain_states(p, _):
        pair_copy(p).wait_send()

        @pl.when(z < n_z - 1)
        def _():
            chain_copy(p).wait_send()

        return 0

    lax.fori_loop(0, pairs, drain_states, 0)

    def drain_parts(k, _):
        out_copy(k).wait()
        for slot in range(n_y):
            core_copy(slot, k).wait_send()
        for slot in range(1, n_y):
            y_copy(slot, k).wait_send()
        return 0

    lax.fori_loop(0, n_chunks, drain_parts, 0)


def on_device(n_ctx, n_tp, *args):
    (x_inputs, state_maps, z_gate, step_raw, step_bias, decay_log, skip_gain,
     x_filter, state_filter, norm_gain, out_weight) = args
    length, channels = x_inputs.shape
    heads = step_raw.shape[1]
    pairs = channels // LANES
    model = out_weight.shape[1]
    rows = length // n_tp
    n_y = n_tp // 2
    chunk = 256
    n_chunks = model // chunk
    state = state_maps.shape[1] // 2
    bf16, f32 = jnp.bfloat16, jnp.float32
    vmem = pl.BlockSpec(memory_space=pltpu.VMEM)
    anywhere = pl.BlockSpec(memory_space=pl.ANY)
    dma = pltpu.SemaphoreType.DMA
    scratch = [
        pltpu.VMEM(out_weight.shape, bf16),
        pltpu.VMEM(x_inputs.shape, bf16),
        pltpu.VMEM(state_maps.shape, bf16),
        pltpu.VMEM(z_gate.shape, bf16),
        pltpu.VMEM((HALO, channels), bf16),
        pltpu.VMEM((HALO, 2 * state), bf16),
        pltpu.VMEM((2, length + 8, LANES), f32),
        pltpu.VMEM((pairs, x_filter.shape[0], LANES), f32),
        pltpu.VMEM((2, x_filter.shape[0], LANES), f32),
        pltpu.VMEM((pairs, 8, LANES), f32),
        pltpu.VMEM((pairs, 8, LANES), f32),
        pltpu.VMEM((LANES, length), f32),
        pltpu.VMEM((length, LANES), bf16),
        pltpu.VMEM((pairs, LANES, 2 * LANES), bf16),
        pltpu.VMEM((pairs, 8, LANES), f32),
        pltpu.VMEM((pairs, 8, LANES), f32),
        pltpu.VMEM((pairs, length, LANES), bf16),
        pltpu.VMEM((pairs, length, LANES), bf16),
        pltpu.VMEM((pairs, 4, 8, LANES), f32),
        pltpu.VMEM((pairs, state, LANES), bf16),
        pltpu.VMEM((state, length), bf16),
        pltpu.VMEM((length, state), bf16),
        pltpu.VMEM((2, length // 2, length // 2), bf16),
        pltpu.VMEM((pairs, state, LANES), f32),
        pltpu.VMEM((pairs, state, LANES), bf16),
        pltpu.VMEM((pairs, state, LANES), bf16),
        pltpu.VMEM((pairs, state, LANES), bf16),
        pltpu.VMEM((pairs, state, LANES), bf16),
        pltpu.VMEM((pairs, state, LANES), bf16),
        pltpu.VMEM((pairs, length, LANES), f32),
        pltpu.VMEM((pairs, length, LANES), f32),
        pltpu.VMEM((length, LANES), f32),
        pltpu.VMEM((pairs, length, LANES), f32),
        pltpu.VMEM((length, channels), bf16),
        pltpu.VMEM((n_y, n_chunks, 2, rows, chunk), bf16),
        pltpu.VMEM((n_y, n_chunks, rows, chunk), bf16),
        pltpu.VMEM((n_y - 1, n_chunks, rows, chunk), bf16),
        pltpu.VMEM((n_y - 1, n_chunks, rows, chunk), bf16),
        pltpu.VMEM((n_chunks, rows, chunk), bf16),
        dma, dma((3,)), dma((n_chunks,)), dma((2,)), dma((2,)), dma, dma,
        dma((pairs,)), dma((pairs,)), dma((pairs,)), dma((pairs,)),
        dma((n_y, n_chunks)), dma((n_y, n_chunks)),
        dma((n_y - 1, n_chunks)), dma((n_y - 1, n_chunks)),
    ]
    return pl.pallas_call(
        functools.partial(layer_kernel, n_ctx, n_tp, chunk),
        out_shape=jax.ShapeDtypeStruct((rows, model), bf16),
        in_specs=[anywhere] * 3 + [vmem] * 7 + [anywhere],
        out_specs=anywhere,
        scratch_shapes=scratch,
        compiler_params=pltpu.CompilerParams(
            collective_id=0, has_side_effects=True, vmem_limit_bytes=58 * 1024 * 1024
        ),
        cost_estimate=pl.CostEstimate(
            flops=2 * length * channels * (model + 2 * length), bytes_accessed=4 * out_weight.size,
            transcendentals=length * length * heads,
        ),
        name="layer",
    )(
        x_inputs, state_maps, z_gate, step_raw.T, step_bias[None], decay_log[None], skip_gain[None],
        x_filter, state_filter, norm_gain[None], out_weight,
    )


def solution(mesh):
    return jax.shard_map(
        functools.partial(on_device, mesh.shape["ctx"], mesh.shape["tp"]),
        mesh=mesh,
        in_specs=(
            P("ctx", "tp"),
            P("ctx", "tp"),
            P("ctx", "tp"),
            P("ctx", "tp"),
            P("tp"),
            P("tp"),
            P("tp"),
            P(None, "tp"),
            P(None, "tp"),
            P("tp"),
            P("tp", None),
        ),
        out_specs=P(("ctx", "tp"), None),
        check_vma=False,
    )
```

```python
import functools

import jax
import jax.numpy as jnp
from jax import lax
from jax.experimental import pallas as pl
from jax.experimental.pallas import tpu as pltpu
from jax.sharding import PartitionSpec as P

MESH = pl.DeviceIdType.MESH
LANES = 128
HALO = 16


def half_silu(v):
    h = 0.5 * v
    return h + h * jnp.tanh(h)


def layer_kernel(
    n_ctx, n_tp, chunk,
    x_hbm, m_hbm, z_hbm, step_ref, bias_ref, decay_ref, skip_ref, xf_ref, mf_ref, gain_ref, w_hbm,
    out_ref,
    w_ref, x_ref, m_ref, z_ref, hx_ref, hm_ref, pad_ref, xfs_ref, mfs_ref, gains_ref, skips_ref,
    parts_ref, left_ref, pick_ref, dsend_ref, drecv_ref,
    xc_ref, uc_ref, mid_ref, first_ref, bt_ref, c_ref, cb_ref, lown_ref, lsend_ref, lrecv_ref, csend_ref, crecv_ref, sr_ref,
    yg_ref, eg_ref, squares_ref, gated_ref, normed_ref, part_ref, core_ref, ysend_ref, yrecv_ref, out_buf,
    w_sem, in_sem, out_sem, halo_send, halo_recv, dec_send, dec_recv, pair_send, pair_recv, chain_send, chain_recv,
    core_send, core_recv, y_send, y_recv,
):
    length = x_ref.shape[0]
    pairs = x_ref.shape[1] // LANES
    heads = step_ref.shape[0]
    n_y = n_tp // 2
    rows = length // n_tp
    n_chunks = w_hbm.shape[1] // chunk
    n_z = n_ctx // 2
    ctx = lax.axis_index("ctx")
    tp = lax.axis_index("tp")
    y, core = tp // 2, tp % 2
    z, odd = ctx // 2, ctx % 2
    mate = ctx + 1 - 2 * odd
    other_core = y * 2 + 1 - core

    w_copy = pltpu.make_async_copy(w_hbm, w_ref, w_sem)
    m_copy = pltpu.make_async_copy(m_hbm, m_ref, in_sem.at[0])
    x_copy = pltpu.make_async_copy(x_hbm, x_ref, in_sem.at[1])
    z_copy = pltpu.make_async_copy(z_hbm, z_ref, in_sem.at[2])

    barrier = pltpu.get_barrier_semaphore()
    has_prev, has_next = ctx >= 1, ctx <= n_ctx - 2
    for there, off in ((has_prev, -1), (has_next, 1), (ctx >= 2, -2), (ctx <= n_ctx - 3, 2)):

        @pl.when(there)
        def _(off=off):
            pl.semaphore_signal(barrier, inc=1, device_id={"ctx": ctx + off}, device_id_type=MESH)

    pl.semaphore_signal(barrier, inc=1, device_id={"tp": other_core}, device_id_type=MESH)
    for off in range(1, n_y):
        pl.semaphore_signal(
            barrier, inc=1, device_id={"tp": ((y + off) % n_y) * 2 + core}, device_id_type=MESH
        )

    for copy in (m_copy, x_copy, z_copy, w_copy):
        copy.start()

    def remote(src, dst, send, recv, where):
        return pltpu.make_async_remote_copy(
            src_ref=src, dst_ref=dst, send_sem=send, recv_sem=recv, device_id=where, device_id_type=MESH
        )

    def three_terms(v):
        first = v.astype(jnp.bfloat16).astype(jnp.float32)
        second = (v - first).astype(jnp.bfloat16).astype(jnp.float32)
        return [first, second, (v - first - second).astype(jnp.bfloat16).astype(jnp.float32)]

    def all_tokens(column):
        return jnp.concatenate([column] * (length // LANES), axis=1)

    filling = jnp.zeros((1, LANES - 3 * heads), jnp.float32)
    vectors = jnp.concatenate([bias_ref[...], decay_ref[...], skip_ref[...], filling], axis=1)
    columns = jnp.broadcast_to(vectors, (LANES, LANES)).T
    step = jnp.log(1.0 + jnp.exp(step_ref[...] + all_tokens(columns[:heads])))
    rate = step * jnp.exp(all_tokens(columns[heads : 2 * heads]))
    skip_t = columns[2 * heads : 3 * heads]

    greeted = jnp.minimum(ctx, 2) + jnp.minimum(n_ctx - 1 - ctx, 2)
    pl.semaphore_wait(barrier, greeted + 1 + (n_y - 1))

    following = {"ctx": (ctx + 1) % n_ctx}
    halo_x = remote(x_hbm.at[pl.ds(length - HALO, HALO)], hx_ref, halo_send.at[0], halo_recv.at[0], following)
    halo_m = remote(m_hbm.at[pl.ds(length - HALO, HALO)], hm_ref, halo_send.at[1], halo_recv.at[1], following)

    @pl.when(has_next)
    def _():
        halo_m.start()
        halo_x.start()

    @pl.when(ctx == 0)
    def _():
        hm_ref[...] = jnp.zeros_like(hm_ref)
        hx_ref[...] = jnp.zeros_like(hx_ref)


    s_ids = lax.broadcasted_iota(jnp.int32, (length, length), 0)
    t_ids = lax.broadcasted_iota(jnp.int32, (length, length), 1)
    upper = jnp.where(s_ids <= t_ids, 1.0, 0.0).astype(jnp.bfloat16)
    sums = jnp.dot(
        jnp.concatenate(three_terms(rate), axis=0).astype(jnp.bfloat16), upper,
        preferred_element_type=jnp.float32,
    )
    sums = sums[:heads] + sums[heads : 2 * heads] + sums[2 * heads :]
    source = sums + jnp.log(step)
    filler = jnp.ones((LANES - 6 * heads, length), jnp.float32)
    parts_ref[...] = jnp.concatenate(three_terms(sums) + three_terms(source) + [filler], axis=0)
    left_ref[...] = parts_ref[...].T.astype(jnp.bfloat16)

    lane_row = lax.broadcasted_iota(jnp.int32, (1, LANES), 1) < LANES // 2
    x_taps = xf_ref[...].astype(jnp.float32)
    m_taps = mf_ref[...].astype(jnp.float32)
    for p in range(pairs):
        skips_ref[p] = jnp.broadcast_to(
            jnp.where(lane_row, skip_t[2 * p : 2 * p + 1], skip_t[2 * p + 1 : 2 * p + 2]), (8, LANES)
        )
        gains_ref[p] = jnp.broadcast_to(gain_ref[:, p * LANES : (p + 1) * LANES], (8, LANES))
        xfs_ref[p] = x_taps[:, p * LANES : (p + 1) * LANES]
    for p in range(2):
        mfs_ref[p] = m_taps[:, p * LANES : (p + 1) * LANES]

    channels = x_ref.shape[1]
    term = lax.broadcasted_iota(jnp.int32, (LANES, channels), 0)
    lane = lax.broadcasted_iota(jnp.int32, (LANES, channels), 1)
    width = channels // heads
    match = (lane >= (term & (heads - 1)) * width) & (lane < ((term & (heads - 1)) + 1) * width)
    pick_sum = jnp.where(match & (term < 3 * heads), 1.0, 0.0).astype(jnp.bfloat16)
    pick_source = jnp.where(match & (term >= 3 * heads) & (term < 6 * heads), 1.0, 0.0).astype(jnp.bfloat16)
    quarter = length // 4
    few = jnp.concatenate([left_ref[(j + 1) * quarter - HALO : (j + 1) * quarter, :] for j in range(4)], axis=0)
    few = jnp.dot(few, pick_sum, preferred_element_type=jnp.float32)
    for p in range(pairs):
        cols = slice(p * LANES, (p + 1) * LANES)
        pick_ref[p, :, :LANES] = pick_sum[:, cols]
        pick_ref[p, :, LANES:] = pick_source[:, cols]
        for j in range(4):
            row = few[(j + 1) * HALO - 1 : (j + 1) * HALO, cols]
            mid_ref[p, j] = jnp.broadcast_to(row, (8, LANES))
        dsend_ref[p] = jnp.broadcast_to(few[4 * HALO - 1 :, cols], (8, LANES))
    dec_copy = remote(dsend_ref, drecv_ref, dec_send, dec_recv, {"ctx": mate})
    dec_copy.start()

    taps = xf_ref.shape[0]

    def conv(block, halo, filters, slot):
        pad_ref[slot, 0:8] = halo.astype(jnp.float32)[HALO - 8 :]
        pad_ref[slot, 8:] = block.astype(jnp.float32)
        total = filters[0:1] * pad_ref[slot, 9 - taps : 9 - taps + length]
        for k in range(1, taps):
            start = 9 - taps + k
            total = total + filters[k : k + 1] * pad_ref[slot, start : start + length]
        return half_silu(total)

    m_copy.wait()

    @pl.when(has_prev)
    def _():
        halo_m.wait_recv()
        halo_x.wait_recv()

    bt_ref[...] = conv(m_ref[:, :LANES], hm_ref[:, :LANES], mfs_ref[0], 0).T.astype(jnp.bfloat16)
    x_copy.wait()

    def pair_copy(p):
        return remote(lsend_ref.at[p], lrecv_ref.at[p], pair_send.at[p], pair_recv.at[p], {"ctx": mate})

    half = length // 2

    def local_state(p, slot):
        cols = pl.ds(pl.multiple_of(p * LANES, LANES), LANES)
        xc = conv(x_ref[:, cols], hx_ref[:, cols], xfs_ref[p], slot).astype(jnp.bfloat16)
        xc_ref[p] = xc
        source = jnp.dot(left_ref[...], pick_ref[p, :, LANES:], preferred_element_type=jnp.float32)
        wide = xc.astype(jnp.float32)
        end = dsend_ref[p][0:1]
        border = mid_ref[p, 1][0:1]
        mids, states = [], []
        for j, stop in ((0, border), (1, end)):
            here = slice(j * half, (j + 1) * half)
            mid = mid_ref[p, 2 * j][0:1]
            u = (jnp.exp(source[here] - mid) * wide[here]).astype(jnp.bfloat16)
            uc_ref[p, here] = u
            fresh = jnp.dot(bt_ref[:, here], u, preferred_element_type=jnp.float32)
            mids.append(mid)
            states.append(fresh * jnp.exp(mid - stop))
        first_ref[p] = (states[0] * jnp.exp(border - mids[1])).astype(jnp.bfloat16)
        state = states[0] * jnp.exp(border - end) + states[1]
        lown_ref[p] = state
        lsend_ref[p] = state.astype(jnp.bfloat16)
        pair_copy(p).start()

    is_odd = odd.astype(jnp.float32)
    is_even = 1.0 - is_odd
    next_pair = {"ctx": (ctx + 2) % n_ctx}

    def chain_copy(p):
        return remote(csend_ref.at[p], crecv_ref.at[p], chain_send.at[p], chain_recv.at[p], next_pair)

    @pl.when(z == 0)
    def _():
        crecv_ref[...] = jnp.zeros_like(crecv_ref)

    dec_copy.wait_recv()

    def relay(p):
        pair_copy(p).wait_recv()
        mine = lown_ref[p]
        theirs = lrecv_ref[p].astype(jnp.float32)
        d_mine = jnp.exp(-dsend_ref[p][0:1])
        d_theirs = jnp.exp(-drecv_ref[p][0:1])
        l_even = mine * is_even + theirs * is_odd
        l_odd = mine * is_odd + theirs * is_even
        d_even = d_mine * is_even + d_theirs * is_odd
        d_odd = d_mine * is_odd + d_theirs * is_even

        @pl.when(z > 0)
        def _():
            chain_copy(p).wait_recv()

        entering = crecv_ref[p].astype(jnp.float32)
        middle = d_even * entering + l_even
        sr_ref[p] = (entering * is_even + middle * is_odd).astype(jnp.bfloat16)

        @pl.when(z < n_z - 1)
        def _():
            csend_ref[p] = (d_odd * middle + l_odd).astype(jnp.bfloat16)
            chain_copy(p).start()

    def scores_of_halves():
        c_ref[...] = conv(m_ref[:, LANES:], hm_ref[:, LANES:], mfs_ref[1], 1).astype(jnp.bfloat16)
        row_half = lax.broadcasted_iota(jnp.int32, (half, half), 0)
        col_half = lax.broadcasted_iota(jnp.int32, (half, half), 1)
        for j in range(2):
            here = slice(j * half, (j + 1) * half)
            scores = jnp.dot(c_ref[here, :], bt_ref[:, here], preferred_element_type=jnp.float32)
            cb_ref[j] = jnp.where(row_half >= col_half, scores, 0.0).astype(jnp.bfloat16)

    def within(p):
        cols = pl.ds(pl.multiple_of(p * LANES, LANES), LANES)
        skip = skips_ref[p][0:1]
        sums = jnp.dot(left_ref[...], pick_ref[p, :, :LANES], preferred_element_type=jnp.float32)
        for j in range(2):
            here = slice(j * half, (j + 1) * half)
            own = jnp.dot(cb_ref[j], uc_ref[p, here], preferred_element_type=jnp.float32)
            if j == 1:
                own = own + jnp.dot(c_ref[here, :], first_ref[p], preferred_element_type=jnp.float32)
            mid = mid_ref[p, 2 * j][0:1]
            decay = jnp.exp(mid - sums[here])
            gate = half_silu(z_ref[here, cols].astype(jnp.float32))
            yg_ref[p, here] = (decay * own + skip * xc_ref[p, here].astype(jnp.float32)) * gate
            eg_ref[p, here] = decay * jnp.exp(-mid) * gate

    z_copy.wait()
    twos = pairs // 2
    lag = jnp.minimum(2 + 2 * z, 2 * twos)

    gate_lag = jnp.maximum(lag, twos)
    squares_ref[...] = jnp.zeros_like(squares_ref)

    def gate_rows(p):
        inter = jnp.dot(c_ref[...], sr_ref[p], preferred_element_type=jnp.float32)
        gated = yg_ref[p] + eg_ref[p] * inter
        gated_ref[p] = gated
        squares_ref[...] += gated * gated

    def turn(i, _):
        @pl.when(i < twos)
        def _():
            for slot in range(2):
                local_state(2 * i + slot, slot)

        @pl.when((i >= lag) & (i < lag + twos))
        def _():
            for slot in range(2):
                relay(2 * (i - lag) + slot)

        @pl.when(i == twos)
        def _():
            scores_of_halves()

        @pl.when((i >= twos) & (i < 2 * twos))
        def _():
            for slot in range(2):
                within(2 * (i - twos) + slot)

        @pl.when((i >= gate_lag) & (i < gate_lag + twos))
        def _():
            for slot in range(2):
                gate_rows(2 * (i - gate_lag) + slot)

        return 0

    lax.fori_loop(0, 3 * twos, turn, 0)

    scale = lax.rsqrt(jnp.sum(squares_ref[...], axis=1, keepdims=True) / channels + 1e-05)
    for p in range(pairs):
        normed_ref[:, p * LANES : (p + 1) * LANES] = (
            gated_ref[p] * scale * gains_ref[p][0:1]
        ).astype(jnp.bfloat16)

    def core_copy(slot, k):
        rows_of = (y + slot) % n_y
        return remote(
            part_ref.at[rows_of, k, 1 - core], core_ref.at[rows_of, k],
            core_send.at[slot, k], core_recv.at[slot, k], {"tp": other_core},
        )

    def y_copy(slot, k):
        target = ((y + slot) % n_y) * 2 + core
        return remote(
            ysend_ref.at[slot - 1, k], yrecv_ref.at[slot - 1, k],
            y_send.at[slot - 1, k], y_recv.at[slot - 1, k], {"tp": target},
        )

    def chip_sum(slot, k):
        core_copy(slot, k).wait_recv()
        rows_of = (y + slot) % n_y
        return part_ref[rows_of, k, core].astype(jnp.float32) + core_ref[rows_of, k].astype(jnp.float32)

    def forward(k):
        for slot in range(1, n_y):
            ysend_ref[slot - 1, k] = chip_sum(slot, k).astype(jnp.bfloat16)
            y_copy(slot, k).start()

    def column(k, _):
        cols = pl.ds(pl.multiple_of(k * chunk, chunk), chunk)
        part = jnp.dot(normed_ref[...], w_ref[:, cols], preferred_element_type=jnp.float32)
        part = part.astype(jnp.bfloat16)
        for row_y in range(n_y):
            for row_core in range(2):
                first = (2 * row_y + row_core) * rows
                part_ref[row_y, k, row_core] = part[first : first + rows]
        for slot in range(1, n_y):
            core_copy(slot, k).start()

        @pl.when(k > 0)
        def _():
            forward(k - 1)

        return 0

    w_copy.wait()
    lax.fori_loop(0, n_chunks, column, 0)
    forward(n_chunks - 1)

    def share_own(k, _):
        core_copy(0, k).start()
        return 0

    lax.fori_loop(0, n_chunks, share_own, 0)

    def out_copy(k):
        cols = pl.ds(pl.multiple_of(k * chunk, chunk), chunk)
        return pltpu.make_async_copy(out_buf.at[k], out_ref.at[:, cols], out_sem.at[k])

    def finish(k, _):
        total = chip_sum(0, k)
        for slot in range(1, n_y):
            y_copy(slot, k).wait_recv()
            total = total + yrecv_ref[slot - 1, k].astype(jnp.float32)
        out_buf[k] = total.astype(jnp.bfloat16)
        out_copy(k).start()
        return 0

    lax.fori_loop(0, n_chunks, finish, 0)

    @pl.when(has_next)
    def _():
        halo_m.wait_send()
        halo_x.wait_send()

    dec_copy.wait_send()

    def drain_states(p, _):
        pair_copy(p).wait_send()

        @pl.when(z < n_z - 1)
        def _():
            chain_copy(p).wait_send()

        return 0

    lax.fori_loop(0, pairs, drain_states, 0)

    def drain_parts(k, _):
        out_copy(k).wait()
        for slot in range(n_y):
            core_copy(slot, k).wait_send()
        for slot in range(1, n_y):
            y_copy(slot, k).wait_send()
        return 0

    lax.fori_loop(0, n_chunks, drain_parts, 0)


def on_device(n_ctx, n_tp, *args):
    (x_inputs, state_maps, z_gate, step_raw, step_bias, decay_log, skip_gain,
     x_filter, state_filter, norm_gain, out_weight) = args
    length, channels = x_inputs.shape
    heads = step_raw.shape[1]
    pairs = channels // LANES
    model = out_weight.shape[1]
    rows = length // n_tp
    n_y = n_tp // 2
    chunk = 512
    n_chunks = model // chunk
    state = state_maps.shape[1] // 2
    bf16, f32 = jnp.bfloat16, jnp.float32
    vmem = pl.BlockSpec(memory_space=pltpu.VMEM)
    anywhere = pl.BlockSpec(memory_space=pl.ANY)
    dma = pltpu.SemaphoreType.DMA
    scratch = [
        pltpu.VMEM(out_weight.shape, bf16),
        pltpu.VMEM(x_inputs.shape, bf16),
        pltpu.VMEM(state_maps.shape, bf16),
        pltpu.VMEM(z_gate.shape, bf16),
        pltpu.VMEM((HALO, channels), bf16),
        pltpu.VMEM((HALO, 2 * state), bf16),
        pltpu.VMEM((2, length + 8, LANES), f32),
        pltpu.VMEM((pairs, x_filter.shape[0], LANES), f32),
        pltpu.VMEM((2, x_filter.shape[0], LANES), f32),
        pltpu.VMEM((pairs, 8, LANES), f32),
        pltpu.VMEM((pairs, 8, LANES), f32),
        pltpu.VMEM((LANES, length), f32),
        pltpu.VMEM((length, LANES), bf16),
        pltpu.VMEM((pairs, LANES, 2 * LANES), bf16),
        pltpu.VMEM((pairs, 8, LANES), f32),
        pltpu.VMEM((pairs, 8, LANES), f32),
        pltpu.VMEM((pairs, length, LANES), bf16),
        pltpu.VMEM((pairs, length, LANES), bf16),
        pltpu.VMEM((pairs, 4, 8, LANES), f32),
        pltpu.VMEM((pairs, state, LANES), bf16),
        pltpu.VMEM((state, length), bf16),
        pltpu.VMEM((length, state), bf16),
        pltpu.VMEM((2, length // 2, length // 2), bf16),
        pltpu.VMEM((pairs, state, LANES), f32),
        pltpu.VMEM((pairs, state, LANES), bf16),
        pltpu.VMEM((pairs, state, LANES), bf16),
        pltpu.VMEM((pairs, state, LANES), bf16),
        pltpu.VMEM((pairs, state, LANES), bf16),
        pltpu.VMEM((pairs, state, LANES), bf16),
        pltpu.VMEM((pairs, length, LANES), f32),
        pltpu.VMEM((pairs, length, LANES), f32),
        pltpu.VMEM((length, LANES), f32),
        pltpu.VMEM((pairs, length, LANES), f32),
        pltpu.VMEM((length, channels), bf16),
        pltpu.VMEM((n_y, n_chunks, 2, rows, chunk), bf16),
        pltpu.VMEM((n_y, n_chunks, rows, chunk), bf16),
        pltpu.VMEM((n_y - 1, n_chunks, rows, chunk), bf16),
        pltpu.VMEM((n_y - 1, n_chunks, rows, chunk), bf16),
        pltpu.VMEM((n_chunks, rows, chunk), bf16),
        dma, dma((3,)), dma((n_chunks,)), dma((2,)), dma((2,)), dma, dma,
        dma((pairs,)), dma((pairs,)), dma((pairs,)), dma((pairs,)),
        dma((n_y, n_chunks)), dma((n_y, n_chunks)),
        dma((n_y - 1, n_chunks)), dma((n_y - 1, n_chunks)),
    ]
    return pl.pallas_call(
        functools.partial(layer_kernel, n_ctx, n_tp, chunk),
        out_shape=jax.ShapeDtypeStruct((rows, model), bf16),
        in_specs=[anywhere] * 3 + [vmem] * 7 + [anywhere],
        out_specs=anywhere,
        scratch_shapes=scratch,
        compiler_params=pltpu.CompilerParams(
            collective_id=0, has_side_effects=True, vmem_limit_bytes=58 * 1024 * 1024
        ),
        cost_estimate=pl.CostEstimate(
            flops=2 * length * channels * (model + 2 * length), bytes_accessed=4 * out_weight.size,
            transcendentals=length * length * heads,
        ),
        name="layer",
    )(
        x_inputs, state_maps, z_gate, step_raw.T, step_bias[None], decay_log[None], skip_gain[None],
        x_filter, state_filter, norm_gain[None], out_weight,
    )


def solution(mesh):
    return jax.shard_map(
        functools.partial(on_device, mesh.shape["ctx"], mesh.shape["tp"]),
        mesh=mesh,
        in_specs=(
            P("ctx", "tp"),
            P("ctx", "tp"),
            P("ctx", "tp"),
            P("ctx", "tp"),
            P("tp"),
            P("tp"),
            P("tp"),
            P(None, "tp"),
            P(None, "tp"),
            P("tp"),
            P("tp", None),
        ),
        out_specs=P(("ctx", "tp"), None),
        check_vma=False,
    )
```
